32 devices in a mesh: ctx: 4 (over z), fsdp: 8 (over y, x, core).
Axes of the slice: x: 2, y: 2, z: 4, core: 2. Of those that a mesh axis runs over, the one named last changes fastest.
Arguments:
- inputs: bfloat16 [8, 2, 512, 2048], P('fsdp', None, 'ctx'), may hold values from -6 to 6
- lengths: int32 [8], P('fsdp'), may hold values from 256 to 1024, as said below
- attn_gain: bfloat16 [2048], P(('ctx', 'fsdp')), may hold values from 0.099609375 to 1.8984375
- query_weight: bfloat16 [2048, 2048], P(('ctx', 'fsdp')), may hold values from -0.125 to 0.125
- key_matrix: bfloat16 [2048, 1024], P(('ctx', 'fsdp')), may hold values from -0.125 to 0.125
- value_matrix: bfloat16 [2048, 1024], P(('ctx', 'fsdp')), may hold values from -0.125 to 0.125
- output_weight: bfloat16 [2048, 2048], P(('ctx', 'fsdp')), may hold values from -0.75 to 0.75
- ffn_gain: bfloat16 [2048], P(('ctx', 'fsdp')), may hold values from 0.099609375 to 1.8984375
- gate_weight: bfloat16 [2048, 8192], P(('ctx', 'fsdp')), may hold values from -0.125 to 0.125
- up_weight: bfloat16 [2048, 8192], P(('ctx', 'fsdp')), may hold values from -0.125 to 0.125
- down_weight: bfloat16 [8192, 2048], P(('ctx', 'fsdp')), may hold values from -0.0625 to 0.0625
- cotangent: bfloat16 [8, 2, 512, 2048], P('fsdp', None, 'ctx'), may hold values from -6 to 6
Outputs:
- outputs: bfloat16 [8, 2, 512, 2048], P('fsdp', None, 'ctx')
- input_grad: bfloat16 [8, 2, 512, 2048], P('fsdp', None, 'ctx')
- attn_gain_grad: float32 [2048], P(('ctx', 'fsdp'))
- query_grad: float32 [2048, 2048], P(('ctx', 'fsdp'))
- key_grad: float32 [2048, 1024], P(('ctx', 'fsdp'))
- value_grad: float32 [2048, 1024], P(('ctx', 'fsdp'))
- output_grad: float32 [2048, 2048], P(('ctx', 'fsdp'))
- ffn_gain_grad: float32 [2048], P(('ctx', 'fsdp'))
- gate_grad: float32 [2048, 8192], P(('ctx', 'fsdp'))
- up_grad: float32 [2048, 8192], P(('ctx', 'fsdp'))
- down_grad: float32 [8192, 2048], P(('ctx', 'fsdp'))
The draws below stay inside these ranges and needn't reach their ends.
Inputs may be any that keep to these rules, and one draw needn't show every extreme that they name: `lengths`: one slot, drawn from the seed, has length 1024.
All inputs are finite; a program needn't handle non-finite values.
Results may differ from the reference program's by a relative error of at most 0.017.
Values may be sent and summed in bfloat16 or wider, within the bound.
A program may use at most 704 MiB of HBM per device.

```python
import jax
import jax.numpy as jnp
from jax import lax

MODEL_WIDTH = 2048
QUERY_HEADS = 8
KEY_VALUE_HEADS = 4
HEAD_SIZE = 256
FF = 8192
BLK = 128
SEQS = 8
HALF = 512
LENGTH = 1024
N_CTX = 4


def draw_lengths(key, part):
    key = jax.random.fold_in(key, 17)
    first_key, second_key = jax.random.split(key)
    drawn = jax.random.randint(first_key, (SEQS,), LENGTH // 4, LENGTH + 1)
    chosen = jax.random.randint(second_key, (), 0, SEQS)
    return jnp.where(jnp.arange(SEQS) == chosen, LENGTH, drawn).astype(jnp.int32)


def shard_levels(key, dims, cuts, low, top_value):
    factor_of = 1.0
    for axis_at, blocks in cuts:
        draws = jax.random.uniform(jax.random.fold_in(jax.random.fold_in(key, 6), axis_at), (blocks,), jnp.float32, low / len(cuts), top_value / len(cuts))
        factor_of = factor_of * jnp.repeat(jnp.exp(draws), dims[axis_at] // blocks).reshape((-1,) + (1,) * (len(dims) - 1 - axis_at))
    return factor_of


def normal_values(rng, dims, spread, most, cuts=(), kind=jnp.bfloat16):
    array = jax.random.normal(rng, dims, jnp.float32) * spread
    if len(cuts) > 0:
        array = shard_levels(rng, dims, cuts, -0.22, 0.18) * array
    return jnp.clip(array, min=-most, max=most).astype(kind)


def setup_inputs(seed: int = 0) -> dict:
    streams_of = jax.random.split(jax.random.key(seed), 13)
    inputs = normal_values(streams_of[0], (SEQS, 2, HALF, MODEL_WIDTH), 1.0, 6.0, ((0, 8), (2, 4)))
    lengths = draw_lengths(jax.random.fold_in(streams_of[12], 71), 0)
    attn_gain = jnp.clip(1.0 + 0.18 * jax.random.normal(streams_of[2], (MODEL_WIDTH,), jnp.float32), 0.099609375, 1.8984375).astype(jnp.bfloat16)
    query_weight = normal_values(streams_of[3], (MODEL_WIDTH, QUERY_HEADS * HEAD_SIZE), MODEL_WIDTH ** -0.5, 0.125, ((0, 32),))
    key_matrix = normal_values(streams_of[4], (MODEL_WIDTH, KEY_VALUE_HEADS * HEAD_SIZE), MODEL_WIDTH ** -0.5, 0.125, ((0, 32),))
    value_matrix = normal_values(streams_of[5], (MODEL_WIDTH, KEY_VALUE_HEADS * HEAD_SIZE), MODEL_WIDTH ** -0.5, 0.125, ((0, 32),))
    output_weight = normal_values(streams_of[6], (QUERY_HEADS * HEAD_SIZE, MODEL_WIDTH), (max(1, QUERY_HEADS * HEAD_SIZE // 32)) ** -0.5, 0.75, ((0, 32),))
    ffn_gain = jnp.clip(1.0 + 0.18 * jax.random.normal(streams_of[7], (MODEL_WIDTH,), jnp.float32), 0.099609375, 1.8984375).astype(jnp.bfloat16)
    gate_weight = normal_values(streams_of[8], (MODEL_WIDTH, FF), MODEL_WIDTH ** -0.5, 0.125, ((0, 32),))
    up_weight = normal_values(streams_of[9], (MODEL_WIDTH, FF), MODEL_WIDTH ** -0.5, 0.125, ((0, 32),))
    down_weight = normal_values(streams_of[10], (FF, MODEL_WIDTH), FF ** -0.5, 0.0625, ((0, 32),))
    cotangent = normal_values(streams_of[11], (SEQS, 2, HALF, MODEL_WIDTH), 1.0, 6.0, ((0, 8), (2, 4)))
    return {"inputs": inputs, "lengths": lengths, "attn_gain": attn_gain, "query_weight": query_weight, "key_matrix": key_matrix, "value_matrix": value_matrix, "output_weight": output_weight, "ffn_gain": ffn_gain, "gate_weight": gate_weight, "up_weight": up_weight, "down_weight": down_weight, "cotangent": cotangent}


highest = lax.Precision.HIGHEST
epsilon = 1e-06
rope_base = 1000042.0

@jax.custom_vjp
def lower_precision(v):
    return lax.optimization_barrier(v.astype(jnp.bfloat16)).astype(jnp.float32)

@jax.custom_vjp
def lower_backward(v):
    return v

def low_keep(v):
    return (lower_precision(v), None)

def low_pass(kept, grad):
    return (grad,)

def back_keep(v):
    return (v, None)

def back_low(kept, grad):
    return (lower_precision(grad),)
lower_precision.defvjp(low_keep, low_pass)
lower_backward.defvjp(back_keep, back_low)

def matrix_product(left, right):
    return jnp.dot(left, right, precision=highest)

def apply_rotation(tensor, token_position, direction):
    halfway = tensor.shape[-1] // 2
    frequency = rope_base ** (-2.0 * jnp.arange(halfway).astype(jnp.float32) / tensor.shape[-1])
    rotation_angles = token_position.astype(jnp.float32)[:, None] * frequency[None, :]
    cos_table = jnp.cos(rotation_angles)[:, None, :]
    sin_table = direction * jnp.sin(rotation_angles)[:, None, :]
    front_half = tensor[..., :halfway]
    back_half = tensor[..., halfway:]
    return jnp.concatenate([front_half * cos_table - back_half * sin_table, back_half * cos_table + front_half * sin_table], axis=-1)

def rms_scale(values):
    return lax.rsqrt(lax.optimization_barrier(jnp.mean(values * values, axis=-1, keepdims=True)) + epsilon)

def layer_slot(params, tokens, length):
    w_query, key_projection, value_projection, w_output, w_gating, w_upward, w_downward, gain_first, gain_second = params
    sequence_length = tokens.shape[0]
    token_position = jnp.arange(sequence_length, dtype=jnp.int32)
    valid_rows = (token_position < length).astype(tokens.dtype)[:, None]
    first_normalized = lower_precision(tokens * rms_scale(tokens) * gain_first)
    query_rows = lower_backward(matrix_product(first_normalized, w_query)).reshape(sequence_length, QUERY_HEADS, HEAD_SIZE)
    unrotated_keys = lower_backward(matrix_product(first_normalized, key_projection)).reshape(sequence_length, KEY_VALUE_HEADS, HEAD_SIZE)
    every_value = lower_precision(lower_backward(matrix_product(first_normalized, value_projection))).reshape(sequence_length, KEY_VALUE_HEADS, HEAD_SIZE)
    query_rows = lower_precision(apply_rotation(query_rows, token_position, 1.0)).reshape(sequence_length, KEY_VALUE_HEADS, QUERY_HEADS // KEY_VALUE_HEADS, HEAD_SIZE)
    keys_rot = lower_precision(apply_rotation(unrotated_keys, token_position, 1.0))
    scores = jnp.einsum('qkgd,skd->kgqs', query_rows, keys_rot, precision=highest) * HEAD_SIZE ** (-0.5)
    scores = lower_backward(scores)
    allowed = (token_position[None, :] <= token_position[:, None]) & (token_position[None, :] < length)
    scores = jnp.where(allowed, scores, -jnp.inf)
    softmax_p = jax.nn.softmax(scores, axis=-1)
    attended = jnp.einsum('kgqs,skd->qkgd', lower_precision(softmax_p), every_value, precision=highest).reshape(sequence_length, QUERY_HEADS * HEAD_SIZE)
    attended = lower_precision(lower_backward(attended))
    hidden_one = tokens + lower_backward(matrix_product(attended, w_output))
    normed_two = lower_precision(hidden_one * rms_scale(hidden_one) * gain_second)
    gating = lower_backward(matrix_product(normed_two, w_gating))
    upward = lower_backward(matrix_product(normed_two, w_upward))
    mixed_hidden = lower_precision(jax.nn.silu(gating) * upward)
    return valid_rows * (hidden_one + lower_backward(matrix_product(mixed_hidden, w_downward)))

def to_natural(dealt_array):
    front_part = dealt_array[:, 0]
    back_part = dealt_array[:, 1].reshape(SEQS, N_CTX, BLK, MODEL_WIDTH)[:, ::-1].reshape(SEQS, HALF, MODEL_WIDTH)
    return jnp.concatenate([front_part, back_part], axis=1)

def to_dealt(natural_array):
    front_part = natural_array[:, :HALF]
    back_part = natural_array[:, HALF:].reshape(SEQS, N_CTX, BLK, MODEL_WIDTH)[:, ::-1].reshape(SEQS, HALF, MODEL_WIDTH)
    return jnp.stack([front_part, back_part], axis=1)

def reference(inputs, lengths, attn_gain, query_weight, key_matrix, value_matrix, output_weight, ffn_gain, gate_weight, up_weight, down_weight, cotangent):
    params = tuple((weight.astype(jnp.float32) for weight in (query_weight, key_matrix, value_matrix, output_weight, gate_weight, up_weight, down_weight, attn_gain, ffn_gain)))
    tokens = to_natural(inputs.astype(jnp.float32))

    def forward(params_in, tokens_in):

        def one_slot(slot_item):
            return jax.checkpoint(layer_slot)(params_in, slot_item[0], slot_item[1])
        return lax.map(one_slot, (tokens_in, lengths))
    result, pullback = jax.vjp(forward, params, tokens)
    param_grads, token_grad = pullback(to_natural(cotangent.astype(jnp.float32)))
    grad_query, grad_key, grad_value, grad_output, grad_gate, grad_up, grad_down, grad_gain_one, grad_gain_two = param_grads
    return (to_dealt(result).astype(jnp.bfloat16), to_dealt(token_grad).astype(jnp.bfloat16), grad_gain_one, grad_query, grad_key, grad_value, grad_output, grad_gain_two, grad_gate, grad_up, grad_down)
```

```python
import itertools

import jax
import jax.numpy as jnp
from jax import lax
from jax.experimental import pallas as pl
from jax.experimental.pallas import tpu as pltpu
from jax.sharding import Mesh
from jax.sharding import PartitionSpec as P

HEAD = 256
BLK = 128
EPS = 1e-06
ROPE_BASE = 1000042.0
AXES = ("zh", "zl", "y", "x", "c")
TEAM = ("y", "zl")
PEERS = ("zh", "x", "c")
ROWS_T = (((0,), (0,)), ((), ()))
COLS_T = (((1,), (1,)), ((), ()))
F32 = jnp.float32
BF16 = jnp.bfloat16


def offsets(sizes, axes):
    return [dict(zip(axes, o)) for o in itertools.product(*(range(sizes[a]) for a in axes))]


def exchange(jobs, collective_id):
    sizes = {a: lax.axis_size(a) for a in AXES}
    plans = []
    n_sems = 0
    reached = set()
    for kind, x, layout, orders in jobs:
        plan = []
        if kind == "gather":
            rows = x.shape[0] // len(orders)
            for part, order in enumerate(orders):
                for off in offsets(sizes, order):
                    used = [i for i, a in enumerate(order) if off[a]]
                    last = used[-1] if used else -1
                    sends = []
                    for a in order[last + 1 :]:
                        for d in range(1, sizes[a]):
                            sends.append((a, d, n_sems))
                            n_sems += 1
                            reached.add(tuple(d if b == a else 0 for b in AXES))
                    plan.append((len(used), part, part * rows, rows, order, off, sends))
        else:
            for off in offsets(sizes, layout):
                if any(off.values()):
                    plan.append((off, n_sems))
                    n_sems += 1
                    reached.add(tuple(off.get(b, 0) for b in AXES))
        plans.append(plan)
    count = len(jobs)

    def kernel(*refs):
        ins, outs = refs[:count], refs[count : 2 * count]
        send_sem, recv_sem, local_sem = refs[2 * count :]
        here = {a: lax.axis_index(a) for a in AXES}

        def moved(off, sign=1):
            return {a: lax.rem(here[a] + (sign * off.get(a, 0)) % sizes[a], sizes[a]) for a in AXES}

        def place(at, layout):
            index = 0
            for a in layout:
                index = index * sizes[a] + at[a]
            return index

        def device(at):
            return tuple(at[a] for a in AXES)

        barrier = pltpu.get_barrier_semaphore()
        for off in sorted(reached):
            pl.semaphore_signal(
                barrier,
                inc=1,
                device_id=device(moved(dict(zip(AXES, off)))),
                device_id_type=pl.DeviceIdType.MESH,
            )
        pl.semaphore_wait(barrier, len(reached))

        def copy(src, dst, sem, at):
            return pltpu.make_async_remote_copy(
                src_ref=src,
                dst_ref=dst,
                send_sem=send_sem.at[sem],
                recv_sem=recv_sem.at[sem],
                device_id=device(at),
                device_id_type=pl.DeviceIdType.MESH,
            )

        locals_, sent, swaps, steps = [], [], [], []
        for number, (kind, _, layout, _) in enumerate(jobs):
            mine = place(here, layout)
            src = ins[number] if kind == "gather" else ins[number].at[mine]
            locals_.append(pltpu.make_async_copy(src, outs[number].at[mine], local_sem.at[number]))
            if kind == "swap":
                for off, sem in plans[number]:
                    to = moved(off)
                    swaps.append(
                        copy(ins[number].at[place(to, layout)], outs[number].at[mine], sem, to)
                    )
            else:
                steps.extend((step, number) for step in plans[number])
        steps.sort(key=lambda s: (s[0][0], s[0][1], s[1]))
        arrivals = {}
        for (hops, part, row, rows, order, off, sends), number in steps:
            layout = jobs[number][2]
            window = pl.ds(row, rows)
            owner = moved(off)
            spot = outs[number].at[place(owner, layout), window]
            if hops:
                arrivals[number, part, tuple(sorted(off.items()))].wait_recv()
            source = spot if hops else ins[number].at[window]
            for a, d, sem in sends:
                to = moved({a: d})
                cp = copy(source, spot, sem, to)
                cp.start()
                sent.append(cp)
                came = dict(off)
                came[a] = (-d) % sizes[a]
                arrivals[number, part, tuple(sorted(came.items()))] = cp
            if not hops and (part, number) == (steps[-1][0][1], steps[-1][1]):
                pass
        for cp in swaps:
            cp.start()
        for cp in locals_:
            cp.start()
        for cp in swaps:
            cp.wait_recv()
        for cp in sent + swaps:
            cp.wait_send()
        for cp in locals_:
            cp.wait()

    shapes = []
    for kind, x, layout, _ in jobs:
        n = 1
        for a in layout:
            n *= sizes[a]
        shape = (n,) + x.shape if kind == "gather" else x.shape
        shapes.append(jax.ShapeDtypeStruct(shape, x.dtype))
    return pl.pallas_call(
        kernel,
        out_shape=shapes,
        in_specs=[pl.BlockSpec(memory_space=pl.ANY)] * count,
        out_specs=[pl.BlockSpec(memory_space=pl.ANY)] * count,
        scratch_shapes=[
            pltpu.SemaphoreType.DMA((n_sems,)),
            pltpu.SemaphoreType.DMA((n_sems,)),
            pltpu.SemaphoreType.DMA((count,)),
        ],
        compiler_params=pltpu.CompilerParams(
            collective_id=collective_id, has_side_effects=True
        ),
    )(*[job[1] for job in jobs])


def dot(a, b, dims=None):
    if dims is None:
        return jnp.dot(a, b, preferred_element_type=F32)
    return lax.dot_general(a, b, dims, preferred_element_type=F32)


def rotate(t, cos, sin):
    half = t.shape[-1] // 2
    front, back = t[..., :half], t[..., half:]
    return jnp.concatenate([front * cos - back * sin, back * cos + front * sin], axis=-1)


def rms_scale(values):
    return lax.rsqrt(jnp.mean(values * values, axis=-1, keepdims=True) + EPS)


def positions(members):
    total = lax.axis_size("zh") * lax.axis_size("zl")
    half = jnp.arange(2)[None, :, None]
    row = jnp.arange(BLK)[None, None, :]
    j = members[:, None, None]
    return (jnp.where(half == 0, j, 2 * total - 1 - j) * BLK + row).reshape(-1)


GATHER_TEAM = (("y", "zl"), ("zl", "y"))


def on_device(
    inputs,
    lengths,
    attn_gain,
    query_weight,
    key_matrix,
    value_matrix,
    output_weight,
    ffn_gain,
    gate_weight,
    up_weight,
    down_weight,
    cotangent,
):
    size = {a: lax.axis_size(a) for a in AXES}
    at = {a: lax.axis_index(a) for a in AXES}
    width = inputs.shape[3]
    own = inputs.shape[1] * inputs.shape[2]
    rows = query_weight.shape[0]
    n_dev = width // rows
    team = size["y"] * size["zl"]
    q_cols = query_weight.shape[1] // team
    kv_cols = key_matrix.shape[1] // team
    ff_rows = down_weight.shape[0]
    ff = gate_weight.shape[1] // team
    heads = q_cols // HEAD
    scaling = HEAD**-0.5

    def by_team(w):
        return w.reshape(rows, team, -1).transpose(1, 0, 2)

    def ff_by_team(w):
        cut = w.reshape(rows, size["zh"], size["zl"], size["y"], size["x"] * size["c"] * ff_rows)
        return cut.transpose(3, 2, 0, 1, 4).reshape(team, rows, ff)

    attn_cut = jnp.concatenate(
        [by_team(query_weight), by_team(key_matrix), by_team(value_matrix)], axis=2
    )
    ffn_cut = jnp.concatenate([ff_by_team(gate_weight), ff_by_team(up_weight)], axis=2)
    tile = jnp.zeros((8, 128), F32)
    tile = tile.at[0, :rows].set(attn_gain.astype(F32))
    tile = tile.at[0, 64 : 64 + rows].set(ffn_gain.astype(F32))
    tile = tile.at[1].set(lengths[0].astype(F32))
    tiles, attn_part, ffn_part = exchange(
        [
            ("gather", tile, AXES, (("c", "x", "y", "zl", "zh"),)),
            ("swap", attn_cut, TEAM, None),
            ("swap", ffn_cut, TEAM, None),
        ],
        1,
    )
    gain_one = tiles[:, 0, :rows].reshape(1, width)
    gain_two = tiles[:, 0, 64 : 64 + rows].reshape(1, width)
    slots = tiles[: n_dev // (size["zh"] * size["zl"]), 1, 0].reshape(
        size["y"], size["x"], size["c"]
    )
    lens = slots[:, at["x"], at["c"]].astype(jnp.int32)

    n_peer = size["zh"] * size["x"] * size["c"]
    per_head = n_dev // team

    def head_home(i):
        f, t = i // per_head, i % per_head
        c, t = t % size["c"], t // size["c"]
        x, zh = t % size["x"], t // size["x"]
        zl, y = f % size["zl"], f // size["zl"]
        return (((zh * size["zl"] + zl) * size["y"] + y) * size["x"] + x) * size["c"] + c

    homes = [(i, head_home(i)) for i in range(n_dev)]
    out_part = lax.ppermute(output_weight, AXES, homes)
    w_down = lax.all_gather(down_weight, PEERS, axis=0, tiled=True)

    def natural(w):
        w = w.reshape(size["zh"], size["x"], size["c"], size["y"], size["zl"], rows, -1)
        return w.transpose(0, 4, 3, 1, 2, 5, 6).reshape(width, -1)

    def peer_major(w):
        w = w.reshape(size["zh"], size["zl"], size["y"], size["x"], size["c"], rows, -1)
        return w.transpose(0, 3, 4, 2, 1, 5, 6).reshape(width, -1)

    w_ffn = natural(lax.all_gather(ffn_part, PEERS, axis=0))
    w_gate, w_up = w_ffn[:, :ff], w_ffn[:, ff:]

    my_pos = positions((at["zh"] * size["zl"] + at["zl"])[None])
    my_len = lengths[0]
    valid = (my_pos < my_len).astype(F32)[:, None]
    zl_all = jnp.arange(size["zl"])
    q_pos = positions(at["zh"] * size["zl"] + zl_all)
    k_pos = positions(jnp.arange(size["zh"] * size["zl"]))
    half = HEAD // 2
    freq = ROPE_BASE ** (-2.0 * jnp.arange(half).astype(F32) / HEAD)
    angles = q_pos.astype(F32)[:, None] * freq[None, :]
    cos = jnp.tile(jnp.cos(angles), (size["y"], 1))[:, None, :]
    sin = jnp.tile(jnp.sin(angles), (size["y"], 1))[:, None, :]

    tokens = inputs.reshape(own, width).astype(F32)
    scale_one = rms_scale(tokens)
    norm_one = (tokens * scale_one * gain_one).astype(BF16)
    norm_one_all, w_attn, w_out = exchange(
        [
            ("gather", norm_one, TEAM, GATHER_TEAM),
            ("gather", attn_part, PEERS, (PEERS,)),
            ("gather", out_part, PEERS, (PEERS,)),
        ],
        2,
    )
    n_tok = team * own
    norm_one_all = norm_one_all.reshape(n_tok, width)
    w_attn = natural(w_attn)
    w_out = w_out.reshape(q_cols, width)
    qkv = dot(norm_one_all, w_attn)
    q = rotate(qkv[:, :q_cols].reshape(n_tok, heads, HEAD), cos, sin).astype(BF16)
    k = rotate(qkv[:, q_cols : q_cols + kv_cols].reshape(n_tok, 1, HEAD), cos, sin).astype(BF16)
    v = qkv[:, q_cols + kv_cols :].astype(BF16)
    kv = jnp.concatenate([k.reshape(n_tok, kv_cols), v], axis=1)
    gy = valid * cotangent.reshape(own, width).astype(F32)
    kv_all, gd_all = exchange(
        [
            ("gather", kv, ("zh",), (("zh",),)),
            ("gather", gy.astype(BF16), TEAM, GATHER_TEAM),
        ],
        3,
    )
    gd_all = gd_all.reshape(n_tok, width)
    n_slot = size["y"]
    n_q = n_tok // n_slot
    q = q.reshape(n_slot, n_q, heads, HEAD)
    kv_all = kv_all.reshape(size["zh"], n_slot, n_q, 2 * kv_cols).transpose(1, 0, 2, 3)
    kv_all = kv_all.reshape(n_slot, size["zh"] * n_q, 2 * kv_cols)
    k_all, v_all = kv_all[:, :, :kv_cols], kv_all[:, :, kv_cols:]
    allowed = (k_pos[None, None, :] <= q_pos[None, :, None]) & (
        k_pos[None, None, :] < lens[:, None, None]
    )
    scores = jnp.einsum("bqgd,bkd->bgqk", q, k_all, preferred_element_type=F32) * scaling
    scores = jnp.where(allowed[:, None], scores, -jnp.inf)
    peak = jnp.max(scores, axis=-1, keepdims=True)
    exps = jnp.exp(scores - peak)
    prob = exps / jnp.sum(exps, axis=-1, keepdims=True)
    prob_b = prob.astype(BF16)
    o = jnp.einsum("bgqk,bkd->bqgd", prob_b, v_all, preferred_element_type=F32)
    o = o.reshape(n_tok, q_cols).astype(BF16)

    def team_sum(parts):
        return sum(parts[i].astype(F32) for i in range(team))

    def blocks(partial):
        return partial.astype(BF16).reshape(team, own, width)

    (o_parts,) = exchange([("swap", blocks(dot(o, w_out)), TEAM, None)], 4)
    h1 = tokens + team_sum(o_parts)
    scale_two = rms_scale(h1)
    norm_two = (h1 * scale_two * gain_two).astype(BF16)
    (norm_two_all,) = exchange([("gather", norm_two, TEAM, GATHER_TEAM)], 5)
    norm_two_all = norm_two_all.reshape(n_tok, width)

    gate = dot(norm_two_all, w_gate)
    up = dot(norm_two_all, w_up)
    sg = jax.nn.sigmoid(gate)
    mixed = (gate * sg * up).astype(BF16)
    gm = dot(gd_all, w_down, COLS_T)
    g_gate = (gm * up * sg * (1.0 + gate * (1.0 - sg))).astype(BF16)
    g_up = (gm * gate * sg).astype(BF16)
    down_term = dot(mixed, gd_all, ROWS_T).astype(BF16)
    down_grad = lax.psum_scatter(down_term, PEERS, scatter_dimension=0, tiled=True)
    gate_term = dot(norm_two_all, g_gate, ROWS_T)
    up_term = dot(norm_two_all, g_up, ROWS_T)
    ffn_term = peer_major(jnp.concatenate([gate_term, up_term], axis=1).astype(BF16))
    ffn_sum = lax.psum_scatter(ffn_term, PEERS, scatter_dimension=0, tiled=True)
    gn2_parts = blocks(dot(g_gate, w_gate, COLS_T) + dot(g_up, w_up, COLS_T))
    (gn2_parts,) = exchange([("swap", gn2_parts, TEAM, None)], 6)
    gn2 = team_sum(gn2_parts) * gain_two
    gh1 = gy + scale_two * gn2 - h1 * scale_two**3 * jnp.mean(h1 * gn2, axis=-1, keepdims=True)
    (ga_all,) = exchange([("gather", gh1.astype(BF16), TEAM, GATHER_TEAM)], 7)
    ga_all = ga_all.reshape(n_tok, width)

    go = dot(ga_all, w_out, COLS_T).astype(BF16).reshape(n_slot, n_q, heads, HEAD)
    gp = jnp.einsum("bqgd,bkd->bgqk", go, v_all, preferred_element_type=F32)
    delta = jnp.sum(prob * gp, axis=-1, keepdims=True)
    gs = (prob * (gp - delta)).astype(BF16)
    gq_rot = jnp.einsum("bgqk,bkd->bqgd", gs, k_all, preferred_element_type=F32) * scaling
    gk_rot = jnp.einsum("bgqk,bqgd->bkd", gs, q, preferred_element_type=F32) * scaling
    gv_sum = jnp.einsum("bgqk,bqgd->bkd", prob_b, go, preferred_element_type=F32)
    gkv = jnp.concatenate([gk_rot, gv_sum], axis=-1).astype(BF16)
    gkv = gkv.reshape(n_slot, size["zh"], n_q, 2 * kv_cols).transpose(1, 0, 2, 3)
    gkv = gkv.reshape(size["zh"], n_tok, 2 * kv_cols)
    out_parts = blocks(dot(mixed, w_down))
    gkv_parts, out_parts = exchange(
        [("swap", gkv, ("zh",), None), ("swap", out_parts, TEAM, None)], 8
    )
    outputs = (valid * (h1 + team_sum(out_parts))).astype(BF16).reshape(inputs.shape)
    gkv = sum(gkv_parts[i].astype(F32) for i in range(size["zh"]))
    gq = rotate(gq_rot.reshape(n_tok, heads, HEAD), cos, -sin).astype(BF16)
    gk = rotate(gkv[:, :kv_cols].reshape(n_tok, 1, HEAD), cos, -sin).astype(BF16)
    g_qkv = jnp.concatenate(
        [gq.reshape(n_tok, q_cols), gk.reshape(n_tok, kv_cols), gkv[:, kv_cols:].astype(BF16)],
        axis=1,
    )
    attn_term = peer_major(dot(norm_one_all, g_qkv, ROWS_T).astype(BF16))
    attn_sum = lax.psum_scatter(attn_term, PEERS, scatter_dimension=0, tiled=True)
    out_term = dot(o, ga_all, ROWS_T).astype(BF16)
    out_sum = lax.psum_scatter(out_term, PEERS, scatter_dimension=0, tiled=True)
    output_grad = lax.ppermute(out_sum, AXES, [(b, a) for a, b in homes]).astype(F32)
    gn1_parts = blocks(dot(g_qkv, w_attn, COLS_T))
    gn1_parts, attn_sum, ffn_sum = exchange(
        [
            ("swap", gn1_parts, TEAM, None),
            ("swap", attn_sum.reshape(team, rows, -1), TEAM, None),
            ("swap", ffn_sum.reshape(team, rows, -1), TEAM, None),
        ],
        9,
    )
    gn1 = team_sum(gn1_parts) * gain_one
    g_tokens = (
        gh1
        + scale_one * gn1
        - tokens * scale_one**3 * jnp.mean(tokens * gn1, axis=-1, keepdims=True)
    )
    input_grad = g_tokens.astype(BF16).reshape(inputs.shape)

    def from_team(part):
        return part.astype(F32).transpose(1, 0, 2).reshape(rows, -1)

    def ff_from_team(part):
        cut = part.astype(F32).reshape(
            size["y"], size["zl"], rows, size["zh"], size["x"] * size["c"] * ff_rows
        )
        return cut.transpose(2, 3, 1, 0, 4).reshape(rows, -1)

    query_grad = from_team(attn_sum[:, :, :q_cols])
    key_grad = from_team(attn_sum[:, :, q_cols : q_cols + kv_cols])
    value_grad = from_team(attn_sum[:, :, q_cols + kv_cols :])
    gate_grad = ff_from_team(ffn_sum[:, :, :ff])
    up_grad = ff_from_team(ffn_sum[:, :, ff:])

    def against(w, g):
        return jnp.sum(w.astype(F32) * g, axis=1)

    attn_gain_grad = (
        against(query_weight, query_grad)
        + against(key_matrix, key_grad)
        + against(value_matrix, value_grad)
    ) / attn_gain.astype(F32)
    ffn_gain_grad = (against(gate_weight, gate_grad) + against(up_weight, up_grad)) / (
        ffn_gain.astype(F32)
    )
    return (
        outputs,
        input_grad,
        attn_gain_grad,
        query_grad,
        key_grad,
        value_grad,
        output_grad,
        ffn_gain_grad,
        gate_grad,
        up_grad,
        down_grad.astype(F32),
    )


def solution(mesh):
    ctx, fsdp = mesh.shape["ctx"], mesh.shape["fsdp"]
    grid = Mesh(mesh.devices.reshape(ctx // 2, 2, 2, fsdp // 4, 2), AXES)
    act = P(("y", "x", "c"), None, ("zh", "zl"), None)
    row = P(AXES)
    return jax.shard_map(
        on_device,
        mesh=grid,
        in_specs=(act, P(("y", "x", "c"))) + (row,) * 9 + (act,),
        out_specs=(act, act) + (row,) * 9,
        check_vma=False,
    )
```

```python
import itertools
import math

import jax
import jax.numpy as jnp
from jax import lax
from jax.experimental import pallas as pl
from jax.experimental.pallas import tpu as pltpu
from jax.sharding import Mesh
from jax.sharding import PartitionSpec as P

HEAD = 256
VMEM_LIMIT = 48 << 20
BLK = 128
EPS = 1e-06
ROPE_BASE = 1000042.0
AXES = ("zh", "zl", "y", "x", "c")
TEAM = ("zl", "y")
SLOTS = ("y", "zl")
SHARES = ("c", "x", "zh")
OWNERS = ("zl", "y", "c")
ROWS_T = (((0,), (0,)), ((), ()))
PAIR_ROWS_T = (((0, 1), (0, 1)), ((), ()))
COLS_T = (((1,), (1,)), ((), ()))
F32 = jnp.float32
BF16 = jnp.bfloat16


def offsets(sizes, axes):
    return [dict(zip(axes, o)) for o in itertools.product(*(range(sizes[a]) for a in axes))]


def place(at, layout, sizes):
    index = 0
    for a in layout:
        index = index * sizes[a] + at[a]
    return index


class Gather:
    def __init__(self, x, layout, order, chunks=1, dim=0, rank=1):
        self.rank = rank
        self.x, self.layout, self.chunks, self.dim = x, layout, chunks, dim
        self.orders = [order] * chunks if isinstance(order[0], str) else order
        self.chunks = len(self.orders)

    def out_shape(self, sizes):
        return (math.prod(sizes[a] for a in self.layout),) + self.x.shape

    def own_shape(self, sizes):
        return self.x.shape

    def cut(self, ref, part):
        rows = self.x.shape[self.dim] // self.chunks
        return ref.at[(slice(None),) * self.dim + (pl.ds(part * rows, rows),)]

    def spot(self, out, owner, off, sizes):
        return out.at[place(owner, self.layout, sizes)]


class PairGather(Gather):
    def out_shape(self, sizes):
        return (2, math.prod(sizes[a] for a in self.layout)) + self.x.shape

    def spot(self, out, owner, off, sizes):
        return out.at[off["c"], place(owner, self.layout, sizes)]


class RowGather(Gather):
    def out_shape(self, sizes):
        zl, y, rows, columns = self.x.shape
        return (sizes["x"], sizes["zh"], zl, y, sizes["c"], rows, columns)

    def spot(self, out, owner, off, sizes):
        return out.at[owner["x"], owner["zh"], :, :, owner["c"]]


class Swap:
    def __init__(self, x, layout):
        self.x, self.layout = x, layout

    def out_shape(self, sizes):
        return self.x.shape

    def own_shape(self, sizes):
        return self.x.shape[1:]

    def offsets(self, sizes):
        return offsets(sizes, self.layout)

    def pair(self, x, out, here, to, off, sizes):
        return x.at[place(to, self.layout, sizes)], out.at[place(here, self.layout, sizes)]


class Halves:
    def __init__(self, x):
        self.x = x

    def out_shape(self, sizes):
        rows, columns = self.x.shape
        return (2, rows, columns // 2)

    def own_shape(self, sizes):
        rows, columns = self.x.shape
        return (rows, columns // 2)

    def offsets(self, sizes):
        return offsets(sizes, ("c",))

    def pair(self, x, out, here, to, off, sizes):
        width = self.x.shape[1] // 2
        start = pl.multiple_of(to["c"] * width, 128)
        return x.at[:, pl.ds(start, width)], out.at[off["c"]]


def exchange(jobs, collective_id, micros=50):
    sizes = {a: lax.axis_size(a) for a in AXES}
    n_sems = 0
    reached = set()
    steps, swaps = [], []
    for number, job in enumerate(jobs):
        if isinstance(job, Gather):
            for part, order in enumerate(job.orders):
                for off in offsets(sizes, order):
                    used = [i for i, a in enumerate(order) if off[a]]
                    sends = []
                    for a in order[used[-1] + 1 if used else 0 :]:
                        for d in range(1, sizes[a]):
                            sends.append((a, d, n_sems))
                            n_sems += 1
                            reached.add(tuple(d if b == a else 0 for b in AXES))
                    steps.append((job.rank, part + 2 * len(used), len(used), number, part, off, sends))
        else:
            for off in job.offsets(sizes):
                if any(off.values()):
                    swaps.append((number, off, n_sems))
                    n_sems += 1
                    reached.add(tuple(off.get(b, 0) for b in AXES))
    steps.sort(key=lambda s: s[:4])
    count = len(jobs)

    def kernel(*refs):
        ins, outs = refs[:count], refs[count : 2 * count]
        stages = refs[2 * count : 3 * count]
        send_sem, recv_sem, local_sem = refs[3 * count :]
        here = {a: lax.axis_index(a) for a in AXES}

        def moved(off):
            return {
                a: lax.rem(here[a] + off[a], sizes[a]) if off.get(a, 0) else here[a] for a in AXES
            }

        def device(at):
            return tuple(at[a] for a in AXES)

        barrier = pltpu.get_barrier_semaphore()
        for off in sorted(reached):
            pl.semaphore_signal(
                barrier,
                inc=1,
                device_id=device(moved(dict(zip(AXES, off)))),
                device_id_type=pl.DeviceIdType.MESH,
            )
        pl.semaphore_wait(barrier, len(reached))

        def copy(src, dst, sem, at):
            return pltpu.make_async_remote_copy(
                src_ref=src,
                dst_ref=dst,
                send_sem=send_sem.at[sem],
                recv_sem=recv_sem.at[sem],
                device_id=device(at),
                device_id_type=pl.DeviceIdType.MESH,
            )

        local, sent, received = [], [], []
        arrivals = {}

        def pass_on(step):
            _, _, hops, number, part, off, sends = step
            job = jobs[number]
            spot = job.cut(job.spot(outs[number], moved(off), off, sizes), part)
            if hops:
                arrivals[number, part, tuple(sorted(off.items()))].wait_recv()
            source = spot if hops else job.cut(ins[number], part)
            for a, d, sem in sends:
                there = dict(off)
                there[a] = (-d) % sizes[a]
                dst = job.cut(job.spot(outs[number], moved(off), there, sizes), part)
                cp = copy(source, dst, sem, moved({a: d}))
                cp.start()
                sent.append(cp)
                arrivals[number, part, tuple(sorted(there.items()))] = cp

        for number, job in enumerate(jobs):
            none = {a: 0 for a in AXES}
            if isinstance(job, Gather):
                src, dst = ins[number], job.spot(outs[number], here, none, sizes)
            else:
                src, dst = job.pair(ins[number], outs[number], here, here, none, sizes)
            load = pltpu.make_async_copy(src, stages[number], local_sem.at[number, 0])
            load.start()
            local.append((load, pltpu.make_async_copy(stages[number], dst, local_sem.at[number, 1])))
        for step in steps:
            if not step[1]:
                pass_on(step)
        for number, off, sem in swaps:
            to = moved(off)
            src, dst = jobs[number].pair(ins[number], outs[number], here, to, off, sizes)
            cp = copy(src, dst, sem, to)
            cp.start()
            sent.append(cp)
            received.append(cp)
        for load, store in local:
            load.wait()
            store.start()
        for step in steps:
            if step[1]:
                pass_on(step)
        for cp in received:
            cp.wait_recv()
        for cp in sent:
            cp.wait_send()
        for _, store in local:
            store.wait()

    return pl.pallas_call(
        kernel,
        out_shape=[jax.ShapeDtypeStruct(job.out_shape(sizes), job.x.dtype) for job in jobs],
        in_specs=[pl.BlockSpec(memory_space=pl.ANY)] * count,
        out_specs=[pl.BlockSpec(memory_space=pl.ANY)] * count,
        scratch_shapes=[pltpu.VMEM(job.own_shape(sizes), job.x.dtype) for job in jobs]
        + [
            pltpu.SemaphoreType.DMA((n_sems,)),
            pltpu.SemaphoreType.DMA((n_sems,)),
            pltpu.SemaphoreType.DMA((count, 2)),
        ],
        cost_estimate=pl.CostEstimate(
            flops=0, bytes_accessed=micros * 3_000_000, transcendentals=0
        ),
        compiler_params=pltpu.CompilerParams(
            collective_id=collective_id, has_side_effects=True, vmem_limit_bytes=VMEM_LIMIT
        ),
    )(*[job.x for job in jobs])


def sum_over(term, axis):
    size = lax.axis_size(axis)
    me = lax.axis_index(axis)
    while size > 1:
        size //= 2
        rows = term.shape[0] // 2
        pairs = [(i, i ^ size) for i in range(lax.axis_size(axis))]
        side = (me // size) % 2
        kept = lax.dynamic_slice_in_dim(term, side * rows, rows)
        other = lax.ppermute(
            lax.dynamic_slice_in_dim(term, (1 - side) * rows, rows), axis, pairs
        )
        term = kept.astype(F32) + other.astype(F32)
        if size > 1:
            term = term.astype(BF16)
    return term


def dot(a, b, dims=None):
    if dims is None:
        return jnp.dot(a, b, preferred_element_type=F32)
    return lax.dot_general(a, b, dims, preferred_element_type=F32)


def rotate(t, cos, sin):
    half = t.shape[-1] // 2
    front, back = t[..., :half], t[..., half:]
    return jnp.concatenate([front * cos - back * sin, back * cos + front * sin], axis=-1)


def rms_scale(values):
    return lax.rsqrt(jnp.mean(values * values, axis=-1, keepdims=True) + EPS)


def positions(members):
    total = lax.axis_size("zh") * lax.axis_size("zl")
    half = jnp.arange(2)[None, :, None]
    row = jnp.arange(BLK)[None, None, :]
    j = members[:, None, None]
    return (jnp.where(half == 0, j, 2 * total - 1 - j) * BLK + row).reshape(-1)


OUTWARD = ("zh", "x", "c")
TO_TEAM = (("zl", "y", "c"), ("zl", "y", "c"))
TO_TEAM_EVEN = (("zl", "y", "c"), ("y", "zl", "c"))


def on_device(
    inputs,
    lengths,
    attn_gain,
    query_weight,
    key_matrix,
    value_matrix,
    output_weight,
    ffn_gain,
    gate_weight,
    up_weight,
    down_weight,
    cotangent,
):
    size = {a: lax.axis_size(a) for a in AXES}
    at = {a: lax.axis_index(a) for a in AXES}
    width = inputs.shape[3]
    own = inputs.shape[1] * inputs.shape[2]
    rows = query_weight.shape[0]
    n_dev = width // rows
    team = size["y"] * size["zl"]
    q_cols = query_weight.shape[1] // team
    kv_cols = key_matrix.shape[1] // team
    ff_rows = down_weight.shape[0]
    ff = gate_weight.shape[1] // team
    heads = q_cols // HEAD
    n_tok = team * own
    scaling = HEAD**-0.5

    def by_team(w):
        return w.reshape(rows, team, -1).transpose(1, 0, 2)

    def ff_by_team(w):
        cut = w.reshape(rows, *(size[a] for a in AXES), ff_rows)
        return cut.transpose(2, 3, 0, 5, 4, 1, 6).reshape(team, rows, ff)

    attn_cut = jnp.concatenate(
        [by_team(query_weight), by_team(key_matrix), by_team(value_matrix)], axis=2
    )
    tile = jnp.zeros((8, 128), F32)
    tile = tile.at[0, :rows].set(attn_gain.astype(F32))
    tile = tile.at[0, 64 : 64 + rows].set(ffn_gain.astype(F32))
    tile = tile.at[1].set(lengths[0].astype(F32))
    tiles, attn_part, gate_part, up_part = exchange(
        [
            Gather(tile, AXES, ("c", "x", "y", "zl", "zh"), rank=0),
            Swap(attn_cut, TEAM),
            Swap(ff_by_team(gate_weight), TEAM),
            Swap(ff_by_team(up_weight), TEAM),
        ],
        1,
    )
    w_down = lax.all_gather(down_weight, SHARES, axis=0, tiled=True)
    gain_one = tiles[:, 0, :rows].reshape(1, width)
    gain_two = tiles[:, 0, 64 : 64 + rows].reshape(1, width)
    slots = tiles[: n_dev // (size["zh"] * size["zl"]), 1, 0].reshape(
        size["y"], size["x"], size["c"]
    )
    lens = slots[:, at["x"], at["c"]].astype(jnp.int32)

    per_head = n_dev // team

    def head_home(i):
        f, t = i // per_head, i % per_head
        zl, y = f // size["y"], f % size["y"]
        zh, t = t % size["zh"], t // size["zh"]
        x, c = t % size["x"], t // size["x"]
        return (((zh * size["zl"] + zl) * size["y"] + y) * size["x"] + x) * size["c"] + c

    homes = [(i, head_home(i)) for i in range(n_dev)]
    out_part = lax.ppermute(output_weight, AXES, homes)

    def row_gather(part):
        part = part.reshape(size["zl"], size["y"], rows, -1)
        return RowGather(part, None, OUTWARD, chunks=rows // 16, dim=2)

    def spread(v):
        cut = v.reshape(own, size["zh"], size["zl"], size["y"], size["x"], size["c"] * rows)
        return cut.transpose(0, 4, 1, 2, 3, 5).reshape(own, width)

    def natural(v):
        cut = v.reshape(own, size["x"], size["zh"], size["zl"], size["y"], size["c"] * rows)
        return cut.transpose(0, 2, 3, 4, 1, 5).reshape(own, width)

    my_pos = positions((at["zh"] * size["zl"] + at["zl"])[None])
    valid = (my_pos < lengths[0]).astype(F32)[:, None]
    q_pos = positions(at["zh"] * size["zl"] + jnp.arange(size["zl"]))
    k_pos = positions(jnp.arange(size["zh"] * size["zl"]))
    half = HEAD // 2
    freq = ROPE_BASE ** (-2.0 * jnp.arange(half).astype(F32) / HEAD)
    angles = q_pos.astype(F32)[:, None] * freq[None, :]
    cos = jnp.tile(jnp.cos(angles), (size["y"], 1))[:, None, :]
    sin = jnp.tile(jnp.sin(angles), (size["y"], 1))[:, None, :]

    tokens = inputs.reshape(own, width).astype(F32)
    scale_one = rms_scale(tokens)
    norm_one = (tokens * scale_one * gain_one).astype(BF16)
    norm_one_pair, w_attn, w_out = exchange(
        [
            PairGather(spread(norm_one), SLOTS, TO_TEAM),
            row_gather(attn_part),
            Gather(out_part, SHARES, OUTWARD, chunks=rows // 16),
        ],
        2,
    )
    norm_one_pair = norm_one_pair.reshape(2, n_tok, width)
    w_attn = w_attn.reshape(width, -1)
    w_out = w_out.reshape(q_cols, width)
    qkv = dot(norm_one_pair[0], w_attn)
    q = rotate(qkv[:, :q_cols].reshape(n_tok, heads, HEAD), cos, sin).astype(BF16)
    k = rotate(qkv[:, q_cols : q_cols + kv_cols].reshape(n_tok, 1, HEAD), cos, sin).astype(BF16)
    v = qkv[:, q_cols + kv_cols :].astype(BF16)
    kv = jnp.concatenate([k.reshape(n_tok, kv_cols), v], axis=1)
    gy = valid * cotangent.reshape(own, width).astype(F32)
    kv_all, gd_pair = exchange(
        [Gather(kv, ("zh",), ("zh",)), PairGather(gy.astype(BF16), SLOTS, TO_TEAM)], 3
    )
    gd_pair = gd_pair.reshape(2, n_tok, width)
    n_slot = size["y"]
    n_q = n_tok // n_slot
    q = q.reshape(n_slot, n_q, heads, HEAD)
    kv_all = kv_all.reshape(size["zh"], n_slot, n_q, 2 * kv_cols).transpose(1, 0, 2, 3)
    kv_all = kv_all.reshape(n_slot, size["zh"] * n_q, 2 * kv_cols)
    k_all, v_all = kv_all[:, :, :kv_cols], kv_all[:, :, kv_cols:]
    allowed = (k_pos[None, None, :] <= q_pos[None, :, None]) & (
        k_pos[None, None, :] < lens[:, None, None]
    )
    scores = jnp.einsum("bqgd,bkd->bgqk", q, k_all, preferred_element_type=F32) * scaling
    scores = jnp.where(allowed[:, None], scores, -jnp.inf)
    peak = jnp.max(scores, axis=-1, keepdims=True)
    exps = jnp.exp(scores - peak)
    prob = exps / jnp.sum(exps, axis=-1, keepdims=True)
    prob_b = prob.astype(BF16)
    o = jnp.einsum("bgqk,bkd->bqgd", prob_b, v_all, preferred_element_type=F32)
    o = o.reshape(n_tok, q_cols).astype(BF16)

    def team_sum(parts):
        return sum(parts[i].astype(F32) for i in range(team))

    def blocks(partial):
        return partial.astype(BF16).reshape(team, own, width)

    o_parts, w_gate = exchange(
        [Swap(blocks(dot(o, w_out)), SLOTS), row_gather(gate_part)], 4
    )
    w_gate = w_gate.reshape(width, ff)
    h1 = tokens + team_sum(o_parts)
    scale_two = rms_scale(h1)
    norm_two = (h1 * scale_two * gain_two).astype(BF16)
    norm_two_pair, w_up = exchange(
        [PairGather(spread(norm_two), SLOTS, TO_TEAM), row_gather(up_part)], 5
    )
    w_up = w_up.reshape(width, ff)
    norm_two_pair = norm_two_pair.reshape(2, n_tok, width)

    gate = dot(norm_two_pair[0], w_gate)
    up = dot(norm_two_pair[0], w_up)
    sg = jax.nn.sigmoid(gate)
    mixed = (gate * sg * up).astype(BF16)
    gm = dot(gd_pair[0], w_down, COLS_T)
    g_gate = (gm * up * sg * (1.0 + gate * (1.0 - sg))).astype(BF16)
    g_up = (gm * gate * sg).astype(BF16)
    gate_half, up_half, mixed_half = exchange(
        [Halves(g_gate), Halves(g_up), Halves(mixed)], 6, micros=10
    )
    tie = lax.optimization_barrier
    down_term = dot(mixed_half, gd_pair, PAIR_ROWS_T).astype(BF16)
    gn2_parts = blocks(dot(g_gate, w_gate, COLS_T) + dot(g_up, w_up, COLS_T))
    gn2_parts, down_term = tie((gn2_parts, down_term))
    down_x = sum_over(down_term, "x").astype(BF16)
    (gn2_parts,) = exchange([Swap(gn2_parts, SLOTS)], 7)
    gn2_parts, down_x = tie((gn2_parts, down_x))
    gn2 = natural(team_sum(gn2_parts)) * gain_two
    gh1 = gy + scale_two * gn2 - h1 * scale_two**3 * jnp.mean(h1 * gn2, axis=-1, keepdims=True)

    gate_term = dot(norm_two_pair, gate_half, PAIR_ROWS_T).astype(BF16)
    up_term = dot(norm_two_pair, up_half, PAIR_ROWS_T).astype(BF16)
    ga, gate_term, up_term, down_x = tie((gh1.astype(BF16), gate_term, up_term, down_x))
    gate_x = sum_over(gate_term, "x").astype(BF16)
    down_grad = sum_over(down_x, "zh")
    ga_pair, o_half = exchange([PairGather(ga, SLOTS, TO_TEAM_EVEN), Halves(o)], 8)
    ga_pair, gate_x, down_grad = tie((ga_pair, gate_x, down_grad))
    ga_pair = ga_pair.reshape(2, n_tok, width)

    go = dot(ga_pair[0], w_out, COLS_T).astype(BF16).reshape(n_slot, n_q, heads, HEAD)
    gp = jnp.einsum("bqgd,bkd->bgqk", go, v_all, preferred_element_type=F32)
    delta = jnp.sum(prob * gp, axis=-1, keepdims=True)
    gs = (prob * (gp - delta)).astype(BF16)
    gq_rot = jnp.einsum("bgqk,bkd->bqgd", gs, k_all, preferred_element_type=F32) * scaling
    gk_rot = jnp.einsum("bgqk,bqgd->bkd", gs, q, preferred_element_type=F32) * scaling
    gv_sum = jnp.einsum("bgqk,bqgd->bkd", prob_b, go, preferred_element_type=F32)
    gkv = jnp.concatenate([gk_rot, gv_sum], axis=-1).astype(BF16)
    gkv = gkv.reshape(n_slot, size["zh"], n_q, 2 * kv_cols).transpose(1, 0, 2, 3)
    gkv = gkv.reshape(size["zh"], n_tok, 2 * kv_cols)
    out_parts = blocks(dot(mixed, w_down))
    out_term = dot(o_half, ga_pair, PAIR_ROWS_T).astype(BF16)
    gkv, out_parts, gate_x, up_term, out_term = tie((gkv, out_parts, gate_x, up_term, out_term))
    up_x = sum_over(up_term, "x").astype(BF16)
    out_x = sum_over(out_term, "x").astype(BF16)
    gate_sum = sum_over(gate_x, "zh").astype(BF16)
    gkv_parts, out_parts = exchange([Swap(gkv, ("zh",)), Swap(out_parts, SLOTS)], 9)
    gkv_parts, up_x, out_x, gate_sum = tie((gkv_parts, up_x, out_x, gate_sum))
    gkv = sum(gkv_parts[i].astype(F32) for i in range(size["zh"]))
    gq = rotate(gq_rot.reshape(n_tok, heads, HEAD), cos, -sin).astype(BF16)
    gk = rotate(gkv[:, :kv_cols].reshape(n_tok, 1, HEAD), cos, -sin).astype(BF16)
    g_qkv = jnp.concatenate(
        [gq.reshape(n_tok, q_cols), gk.reshape(n_tok, kv_cols), gkv[:, kv_cols:].astype(BF16)],
        axis=1,
    )
    cols = g_qkv.shape[1] // 2
    mine = lax.dynamic_slice_in_dim(g_qkv, at["c"] * cols, cols, axis=1)
    other = lax.dynamic_slice_in_dim(g_qkv, (1 - at["c"]) * cols, cols, axis=1)
    g_qkv_half = jnp.stack([mine, lax.ppermute(other, "c", [(0, 1), (1, 0)])])
    attn_term = dot(norm_one_pair, g_qkv_half, PAIR_ROWS_T).astype(BF16)
    gn1_parts = blocks(dot(g_qkv, w_attn, COLS_T))
    gn1_parts, attn_term, up_x, out_x = tie((gn1_parts, attn_term, up_x, out_x))
    attn_x = sum_over(attn_term, "x").astype(BF16)
    up_sum = sum_over(up_x, "zh").astype(BF16)
    out_sum = sum_over(out_x, "zh").astype(BF16)
    (gn1_parts,) = exchange([Swap(gn1_parts, SLOTS)], 10)
    gn1_parts, attn_x, up_sum, out_sum = tie((gn1_parts, attn_x, up_sum, out_sum))
    attn_sum = sum_over(attn_x, "zh")
    out_sum = lax.ppermute(out_sum, AXES, [(b, a) for a, b in homes])
    outputs = (valid * (h1 + team_sum(out_parts))).astype(BF16).reshape(inputs.shape)
    n_owners = math.prod(size[a] for a in OWNERS)

    def by_owner(total):
        return total.astype(BF16).reshape(n_owners, rows, -1)

    gate_sum, up_sum = exchange([Swap(by_owner(t), OWNERS) for t in (gate_sum, up_sum)], 11)
    attn_sum, gate_sum, up_sum = tie((attn_sum, gate_sum, up_sum))
    (attn_sum,) = exchange([Swap(by_owner(attn_sum), OWNERS)], 12)
    gn1 = natural(team_sum(gn1_parts)) * gain_one
    g_tokens = (
        gh1
        + scale_one * gn1
        - tokens * scale_one**3 * jnp.mean(tokens * gn1, axis=-1, keepdims=True)
    )
    input_grad = g_tokens.astype(BF16).reshape(inputs.shape)

    def ff_natural(total):
        cut = total.reshape(
            size["zl"], size["y"], size["c"], rows, size["x"], size["zh"], ff_rows
        )
        return cut.transpose(3, 5, 0, 1, 4, 2, 6).reshape(rows, -1).astype(F32)

    def side(part):
        return part.transpose(1, 0, 2).reshape(rows, -1).astype(F32)

    attn_sum = attn_sum.reshape(team, 2, rows, -1)
    query_grad = side(attn_sum[:, 0])
    key_grad = side(attn_sum[:, 1, :, :kv_cols])
    value_grad = side(attn_sum[:, 1, :, kv_cols:])
    gate_grad = ff_natural(gate_sum)
    up_grad = ff_natural(up_sum)

    def against(w, g):
        return jnp.sum(w.astype(F32) * g, axis=1)

    attn_gain_grad = (
        against(query_weight, query_grad)
        + against(key_matrix, key_grad)
        + against(value_matrix, value_grad)
    ) / attn_gain.astype(F32)
    ffn_gain_grad = (against(gate_weight, gate_grad) + against(up_weight, up_grad)) / (
        ffn_gain.astype(F32)
    )
    return (
        outputs,
        input_grad,
        attn_gain_grad,
        query_grad,
        key_grad,
        value_grad,
        out_sum.astype(F32),
        ffn_gain_grad,
        gate_grad,
        up_grad,
        down_grad,
    )


def solution(mesh):
    ctx, fsdp = mesh.shape["ctx"], mesh.shape["fsdp"]
    grid = Mesh(mesh.devices.reshape(ctx // 2, 2, 2, fsdp // 4, 2), AXES)
    act = P(("y", "x", "c"), None, ("zh", "zl"), None)
    row = P(AXES)
    return jax.shard_map(
        on_device,
        mesh=grid,
        in_specs=(act, P(("y", "x", "c"))) + (row,) * 9 + (act,),
        out_specs=(act, act) + (row,) * 9,
        check_vma=False,
    )
```

```python
import itertools
import math

import jax
import jax.numpy as jnp
from jax import lax
from jax.experimental import pallas as pl
from jax.experimental.pallas import tpu as pltpu
from jax.sharding import Mesh
from jax.sharding import PartitionSpec as P

HEAD = 256
VMEM_LIMIT = 48 << 20
FFN_VMEM_LIMIT = 62 << 20
BLK = 128
EPS = 1e-06
ROPE_BASE = 1000042.0
AXES = ("zh", "zl", "y", "x", "c")
TEAM = ("zl", "y")
SLOTS = ("y", "zl")
PAIRED_SLOTS = ("c", "y", "zl")
SHARES = ("c", "x", "zh")
OWNERS = ("zl", "y", "c")
ROWS_T = (((0,), (0,)), ((), ()))
PAIR_ROWS_T = (((0, 1), (0, 1)), ((), ()))
COLS_T = (((1,), (1,)), ((), ()))
F32 = jnp.float32
BF16 = jnp.bfloat16


def offsets(sizes, axes):
    return [dict(zip(axes, o)) for o in itertools.product(*(range(sizes[a]) for a in axes))]


def place(at, layout, sizes):
    index = 0
    for a in layout:
        index = index * sizes[a] + at[a]
    return index


class Gather:
    def __init__(self, x, layout, orders, rank=1):
        self.x, self.layout, self.orders, self.rank = x, layout, orders, rank

    def shape(self, sizes):
        return (math.prod(sizes[a] for a in self.layout),) + self.x.shape

    def cut(self, ref, part):
        rows = self.x.shape[0] // len(self.orders)
        return ref.at[pl.ds(part * rows, rows)]

    def spot(self, out, owner, off, part, sizes):
        return self.cut(out.at[place(owner, self.layout, sizes)], part)


class NearGather(Gather):
    def shape(self, sizes):
        return tuple(sizes[a] for a in self.layout) + self.x.shape

    def spot(self, out, owner, off, part, sizes):
        return self.cut(out.at[tuple(off[a] for a in self.layout)], part)


class RowGather(Gather):
    def shape(self, sizes):
        team, rows, columns = self.x.shape
        return (sizes["x"] * sizes["zh"] * team * sizes["c"] * rows, columns)

    def cut(self, ref, part):
        return ref.at[part]

    def spot(self, out, owner, off, part, sizes):
        team, rows, _ = self.x.shape
        block = place(owner, ("x", "zh"), sizes) * team + part
        start = pl.multiple_of((block * sizes["c"] + owner["c"]) * rows, rows)
        return out.at[pl.ds(start, rows)]


class Swap:
    def __init__(self, x, layout):
        self.x, self.layout = x, layout

    def shape(self, sizes):
        return self.x.shape

    def own_shape(self):
        return self.x.shape[1:]

    def offsets(self, sizes):
        return offsets(sizes, self.layout)

    def pair(self, x, out, here, to, off, sizes):
        return x.at[place(to, self.layout, sizes)], out.at[place(here, self.layout, sizes)]


class NearSwap(Swap):
    def pair(self, x, out, here, to, off, sizes):
        i = off[self.layout[0]]
        return x.at[i], out.at[i]


class Halves:
    def __init__(self, x):
        self.x = x

    def shape(self, sizes):
        rows, columns = self.x.shape
        return (2, rows, columns // 2)

    def own_shape(self):
        rows, columns = self.x.shape
        return (rows, columns // 2)

    def offsets(self, sizes):
        return offsets(sizes, ("c",))

    def pair(self, x, out, here, to, off, sizes):
        width = self.x.shape[1] // 2
        start = pl.multiple_of(to["c"] * width, width)
        return x.at[:, pl.ds(start, width)], out.at[off["c"]]


CHUNKS = 4


class TeamSum:
    def __init__(self, x, y_first=2):
        self.x, self.y_first = x, y_first

    def shape(self, sizes):
        return (2,) + self.x.shape[2:]


class Net:
    def __init__(self, sizes):
        self.sizes, self.count, self.reached = sizes, 0, set()

    def wire(self, off):
        self.reached.add(tuple(off.get(a, 0) for a in AXES))
        self.count += 1
        return self.count - 1, off

    def open(self, send_sem, recv_sem):
        self.send_sem, self.recv_sem = send_sem, recv_sem
        self.here = {a: lax.axis_index(a) for a in AXES}
        self.sent = []
        barrier = pltpu.get_barrier_semaphore()
        for off in sorted(self.reached):
            pl.semaphore_signal(
                barrier,
                inc=1,
                device_id=self.device(self.moved(dict(zip(AXES, off)))),
                device_id_type=pl.DeviceIdType.MESH,
            )
        pl.semaphore_wait(barrier, len(self.reached))

    def moved(self, off):
        return {
            a: lax.rem(self.here[a] + off[a], self.sizes[a]) if off.get(a, 0) else self.here[a]
            for a in AXES
        }

    def device(self, at):
        return tuple(at[a] for a in AXES)

    def send(self, src, dst, wire):
        sem, off = wire
        cp = pltpu.make_async_remote_copy(
            src_ref=src,
            dst_ref=dst,
            send_sem=self.send_sem.at[sem],
            recv_sem=self.recv_sem.at[sem],
            device_id=self.device(self.moved(off)),
            device_id_type=pl.DeviceIdType.MESH,
        )
        cp.start()
        self.sent.append(cp)
        return cp

    def settle(self, cp):
        cp.wait_send()
        self.sent = [other for other in self.sent if other is not cp]

    def close(self):
        for cp in self.sent:
            cp.wait_send()


class Relay:
    def __init__(self, job, number, net):
        self.job, self.net, self.sizes = job, net, net.sizes
        self.steps = []
        for part, order in enumerate(job.orders):
            for off in offsets(self.sizes, order):
                used = [i for i, a in enumerate(order) if off[a]]
                sends = [
                    net.wire({a: d})
                    for a in order[used[-1] + 1 if used else 0 :]
                    for d in range(1, self.sizes[a])
                ]
                hops = len(used)
                key = (job.rank, part + 2 * hops, hops, number, part)
                self.steps.append((key, self, hops, part, off, sends))

    def open(self, x, out):
        self.x, self.out, self.arrivals = x, out, {}

    def run(self, hops, part, off, sends):
        job, net = self.job, self.net
        owner = net.moved(off)
        if hops:
            self.arrivals[part, tuple(sorted(off.items()))].wait_recv()
            source = job.spot(self.out, owner, off, part, self.sizes)
        else:
            source = job.cut(self.x, part)
        for wire in sends:
            ((a, d),) = wire[1].items()
            there = dict(off)
            there[a] = (-d) % self.sizes[a]
            dst = job.spot(self.out, owner, there, part, self.sizes)
            self.arrivals[part, tuple(sorted(there.items()))] = net.send(source, dst, wire)

    def own(self, part):
        return self.job.spot(self.out, self.net.here, {a: 0 for a in AXES}, part, self.sizes)


class Adder:
    def __init__(self, job, number, net):
        self.job, self.net = job, net
        rows = job.x.shape[2] // CHUNKS
        self.steps = []
        self.parts = []
        for part in range(CHUNKS):
            first, second = ("y", "zl") if part < job.y_first else ("zl", "y")
            wires = net.wire({first: 1}), net.wire({first: 1}), net.wire({second: 1})
            self.parts.append((pl.ds(part * rows, rows), first, second, wires))
            self.steps.append(((0, part, 0, number, part), self, 0, part, None, None))
            self.steps.append(((1, part + 2, 1, number, part), self, 1, part, None, None))

    def scratch(self):
        shape = self.job.x.shape[2:]
        return [pltpu.VMEM(shape, self.job.x.dtype)] * 2 + [pltpu.SemaphoreType.DMA((CHUNKS,))]

    def open(self, x, out, term, far, sem):
        self.x, self.out, self.term, self.far, self.sem = x, out, term, far, sem
        self.waits, self.direct, self.summed = {}, [], []

    def run(self, hops, part, *_):
        window, first, second, wires = self.parts[part]
        y_first = first == "y"
        if not hops:
            self.waits[part] = self.net.send(
                self.x.at[1, 1, window], self.far.at[window], wires[0]
            )
            near = self.x.at[1, 0, window] if y_first else self.x.at[0, 1, window]
            self.direct.append(
                self.net.send(near, self.out.at[0 if y_first else 1, window], wires[1])
            )
            mine = self.x.at[0, 1, window] if y_first else self.x.at[1, 0, window]
            load = pltpu.make_async_copy(mine, self.term.at[window], self.sem.at[part])
            load.start()
            self.waits[part] = self.waits[part], load
            return
        far, load = self.waits[part]
        load.wait()
        far.wait_recv()
        total = self.term[window].astype(F32) + self.far[window].astype(F32)
        self.term[window] = total.astype(self.term.dtype)
        self.summed.append(
            self.net.send(
                self.term.at[window], self.out.at[1 if y_first else 0, window], wires[2]
            )
        )

    def finish(self):
        for cp in self.direct + self.summed:
            cp.wait_recv()


def exchange(jobs, collective_id, micros=50):
    net = Net({a: lax.axis_size(a) for a in AXES})
    sizes = net.sizes
    count = len(jobs)
    steps, swaps, runners, scratch = [], [], [], []
    for number, job in enumerate(jobs):
        if isinstance(job, Gather):
            runner = Relay(job, number, net)
            steps += runner.steps
            stage = [pltpu.VMEM(job.x.shape, job.x.dtype)]
        elif isinstance(job, TeamSum):
            runner = Adder(job, number, net)
            steps += runner.steps
            stage = runner.scratch()
        else:
            runner = None
            swaps += [(number, off, net.wire(off)) for off in job.offsets(sizes) if any(off.values())]
            stage = [pltpu.VMEM(job.own_shape(), job.x.dtype)]
        runners.append((runner, len(scratch), len(scratch) + len(stage)))
        scratch += stage
    steps.sort(key=lambda s: s[0])

    def kernel(*refs):
        ins, outs, rest = refs[:count], refs[count : 2 * count], refs[2 * count :]
        send_sem, recv_sem, local_sem = rest[-3:]
        net.open(send_sem, recv_sem)
        loads, stores = [], []
        for number, job in enumerate(jobs):
            runner, lo, hi = runners[number]
            if isinstance(job, TeamSum):
                runner.open(ins[number], outs[number], *rest[lo:hi])
                continue
            (stage,) = rest[lo:hi]
            if runner:
                runner.open(ins[number], outs[number])
                src = ins[number]
                puts = [
                    (job.cut(stage, part), runner.own(part)) for part in range(len(job.orders))
                ]
            else:
                none = {a: 0 for a in AXES}
                src, dst = job.pair(ins[number], outs[number], net.here, net.here, none, sizes)
                puts = [(stage, dst)]
            load = pltpu.make_async_copy(src, stage, local_sem.at[number, 0])
            load.start()
            loads.append((load, number, puts))
        for _, runner, hops, *what in steps:
            if not hops:
                runner.run(hops, *what)
        received = []
        for number, off, wire in swaps:
            to = net.moved(off)
            src, dst = jobs[number].pair(ins[number], outs[number], net.here, to, off, sizes)
            received.append(net.send(src, dst, wire))
        for load, number, puts in loads:
            load.wait()
            for i, (src, dst) in enumerate(puts):
                store = pltpu.make_async_copy(src, dst, local_sem.at[number, 1 + i])
                store.start()
                stores.append(store)
        for _, runner, hops, *what in steps:
            if hops:
                runner.run(hops, *what)
        for cp in received:
            cp.wait_recv()
        for runner, _, _ in runners:
            if isinstance(runner, Adder):
                runner.finish()
        net.close()
        for store in stores:
            store.wait()

    return pl.pallas_call(
        kernel,
        out_shape=[jax.ShapeDtypeStruct(job.shape(sizes), job.x.dtype) for job in jobs],
        in_specs=[pl.BlockSpec(memory_space=pl.ANY)] * count,
        out_specs=[pl.BlockSpec(memory_space=pl.ANY)] * count,
        scratch_shapes=scratch
        + [
            pltpu.SemaphoreType.DMA((net.count,)),
            pltpu.SemaphoreType.DMA((net.count,)),
            pltpu.SemaphoreType.DMA((count, 1 + CHUNKS)),
        ],
        cost_estimate=pl.CostEstimate(
            flops=0, bytes_accessed=micros * 3_000_000, transcendentals=0
        ),
        compiler_params=pltpu.CompilerParams(
            collective_id=collective_id, has_side_effects=True, vmem_limit_bytes=VMEM_LIMIT
        ),
    )(*[job.x for job in jobs])


def sum_over(term, axis):
    size = lax.axis_size(axis)
    me = lax.axis_index(axis)
    while size > 1:
        size //= 2
        rows = term.shape[0] // 2
        pairs = [(i, i ^ size) for i in range(lax.axis_size(axis))]
        side = (me // size) % 2
        kept = lax.dynamic_slice_in_dim(term, side * rows, rows)
        other = lax.ppermute(
            lax.dynamic_slice_in_dim(term, (1 - side) * rows, rows), axis, pairs
        )
        term = kept.astype(F32) + other.astype(F32)
        if size > 1:
            term = term.astype(BF16)
    return term


def dot(a, b, dims=None):
    if dims is None:
        return jnp.dot(a, b, preferred_element_type=F32)
    return lax.dot_general(a, b, dims, preferred_element_type=F32)


def rotate(t, cos, sin):
    half = t.shape[-1] // 2
    front, back = t[..., :half], t[..., half:]
    return jnp.concatenate([front * cos - back * sin, back * cos + front * sin], axis=-1)


def rms_scale(values):
    return lax.rsqrt(jnp.mean(values * values, axis=-1, keepdims=True) + EPS)


def positions(members):
    total = lax.axis_size("zh") * lax.axis_size("zl")
    half = jnp.arange(2)[None, :, None]
    row = jnp.arange(BLK)[None, None, :]
    j = members[:, None, None]
    return (jnp.where(half == 0, j, 2 * total - 1 - j) * BLK + row).reshape(-1)


OUTWARD = ("zh", "x", "c")
TILE = 512
TO_TEAM = [("zl", "y", "c")] * CHUNKS
TO_TEAM_EVEN = [("zl", "y", "c"), ("y", "zl", "c")] * (CHUNKS // 2)


def feed_forward(norm, gd, w_gate, w_down, up_part, collective_id):
    net = Net({a: lax.axis_size(a) for a in AXES})
    sizes = net.sizes
    own, width = norm.shape
    ff = w_gate.shape[1]
    half = ff // 2
    norm_job = NearGather(norm, PAIRED_SLOTS, TO_TEAM_EVEN)
    up_job = RowGather(up_part, None, [OUTWARD] * up_part.shape[0])
    norms, ups = Relay(norm_job, 0, net), Relay(up_job, 1, net)
    steps = sorted(norms.steps + ups.steps, key=lambda s: s[0])
    y_rows, zl_rows = pl.ds(0, own // 2), pl.ds(own // 2, own // 2)
    far_wires = net.wire({"y": 1}), net.wire({"zl": 1})
    near_wires = net.wire({"y": 1}), net.wire({"zl": 1})
    half_wires = [[net.wire({"c": 1}) for _ in range(3)] for _ in range(4)]
    n_local = 64

    def kernel(
        norm_ref, gd_ref, w_gate_ref, w_down_ref, up_ref,
        norms_ref, gate_half, up_half, mixed_half, gn2_ref, out_ref,
        wg, wu, wd, nv, gdv, gate, gm, gg, gu, mx, far, send_sem, recv_sem, local_sem,
    ):
        net.open(send_sem, recv_sem)
        norms.open(norm_ref, norms_ref)
        ups.open(up_ref, wu)
        used = iter(range(n_local))

        def local(src, dst):
            cp = pltpu.make_async_copy(src, dst, local_sem.at[next(used)])
            cp.start()
            return cp

        got_norm = local(norm_ref, nv.at[0])
        for _, runner, hops, *what in steps:
            if not hops:
                runner.run(hops, *what)
        got_gate = local(w_gate_ref, wg)
        got_gd = [local(gd_ref.at[0, 0, 0], gdv.at[0]), local(gd_ref.at[0, 1, 0], gdv.at[1])]
        got_down = local(w_down_ref, wd)
        got_up = [local(ups.job.cut(up_ref, p), ups.own(p)) for p in range(len(up_job.orders))]
        got_norm.wait()
        kept_norm = [local(norm_job.cut(nv.at[0], p), norms.own(p)) for p in range(CHUNKS)]

        def tiles(n, body):
            def step(t, _):
                body(pl.ds(pl.multiple_of(t * TILE, TILE), TILE))
                return 0

            lax.fori_loop(0, n // TILE, step, 0)

        gd_turn = [(0, 0), (1, 0), (0, 1), (1, 1)]

        def begin(turn):
            i, j = gd_turn[turn]
            r = 2 * i + j

            def one(t):
                gate[r, :, t] = dot(nv[r], wg[:, t])

            tiles(ff, one)
            got_gd[turn].wait()

            def two(t):
                gm[r, :, t] = dot(gdv[turn % 2], wd[t, :], COLS_T)

            tiles(ff, two)
            if turn + 2 < 4:
                got_gd.append(local(gd_ref.at[(0, *gd_turn[turn + 2])], gdv.at[turn % 2]))

        got_gate.wait()
        got_down.wait()
        begin(0)
        late = []
        arrived = {(1, 0): 0, (0, 1): 0, (1, 1): 0}
        turn = 1
        for _, runner, hops, part, off, sends in steps:
            if not hops:
                continue
            if runner is norms and off["c"]:
                late.append((hops, part, off, sends))
                continue
            runner.run(hops, part, off, sends)
            if runner is norms:
                arrived[off["y"], off["zl"]] += 1
                while turn < 4 and arrived[gd_turn[turn]] == CHUNKS:
                    i, j = gd_turn[turn]
                    local(norms_ref.at[0, i, j], nv.at[2 * i + j]).wait()
                    begin(turn)
                    turn += 1
        for cp in got_up + kept_norm:
            cp.wait()

        halves, busy = [], {}

        def finish(r, buf):
            for cp, remote in busy.pop(buf, []):
                net.settle(cp) if remote else cp.wait()

            def one(t):
                up = dot(nv[r], wu[:, t])
                g, m = gate[r, :, t], gm[r, :, t]
                s = 1.0 / (1.0 + jnp.exp(-g))
                gs = g * s
                mx[r, :, t] = (gs * up).astype(BF16)
                gg[buf, :, t] = (m * up * s * (1.0 + g * (1.0 - s))).astype(BF16)
                gu[buf, :, t] = (m * gs).astype(BF16)

            tiles(ff, one)
            mine = pl.ds(pl.multiple_of(net.here["c"] * half, half), half)
            other = pl.ds(pl.multiple_of((1 - net.here["c"]) * half, half), half)
            rows = pl.ds(r * own, own)
            for n, (ref, out) in enumerate(
                ((gg.at[buf], gate_half), (gu.at[buf], up_half), (mx.at[r], mixed_half))
            ):
                cp = local(ref.at[:, mine], out.at[0, rows])
                sent = net.send(ref.at[:, other], out.at[1, rows], half_wires[r][n])
                halves.append(sent)
                busy.setdefault(buf if n < 2 else "mixed", []).extend([(cp, False), (sent, True)])

            def two(t):
                term = dot(gg[buf], wg[t, :], COLS_T) + dot(gu[buf], wu[t, :], COLS_T)
                nv[r, :, t] = term.astype(BF16)

            tiles(width, two)

        def add(r, window):
            nv[r, window] = (nv[r, window].astype(F32) + far[window].astype(F32)).astype(BF16)

        finish(3, 0)
        to_far = (
            net.send(nv.at[3, y_rows], far.at[y_rows], far_wires[0]),
            net.send(nv.at[3, zl_rows], far.at[zl_rows], far_wires[1]),
        )
        finish(2, 1)
        to_far[1].wait_recv()
        add(2, zl_rows)
        to_y = net.send(nv.at[2], gn2_ref.at[1], near_wires[0])
        finish(1, 0)
        to_far[0].wait_recv()
        add(1, y_rows)
        to_zl = net.send(nv.at[1], gn2_ref.at[2], near_wires[1])
        finish(0, 1)
        stored = [local(nv.at[0], gn2_ref.at[0])]
        for n, r in enumerate((3, 2, 1, 0)):
            buf = n % 2
            for cp, remote in busy.pop(buf, []):
                net.settle(cp) if remote else cp.wait()

            def down(t):
                gg[buf, :, t] = dot(mx[r], wd[:, t]).astype(BF16)

            tiles(width, down)
            busy[buf] = [(local(gg.at[buf], out_ref.at[r // 2, r % 2]), False)]
        for hops, part, off, sends in late:
            norms.run(hops, part, off, sends)
        to_y.wait_recv()
        to_zl.wait_recv()
        for cp in halves:
            cp.wait_recv()
        net.close()
        for cps in busy.values():
            for cp, remote in cps:
                if not remote:
                    cp.wait()
        for cp in stored:
            cp.wait()

    shape = jax.ShapeDtypeStruct
    weight = pltpu.VMEM((width, ff), BF16)
    return pl.pallas_call(
        kernel,
        out_shape=[
            shape((2, 2, 2, own, width), BF16),
            *[shape((2, 4 * own, half), BF16)] * 3,
            shape((3, own, width), BF16),
            shape((2, 2, own, width), BF16),
        ],
        in_specs=[pl.BlockSpec(memory_space=pl.ANY)] * 5,
        out_specs=[pl.BlockSpec(memory_space=pl.ANY)] * 6,
        scratch_shapes=[
            weight,
            weight,
            pltpu.VMEM((ff, width), BF16),
            pltpu.VMEM((4, own, width), BF16),
            pltpu.VMEM((2, own, width), BF16),
            pltpu.VMEM((4, own, ff), F32),
            pltpu.VMEM((4, own, ff), F32),
            pltpu.VMEM((2, own, ff), BF16),
            pltpu.VMEM((2, own, ff), BF16),
            pltpu.VMEM((4, own, ff), BF16),
            pltpu.VMEM((own, width), BF16),
            pltpu.SemaphoreType.DMA((net.count,)),
            pltpu.SemaphoreType.DMA((net.count,)),
            pltpu.SemaphoreType.DMA((n_local,)),
        ],
        cost_estimate=pl.CostEstimate(
            flops=0, bytes_accessed=130 * 3_000_000, transcendentals=0
        ),
        compiler_params=pltpu.CompilerParams(
            collective_id=collective_id, has_side_effects=True, vmem_limit_bytes=FFN_VMEM_LIMIT
        ),
    )(norm, gd, w_gate, w_down, up_part)


def on_device(
    inputs,
    lengths,
    attn_gain,
    query_weight,
    key_matrix,
    value_matrix,
    output_weight,
    ffn_gain,
    gate_weight,
    up_weight,
    down_weight,
    cotangent,
):
    size = {a: lax.axis_size(a) for a in AXES}
    at = {a: lax.axis_index(a) for a in AXES}
    width = inputs.shape[3]
    own = inputs.shape[1] * inputs.shape[2]
    rows = query_weight.shape[0]
    n_dev = width // rows
    team = size["y"] * size["zl"]
    q_cols = query_weight.shape[1] // team
    kv_cols = key_matrix.shape[1] // team
    ff_rows = down_weight.shape[0]
    ff = gate_weight.shape[1] // team
    heads = q_cols // HEAD
    n_tok = team * own
    scaling = HEAD**-0.5

    def by_team(w):
        return w.reshape(rows, team, -1).transpose(1, 0, 2)

    def ff_by_team(w):
        cut = w.reshape(rows, *(size[a] for a in AXES), ff_rows)
        return cut.transpose(2, 3, 0, 5, 4, 1, 6).reshape(team, rows, ff)

    attn_cut = jnp.concatenate(
        [by_team(query_weight), by_team(key_matrix), by_team(value_matrix)], axis=2
    )
    tile = jnp.zeros((8, 128), F32)
    tile = tile.at[0, :rows].set(attn_gain.astype(F32))
    tile = tile.at[0, 64 : 64 + rows].set(ffn_gain.astype(F32))
    tile = tile.at[1].set(lengths[0].astype(F32))
    tiles, attn_part, gate_part, up_part = exchange(
        [
            Gather(tile, AXES, [("c", "x", "y", "zl", "zh")], rank=0),
            Swap(attn_cut, TEAM),
            Swap(ff_by_team(gate_weight), TEAM),
            Swap(ff_by_team(up_weight), TEAM),
        ],
        1,
    )
    w_down = lax.all_gather(down_weight, SHARES, axis=0, tiled=True)
    gain_one = tiles[:, 0, :rows].reshape(1, width)
    gain_two = tiles[:, 0, 64 : 64 + rows].reshape(1, width)
    slots = tiles[: n_dev // (size["zh"] * size["zl"]), 1, 0].reshape(
        size["y"], size["x"], size["c"]
    )
    lens = slots[at["y"] ^ jnp.arange(2), at["x"], at["c"]].astype(jnp.int32)

    per_head = n_dev // team

    def head_home(i):
        f, t = i // per_head, i % per_head
        zl, y = f // size["y"], f % size["y"]
        zh, t = t % size["zh"], t // size["zh"]
        x, c = t % size["x"], t // size["x"]
        return (((zh * size["zl"] + zl) * size["y"] + y) * size["x"] + x) * size["c"] + c

    homes = [(i, head_home(i)) for i in range(n_dev)]
    out_part = lax.ppermute(output_weight, AXES, homes)

    def row_gather(part):
        return RowGather(part, None, [OUTWARD] * team)

    def spread(v):
        cut = v.reshape(own, size["zh"], size["zl"], size["y"], size["x"], size["c"] * rows)
        return cut.transpose(0, 4, 1, 2, 3, 5).reshape(own, width)

    def natural(v):
        cut = v.reshape(own, size["x"], size["zh"], size["zl"], size["y"], size["c"] * rows)
        return cut.transpose(0, 2, 3, 4, 1, 5).reshape(own, width)

    my_pos = positions((at["zh"] * size["zl"] + at["zl"])[None])
    valid = (my_pos < lengths[0]).astype(F32)[:, None]
    near_zl = at["zl"] ^ jnp.arange(2)
    near_zh = (at["zh"] + jnp.arange(size["zh"])) % size["zh"]
    q_pos = positions(at["zh"] * 2 + near_zl)
    k_pos = positions((near_zh[:, None] * 2 + near_zl[None, :]).reshape(-1))
    half = HEAD // 2
    freq = ROPE_BASE ** (-2.0 * jnp.arange(half).astype(F32) / HEAD)
    angles = q_pos.astype(F32)[:, None] * freq[None, :]
    cos = jnp.tile(jnp.cos(angles), (size["y"], 1))[:, None, :]
    sin = jnp.tile(jnp.sin(angles), (size["y"], 1))[:, None, :]

    tokens = inputs.reshape(own, width).astype(F32)
    scale_one = rms_scale(tokens)
    norm_one = (tokens * scale_one * gain_one).astype(BF16)
    norm_one_pair, w_attn, w_out = exchange(
        [
            NearGather(spread(norm_one), PAIRED_SLOTS, TO_TEAM),
            row_gather(attn_part),
            Gather(out_part, SHARES, [OUTWARD] * (rows // 16)),
        ],
        2,
    )
    norm_one_pair = norm_one_pair.reshape(2, n_tok, width)
    w_attn = w_attn.reshape(width, -1)
    w_out = w_out.reshape(q_cols, width)
    qkv = dot(norm_one_pair[0], w_attn)
    q = rotate(qkv[:, :q_cols].reshape(n_tok, heads, HEAD), cos, sin).astype(BF16)
    k = rotate(qkv[:, q_cols : q_cols + kv_cols].reshape(n_tok, 1, HEAD), cos, sin).astype(BF16)
    v = qkv[:, q_cols + kv_cols :].astype(BF16)
    kv = jnp.concatenate([k.reshape(n_tok, kv_cols), v], axis=1)
    gy = valid * cotangent.reshape(own, width).astype(F32)
    kv_all, gd_pair = exchange(
        [
            NearGather(kv, ("zh",), [("zh",)]),
            NearGather(gy.astype(BF16), PAIRED_SLOTS, TO_TEAM_EVEN),
        ],
        3,
    )
    n_slot = size["y"]
    n_q = n_tok // n_slot
    q = q.reshape(n_slot, n_q, heads, HEAD)
    kv_all = kv_all.reshape(size["zh"], n_slot, n_q, 2 * kv_cols).transpose(1, 0, 2, 3)
    kv_all = kv_all.reshape(n_slot, size["zh"] * n_q, 2 * kv_cols)
    k_all, v_all = kv_all[:, :, :kv_cols], kv_all[:, :, kv_cols:]
    allowed = (k_pos[None, None, :] <= q_pos[None, :, None]) & (
        k_pos[None, None, :] < lens[:, None, None]
    )
    scores = jnp.einsum("bqgd,bkd->bgqk", q, k_all, preferred_element_type=F32) * scaling
    scores = jnp.where(allowed[:, None], scores, -jnp.inf)
    peak = jnp.max(scores, axis=-1, keepdims=True)
    exps = jnp.exp(scores - peak)
    prob = exps / jnp.sum(exps, axis=-1, keepdims=True)
    prob_b = prob.astype(BF16)
    o = jnp.einsum("bgqk,bkd->bqgd", prob_b, v_all, preferred_element_type=F32)
    o = o.reshape(n_tok, q_cols).astype(BF16)

    o_parts = dot(o, w_out).astype(BF16).reshape(2, 2, own, width)
    o_added, w_gate, o_half = exchange(
        [TeamSum(o_parts, 4), row_gather(gate_part), Halves(o)], 4, micros=70
    )

    def added(term, others):
        return term.astype(F32) + others[0].astype(F32) + others[1].astype(F32)

    h1 = tokens + added(o_parts[0, 0], o_added)
    scale_two = rms_scale(h1)
    norm_two = (h1 * scale_two * gain_two).astype(BF16)
    norm_two_pair, gate_half, up_half, mixed_half, gn2_terms, out_parts = feed_forward(
        spread(norm_two), gd_pair, w_gate, w_down, up_part, 5
    )
    norm_two_pair = norm_two_pair.reshape(2, n_tok, width)
    gd_pair = gd_pair.reshape(2, n_tok, width)
    gn2 = natural(added(gn2_terms[0], gn2_terms[1:])) * gain_two
    gh1 = gy + scale_two * gn2 - h1 * scale_two**3 * jnp.mean(h1 * gn2, axis=-1, keepdims=True)

    tie = lax.optimization_barrier
    down_term = dot(mixed_half, gd_pair, PAIR_ROWS_T).astype(BF16)
    gate_term = dot(norm_two_pair, gate_half, PAIR_ROWS_T).astype(BF16)
    up_term = dot(norm_two_pair, up_half, PAIR_ROWS_T).astype(BF16)
    ga, down_term, gate_term, up_term = tie((gh1.astype(BF16), down_term, gate_term, up_term))
    down_x = sum_over(down_term, "x").astype(BF16)
    (ga_pair,) = exchange([NearGather(ga, PAIRED_SLOTS, TO_TEAM_EVEN)], 8)
    ga_pair, down_x, gate_term = tie((ga_pair, down_x, gate_term))
    gate_x = sum_over(gate_term, "x").astype(BF16)
    down_grad = sum_over(down_x, "zh")
    ga_pair = ga_pair.reshape(2, n_tok, width)

    go = dot(ga_pair[0], w_out, COLS_T).astype(BF16).reshape(n_slot, n_q, heads, HEAD)
    gp = jnp.einsum("bqgd,bkd->bgqk", go, v_all, preferred_element_type=F32)
    delta = jnp.sum(prob * gp, axis=-1, keepdims=True)
    gs = (prob * (gp - delta)).astype(BF16)
    gq_rot = jnp.einsum("bgqk,bkd->bqgd", gs, k_all, preferred_element_type=F32) * scaling
    gk_rot = jnp.einsum("bgqk,bqgd->bkd", gs, q, preferred_element_type=F32) * scaling
    gv_sum = jnp.einsum("bgqk,bqgd->bkd", prob_b, go, preferred_element_type=F32)
    gkv = jnp.concatenate([gk_rot, gv_sum], axis=-1).astype(BF16)
    gkv = gkv.reshape(n_slot, size["zh"], n_q, 2 * kv_cols).transpose(1, 0, 2, 3)
    gkv = gkv.reshape(size["zh"], n_tok, 2 * kv_cols)
    out_term = dot(o_half, ga_pair, PAIR_ROWS_T).astype(BF16)
    gkv, gate_x, down_grad, up_term, out_term = tie(
        (gkv, gate_x, down_grad, up_term, out_term)
    )
    up_x = sum_over(up_term, "x").astype(BF16)
    out_x = sum_over(out_term, "x").astype(BF16)
    gate_sum = sum_over(gate_x, "zh").astype(BF16)
    gkv_parts, out_added = exchange([NearSwap(gkv, ("zh",)), TeamSum(out_parts, 4)], 9)
    gkv_parts, up_x, out_x, gate_sum = tie((gkv_parts, up_x, out_x, gate_sum))
    gkv = sum(gkv_parts[i].astype(F32) for i in range(size["zh"]))
    gq = rotate(gq_rot.reshape(n_tok, heads, HEAD), cos, -sin).astype(BF16)
    gk = rotate(gkv[:, :kv_cols].reshape(n_tok, 1, HEAD), cos, -sin).astype(BF16)
    g_qkv = jnp.concatenate(
        [gq.reshape(n_tok, q_cols), gk.reshape(n_tok, kv_cols), gkv[:, kv_cols:].astype(BF16)],
        axis=1,
    )
    cols = g_qkv.shape[1] // 2
    mine = lax.dynamic_slice_in_dim(g_qkv, at["c"] * cols, cols, axis=1)
    other = lax.dynamic_slice_in_dim(g_qkv, (1 - at["c"]) * cols, cols, axis=1)
    g_qkv_half = jnp.stack([mine, lax.ppermute(other, "c", [(0, 1), (1, 0)])])
    attn_term = dot(norm_one_pair, g_qkv_half, PAIR_ROWS_T).astype(BF16)
    gn1_parts = dot(g_qkv, w_attn, COLS_T).astype(BF16).reshape(2, 2, own, width)
    gn1_parts, attn_term, up_x, out_x = tie((gn1_parts, attn_term, up_x, out_x))
    attn_x = sum_over(attn_term, "x").astype(BF16)
    up_sum = sum_over(up_x, "zh").astype(BF16)
    out_sum = sum_over(out_x, "zh").astype(BF16)
    (gn1_added,) = exchange([TeamSum(gn1_parts, 4)], 10)
    gn1_added, attn_x, up_sum, out_sum = tie((gn1_added, attn_x, up_sum, out_sum))
    attn_sum = sum_over(attn_x, "zh")
    out_sum = lax.ppermute(out_sum, AXES, [(b, a) for a, b in homes])
    outputs = valid * (h1 + added(out_parts[0, 0], out_added))
    outputs = outputs.astype(BF16).reshape(inputs.shape)
    n_owners = math.prod(size[a] for a in OWNERS)

    def by_owner(total):
        return total.astype(BF16).reshape(n_owners, rows, -1)

    gate_sum, up_sum = exchange([Swap(by_owner(t), OWNERS) for t in (gate_sum, up_sum)], 11)
    attn_sum, gate_sum, up_sum = tie((attn_sum, gate_sum, up_sum))
    (attn_sum,) = exchange([Swap(by_owner(attn_sum), OWNERS)], 12)
    gn1 = natural(added(gn1_parts[0, 0], gn1_added)) * gain_one
    g_tokens = (
        gh1
        + scale_one * gn1
        - tokens * scale_one**3 * jnp.mean(tokens * gn1, axis=-1, keepdims=True)
    )
    input_grad = g_tokens.astype(BF16).reshape(inputs.shape)

    def ff_natural(total):
        cut = total.reshape(
            size["zl"], size["y"], size["c"], rows, size["x"], size["zh"], ff_rows
        )
        return cut.transpose(3, 5, 0, 1, 4, 2, 6).reshape(rows, -1).astype(F32)

    def side(part):
        return part.transpose(1, 0, 2).reshape(rows, -1).astype(F32)

    attn_sum = attn_sum.reshape(team, 2, rows, -1)
    query_grad = side(attn_sum[:, 0])
    key_grad = side(attn_sum[:, 1, :, :kv_cols])
    value_grad = side(attn_sum[:, 1, :, kv_cols:])
    gate_grad = ff_natural(gate_sum)
    up_grad = ff_natural(up_sum)

    def against(w, g):
        return jnp.sum(w.astype(F32) * g, axis=1)

    attn_gain_grad = (
        against(query_weight, query_grad)
        + against(key_matrix, key_grad)
        + against(value_matrix, value_grad)
    ) / attn_gain.astype(F32)
    ffn_gain_grad = (against(gate_weight, gate_grad) + against(up_weight, up_grad)) / (
        ffn_gain.astype(F32)
    )
    return (
        outputs,
        input_grad,
        attn_gain_grad,
        query_grad,
        key_grad,
        value_grad,
        out_sum.astype(F32),
        ffn_gain_grad,
        gate_grad,
        up_grad,
        down_grad,
    )


def solution(mesh):
    ctx, fsdp = mesh.shape["ctx"], mesh.shape["fsdp"]
    grid = Mesh(mesh.devices.reshape(ctx // 2, 2, 2, fsdp // 4, 2), AXES)
    act = P(("y", "x", "c"), None, ("zh", "zl"), None)
    row = P(AXES)
    return jax.shard_map(
        on_device,
        mesh=grid,
        in_specs=(act, P(("y", "x", "c"))) + (row,) * 9 + (act,),
        out_specs=(act, act) + (row,) * 9,
        check_vma=False,
    )
```

```python
import itertools
import math

import jax
import jax.numpy as jnp
from jax import lax
from jax.experimental import pallas as pl
from jax.experimental.pallas import tpu as pltpu
from jax.sharding import Mesh
from jax.sharding import PartitionSpec as P

HEAD = 256
VMEM_LIMIT = 48 << 20
FFN_VMEM_LIMIT = 62 << 20
BLK = 128
EPS = 1e-06
ROPE_BASE = 1000042.0
AXES = ("zh", "zl", "y", "x", "c")
TEAM = ("zl", "y")
SLOTS = ("y", "zl")
PAIRED_SLOTS = ("c", "y", "zl")
SHARES = ("c", "x", "zh")
OWNERS = ("zl", "y", "c")
ROWS_T = (((0,), (0,)), ((), ()))
PAIR_ROWS_T = (((0, 1), (0, 1)), ((), ()))
COLS_T = (((1,), (1,)), ((), ()))
F32 = jnp.float32
BF16 = jnp.bfloat16


def offsets(sizes, axes):
    return [dict(zip(axes, o)) for o in itertools.product(*(range(sizes[a]) for a in axes))]


def place(at, layout, sizes):
    index = 0
    for a in layout:
        index = index * sizes[a] + at[a]
    return index


class Gather:
    def __init__(self, x, layout, orders, rank=1):
        self.x, self.layout, self.orders, self.rank = x, layout, orders, rank

    def shape(self, sizes):
        return (math.prod(sizes[a] for a in self.layout),) + self.x.shape

    def cut(self, ref, part):
        rows = self.x.shape[0] // len(self.orders)
        return ref.at[pl.ds(part * rows, rows)]

    def spot(self, out, owner, off, part, sizes):
        return self.cut(out.at[place(owner, self.layout, sizes)], part)


class NearGather(Gather):
    def shape(self, sizes):
        return tuple(sizes[a] for a in self.layout) + self.x.shape

    def spot(self, out, owner, off, part, sizes):
        return self.cut(out.at[tuple(off[a] for a in self.layout)], part)


class RowGather(Gather):
    def shape(self, sizes):
        team, rows, columns = self.x.shape
        return (sizes["x"] * sizes["zh"] * team * sizes["c"] * rows, columns)

    def cut(self, ref, part):
        return ref.at[part]

    def spot(self, out, owner, off, part, sizes):
        team, rows, _ = self.x.shape
        block = (owner["zh"] * team + part) * sizes["x"] + owner["x"]
        start = pl.multiple_of((block * sizes["c"] + owner["c"]) * rows, rows)
        return out.at[pl.ds(start, rows)]


class Swap:
    def __init__(self, x, layout):
        self.x, self.layout = x, layout

    def shape(self, sizes):
        return self.x.shape

    def own_shape(self, sizes):
        return self.x.shape[1:]

    def offsets(self, sizes):
        return offsets(sizes, self.layout)

    def pair(self, x, out, here, to, off, sizes):
        return x.at[place(to, self.layout, sizes)], out.at[place(here, self.layout, sizes)]


class ColumnSwap:
    def __init__(self, x, block):
        self.x, self.block = x, block

    def shape(self, sizes):
        rows, columns = self.x.shape
        team = sizes["zl"] * sizes["y"]
        return (team, rows, columns // team)

    def own_shape(self, sizes):
        return self.shape(sizes)[1:]

    def offsets(self, sizes):
        return offsets(sizes, TEAM)

    def pieces(self, x, out, to, sizes):
        found = []
        for i, share in enumerate(offsets(sizes, SHARES)):
            start = pl.multiple_of(place({**share, **to}, AXES, sizes) * self.block, self.block)
            found.append(
                (x.at[:, pl.ds(start, self.block)], out.at[:, pl.ds(i * self.block, self.block)])
            )
        return found


class NearSwap(Swap):
    def pair(self, x, out, here, to, off, sizes):
        i = off[self.layout[0]]
        return x.at[i], out.at[i]


class Halves:
    def __init__(self, x):
        self.x = x

    def shape(self, sizes):
        rows, columns = self.x.shape
        return (2, rows, columns // 2)

    def own_shape(self, sizes):
        rows, columns = self.x.shape
        return (rows, columns // 2)

    def offsets(self, sizes):
        return offsets(sizes, ("c",))

    def pair(self, x, out, here, to, off, sizes):
        width = self.x.shape[1] // 2
        start = pl.multiple_of(to["c"] * width, width)
        return x.at[:, pl.ds(start, width)], out.at[off["c"]]


CHUNKS = 4
AHEAD = 2


class TeamSum:
    def __init__(self, x, y_first=2):
        self.x, self.y_first = x, y_first

    def shape(self, sizes):
        return (2,) + self.x.shape[2:]


class PeerSum:
    def __init__(self, x, x_inside):
        self.x, self.x_inside = x, x_inside

    def shape(self, sizes):
        rows, columns = self.x.shape
        return (rows // (sizes["x"] * sizes["zh"]), columns)


class Net:
    def __init__(self, sizes):
        self.sizes, self.count, self.reached = sizes, 0, set()

    def wire(self, off):
        self.reached.add(tuple(off.get(a, 0) for a in AXES))
        self.count += 1
        return self.count - 1, off

    def open(self, send_sem, recv_sem):
        self.send_sem, self.recv_sem = send_sem, recv_sem
        self.here = {a: lax.axis_index(a) for a in AXES}
        self.sent = []
        barrier = pltpu.get_barrier_semaphore()
        for off in sorted(self.reached):
            pl.semaphore_signal(
                barrier,
                inc=1,
                device_id=self.device(self.moved(dict(zip(AXES, off)))),
                device_id_type=pl.DeviceIdType.MESH,
            )
        pl.semaphore_wait(barrier, len(self.reached))

    def moved(self, off):
        return {
            a: lax.rem(self.here[a] + off[a], self.sizes[a]) if off.get(a, 0) else self.here[a]
            for a in AXES
        }

    def device(self, at):
        return tuple(at[a] for a in AXES)

    def send(self, src, dst, wire):
        sem, off = wire
        cp = pltpu.make_async_remote_copy(
            src_ref=src,
            dst_ref=dst,
            send_sem=self.send_sem.at[sem],
            recv_sem=self.recv_sem.at[sem],
            device_id=self.device(self.moved(off)),
            device_id_type=pl.DeviceIdType.MESH,
        )
        cp.start()
        self.sent.append(cp)
        return cp

    def settle(self, cp):
        cp.wait_send()
        self.sent = [other for other in self.sent if other is not cp]

    def close(self):
        for cp in self.sent:
            cp.wait_send()


class Relay:
    def __init__(self, job, number, net):
        self.job, self.net, self.sizes = job, net, net.sizes
        self.steps = []
        for part, order in enumerate(job.orders):
            groups = [(axes,) if isinstance(axes, str) else axes for axes in order]
            for off in offsets(self.sizes, [a for axes in groups for a in axes]):
                used = [i for i, axes in enumerate(groups) if any(off[a] for a in axes)]
                sends = [
                    net.wire(to)
                    for axes in groups[used[-1] + 1 if used else 0 :]
                    for to in offsets(self.sizes, axes)
                    if any(to.values())
                ]
                hops = len(used)
                key = (job.rank, part + 2 * hops, hops, number, part)
                self.steps.append((key, self, hops, part, off, sends))

    def open(self, x, out):
        self.x, self.out, self.arrivals = x, out, {}

    def run(self, hops, part, off, sends):
        job, net = self.job, self.net
        owner = net.moved(off)
        if hops:
            self.arrivals[part, tuple(sorted(off.items()))].wait_recv()
            source = job.spot(self.out, owner, off, part, self.sizes)
        else:
            source = job.cut(self.x, part)
        for wire in sends:
            there = dict(off)
            for a, d in wire[1].items():
                there[a] = -d % self.sizes[a]
            dst = job.spot(self.out, owner, there, part, self.sizes)
            self.arrivals[part, tuple(sorted(there.items()))] = net.send(source, dst, wire)

    def own(self, part):
        return self.job.spot(self.out, self.net.here, {a: 0 for a in AXES}, part, self.sizes)


class Stream:
    def __init__(self, net, shape, x_inside):
        self.net, self.x_inside = net, x_inside
        self.nx, self.nz = net.sizes["x"], net.sizes["zh"]
        self.columns, self.dtype = shape[1], BF16
        self.rows = shape[0] // (self.nx * self.nz * CHUNKS)
        self.chunks = [(z, q) for z in [*range(1, self.nz), 0] for q in range(CHUNKS)]
        self.x_wires = [[net.wire({"x": d}) for d in range(1, self.nx)] for _ in self.chunks]
        self.z_wires = [net.wire({"zh": z}) if z else None for z, _ in self.chunks]

    def shape(self):
        return jax.ShapeDtypeStruct((CHUNKS * self.rows, self.columns), self.dtype)

    def scratch(self):
        n, chunk = len(self.chunks), (self.rows, self.columns)
        return [
            pltpu.VMEM((n, *chunk), self.dtype),
            pltpu.VMEM((self.nx - 1, n, *chunk), self.dtype),
            pltpu.VMEM((self.nz - 1, CHUNKS, *chunk), self.dtype),
            pltpu.SemaphoreType.DMA((n,)),
            pltpu.SemaphoreType.DMA((CHUNKS,)),
        ]

    def open(self, term, out, mine, from_x, from_z, load_sem, store_sem):
        self.term, self.out, self.mine = term, out, mine
        self.from_x, self.from_z = from_x, from_z
        self.load_sem, self.store_sem = load_sem, store_sem
        self.loads, self.x_sent, self.z_sent, self.stores = {}, {}, {}, []

    def window(self, x, z, q):
        zh = self.net.moved({"zh": z})["zh"]
        if self.x_inside:
            block = (zh * CHUNKS + q) * self.nx + x
        else:
            block = (x * self.nz + zh) * CHUNKS + q
        return self.term.at[pl.ds(pl.multiple_of(block * self.rows, self.rows), self.rows)]

    def run(self, step, k):
        (self.issue, self.merge, self.last)[step](k)

    def issue(self, k):
        z, q = self.chunks[k]
        self.x_sent[k] = []
        for d, wire in enumerate(self.x_wires[k], 1):
            x = self.net.moved({"x": d})["x"]
            self.x_sent[k].append(
                self.net.send(self.window(x, z, q), self.from_x.at[d - 1, k], wire)
            )
        load = pltpu.make_async_copy(
            self.window(self.net.here["x"], z, q), self.mine.at[k], self.load_sem.at[k]
        )
        load.start()
        self.loads[k] = load

    def merge(self, k):
        z, q = self.chunks[k]
        self.loads[k].wait()
        for cp in self.x_sent[k]:
            cp.wait_recv()
        total = self.mine[k].astype(F32)
        for d in range(self.nx - 1):
            total += self.from_x[d, k].astype(F32)
        self.mine[k] = total.astype(self.dtype)
        if z:
            self.z_sent[z, q] = self.net.send(
                self.mine.at[k], self.from_z.at[z - 1, q], self.z_wires[k]
            )

    def last(self, q):
        k = self.chunks.index((0, q))
        total = self.mine[k].astype(F32)
        for z in range(1, self.nz):
            self.z_sent[z, q].wait_recv()
            total += self.from_z[z - 1, q].astype(F32)
        self.mine[k] = total.astype(self.dtype)
        store = pltpu.make_async_copy(
            self.mine.at[k], self.out.at[pl.ds(q * self.rows, self.rows)], self.store_sem.at[q]
        )
        store.start()
        self.stores.append(store)

    def close(self):
        for store in self.stores:
            store.wait()


class Adder:
    def __init__(self, job, number, net):
        self.job, self.net = job, net
        rows = job.x.shape[2] // CHUNKS
        self.steps = []
        self.parts = []
        for part in range(CHUNKS):
            first, second = ("y", "zl") if part < job.y_first else ("zl", "y")
            wires = net.wire({first: 1}), net.wire({first: 1}), net.wire({second: 1})
            self.parts.append((pl.ds(part * rows, rows), first, second, wires))
            self.steps.append(((0, part, 0, number, part), self, 0, part, None, None))
            self.steps.append(((1, part + 2, 1, number, part), self, 1, part, None, None))

    def scratch(self):
        shape = self.job.x.shape[2:]
        return [pltpu.VMEM(shape, self.job.x.dtype)] * 2 + [pltpu.SemaphoreType.DMA((CHUNKS,))]

    def open(self, x, out, term, far, sem):
        self.x, self.out, self.term, self.far, self.sem = x, out, term, far, sem
        self.waits, self.direct, self.summed = {}, [], []

    def run(self, hops, part, *_):
        window, first, second, wires = self.parts[part]
        y_first = first == "y"
        if not hops:
            self.waits[part] = self.net.send(
                self.x.at[1, 1, window], self.far.at[window], wires[0]
            )
            near = self.x.at[1, 0, window] if y_first else self.x.at[0, 1, window]
            self.direct.append(
                self.net.send(near, self.out.at[0 if y_first else 1, window], wires[1])
            )
            mine = self.x.at[0, 1, window] if y_first else self.x.at[1, 0, window]
            load = pltpu.make_async_copy(mine, self.term.at[window], self.sem.at[part])
            load.start()
            self.waits[part] = self.waits[part], load
            return
        far, load = self.waits[part]
        load.wait()
        far.wait_recv()
        total = self.term[window].astype(F32) + self.far[window].astype(F32)
        self.term[window] = total.astype(self.term.dtype)
        self.summed.append(
            self.net.send(
                self.term.at[window], self.out.at[1 if y_first else 0, window], wires[2]
            )
        )

    def finish(self):
        for cp in self.direct + self.summed:
            cp.wait_recv()


def exchange(jobs, collective_id, micros=50):
    net = Net({a: lax.axis_size(a) for a in AXES})
    sizes = net.sizes
    count = len(jobs)
    steps, swaps, runners, scratch = [], [], [], []
    for number, job in enumerate(jobs):
        if isinstance(job, Gather):
            runner = Relay(job, number, net)
            steps += runner.steps
            stage = [pltpu.VMEM(job.x.shape, job.x.dtype)]
        elif isinstance(job, TeamSum):
            runner = Adder(job, number, net)
            steps += runner.steps
            stage = runner.scratch()
        elif isinstance(job, PeerSum):
            runner = Stream(net, job.x.shape, job.x_inside)
            for k in range(len(runner.chunks)):
                steps.append(((0, k, 0, number, k), runner, 0, k))
                steps.append(((1, k + 2, 1, number, k), runner, 1, k))
            for k in range(CHUNKS):
                steps.append(((1, k + len(runner.chunks) + 2, 2, number, k), runner, 2, k))
            stage = runner.scratch()
        else:
            runner = None
            n = math.prod(sizes[a] for a in SHARES) if isinstance(job, ColumnSwap) else 1
            for off in job.offsets(sizes):
                if any(off.values()):
                    swaps.append((number, off, [net.wire(off) for _ in range(n)]))
            stage = [pltpu.VMEM(job.own_shape(sizes), job.x.dtype)]
        runners.append((runner, len(scratch), len(scratch) + len(stage)))
        scratch += stage
    steps.sort(key=lambda s: s[0])

    def kernel(*refs):
        ins, outs, rest = refs[:count], refs[count : 2 * count], refs[2 * count :]
        send_sem, recv_sem, local_sem, piece_sem = rest[-4:]
        net.open(send_sem, recv_sem)
        loads, stores = [], []
        for number, job in enumerate(jobs):
            runner, lo, hi = runners[number]
            if isinstance(job, (TeamSum, PeerSum)):
                runner.open(ins[number], outs[number], *rest[lo:hi])
                continue
            (stage,) = rest[lo:hi]
            if runner:
                runner.open(ins[number], outs[number])
                src = ins[number]
                puts = [
                    (job.cut(stage, part), runner.own(part)) for part in range(len(job.orders))
                ]
            elif isinstance(job, ColumnSwap):
                mine = {a: net.here[a] for a in TEAM}
                for i, (src, dst) in enumerate(job.pieces(ins[number], stage, mine, sizes)):
                    load = pltpu.make_async_copy(src, dst, piece_sem.at[number, i])
                    load.start()
                    loads.append((load, number, []))
                loads[-1][2].append((stage, outs[number].at[place(net.here, TEAM, sizes)]))
                continue
            else:
                none = {a: 0 for a in AXES}
                src, dst = job.pair(ins[number], outs[number], net.here, net.here, none, sizes)
                puts = [(stage, dst)]
            load = pltpu.make_async_copy(src, stage, local_sem.at[number, 0])
            load.start()
            loads.append((load, number, puts))
        for _, runner, hops, *what in steps:
            if not hops:
                runner.run(hops, *what)
        received = []
        for number, off, wires in swaps:
            to = net.moved(off)
            job = jobs[number]
            if isinstance(job, ColumnSwap):
                mine = outs[number].at[place(net.here, TEAM, sizes)]
                pairs = job.pieces(ins[number], mine, {a: to[a] for a in TEAM}, sizes)
            else:
                pairs = [job.pair(ins[number], outs[number], net.here, to, off, sizes)]
            for (src, dst), wire in zip(pairs, wires, strict=True):
                received.append(net.send(src, dst, wire))
        for load, number, puts in loads:
            load.wait()
            for i, (src, dst) in enumerate(puts):
                store = pltpu.make_async_copy(src, dst, local_sem.at[number, 1 + i])
                store.start()
                stores.append(store)
        for _, runner, hops, *what in steps:
            if hops:
                runner.run(hops, *what)
        for cp in received:
            cp.wait_recv()
        for runner, _, _ in runners:
            if isinstance(runner, Adder):
                runner.finish()
        net.close()
        for runner, _, _ in runners:
            if isinstance(runner, Stream):
                runner.close()
        for store in stores:
            store.wait()

    return pl.pallas_call(
        kernel,
        out_shape=[jax.ShapeDtypeStruct(job.shape(sizes), job.x.dtype) for job in jobs],
        in_specs=[pl.BlockSpec(memory_space=pl.ANY)] * count,
        out_specs=[pl.BlockSpec(memory_space=pl.ANY)] * count,
        scratch_shapes=scratch
        + [
            pltpu.SemaphoreType.DMA((net.count,)),
            pltpu.SemaphoreType.DMA((net.count,)),
            pltpu.SemaphoreType.DMA((count, 1 + CHUNKS)),
            pltpu.SemaphoreType.DMA((count, math.prod(sizes[a] for a in SHARES))),
        ],
        cost_estimate=pl.CostEstimate(
            flops=0, bytes_accessed=micros * 3_000_000, transcendentals=0
        ),
        compiler_params=pltpu.CompilerParams(
            collective_id=collective_id, has_side_effects=True, vmem_limit_bytes=VMEM_LIMIT
        ),
    )(*[job.x for job in jobs])


def sum_over(term, axis, outer=1):
    size = lax.axis_size(axis)
    me = lax.axis_index(axis)
    columns = term.shape[1]
    term = term.reshape(outer, -1, columns)
    while size > 1:
        size //= 2
        rows = term.shape[1] // 2
        pairs = [(i, i ^ size) for i in range(lax.axis_size(axis))]
        side = (me // size) % 2
        kept = lax.dynamic_slice_in_dim(term, side * rows, rows, axis=1)
        other = lax.ppermute(
            lax.dynamic_slice_in_dim(term, (1 - side) * rows, rows, axis=1), axis, pairs
        )
        term = kept.astype(F32) + other.astype(F32)
        if size > 1:
            term = term.astype(BF16)
    return term.reshape(-1, columns)


def dot(a, b, dims=None):
    if dims is None:
        return jnp.dot(a, b, preferred_element_type=F32)
    return lax.dot_general(a, b, dims, preferred_element_type=F32)


def rotate(t, cos, sin):
    half = t.shape[-1] // 2
    front, back = t[..., :half], t[..., half:]
    return jnp.concatenate([front * cos - back * sin, back * cos + front * sin], axis=-1)


def rms_scale(values):
    return lax.rsqrt(jnp.mean(values * values, axis=-1, keepdims=True) + EPS)


def attention(q, kv, q_pos, k_pos, scaling):
    n_slot, n_zh, _, n = k_pos.shape
    heads = q.shape[1] // HEAD

    def kernel(q_ref, kv_ref, q_pos_ref, k_pos_ref, o_ref, lse_ref):
        for s in range(n_slot):
            rows = slice(s * n, (s + 1) * n)
            for g in range(heads):
                cols = slice(g * HEAD, (g + 1) * HEAD)
                scores = []
                for z in range(n_zh):
                    score = dot(q_ref[rows, cols], kv_ref[z, rows, :HEAD], COLS_T) * scaling
                    allowed = k_pos_ref[s, z] <= q_pos_ref[...]
                    scores.append(jnp.where(allowed, score, -jnp.inf))
                peak = scores[0].max(axis=1, keepdims=True)
                for score in scores[1:]:
                    peak = jnp.maximum(peak, score.max(axis=1, keepdims=True))
                exps = [jnp.exp(score - peak) for score in scores]
                total = sum(e.sum(axis=1, keepdims=True) for e in exps)
                inverse = 1.0 / total
                o_ref[rows, cols] = sum(
                    dot((e * inverse).astype(BF16), kv_ref[z, rows, HEAD:])
                    for z, e in enumerate(exps)
                ).astype(BF16)
                lse_ref[s, g] = peak + jnp.log(total)

    vmem = pl.BlockSpec(memory_space=pltpu.VMEM)
    return pl.pallas_call(
        kernel,
        out_shape=[
            jax.ShapeDtypeStruct(q.shape, BF16),
            jax.ShapeDtypeStruct((n_slot, heads, n, 1), F32),
        ],
        in_specs=[vmem] * 4,
        out_specs=[vmem] * 2,
        compiler_params=pltpu.CompilerParams(vmem_limit_bytes=VMEM_LIMIT),
    )(q, kv, q_pos, k_pos)


def attention_back(
    ga, q, kv, lse, q_pos, k_pos, cos, sin, w_out, w_attn, out_parts, sums, scaling, collective_id
):
    net = Net({a: lax.axis_size(a) for a in AXES})
    own, width = ga.shape
    n_slot, n_zh, _, n = k_pos.shape
    n_tok = n_slot * n
    heads = q.shape[1] // HEAD
    columns = w_attn.shape[1]
    half = columns // 2
    ga_job = NearGather(ga, PAIRED_SLOTS, TO_TEAM_EVEN)
    gas = Relay(ga_job, 0, net)
    ga_steps = sorted(gas.steps, key=lambda step: step[0])
    adder = Adder(TeamSum(out_parts, CHUNKS), 1, net)
    streams, made = [], []
    if sums:
        down, _, gate_half, _, o_half = sums
        made = [(width, gate_half.shape[2])] * 2 + [(o_half.shape[2], width)]
        streams = [Stream(net, down.shape, False)]
        streams += [Stream(net, made[i], i < 2) for i in range(3)]
    n_chunks = n_zh * CHUNKS
    kv_wires = [[net.wire({"zh": z}) for z in range(1, n_zh)] for _ in range(n_slot)]
    half_wires = [net.wire({"c": 1}) for _ in range(n_slot)]
    y_rows, zl_rows = pl.ds(0, own // 2), pl.ds(own // 2, own // 2)
    far_wires = net.wire({"y": 1}), net.wire({"zl": 1})
    near_wires = net.wire({"y": 1}), net.wire({"zl": 1})
    n_sums = len(sums) if sums else 0
    n_local = 48

    def kernel(*refs):
        refs = iter(refs)

        def take(count):
            return list(itertools.islice(refs, count))

        ga_ref, q_ref, kv_ref, lse_ref, q_pos_ref, k_pos_ref = take(6)
        cos_ref, sin_ref, wo_ref, wa_ref, parts_ref = take(5)
        sum_ins = take(n_sums)
        gas_ref, half_ref, gn1_ref, added_ref = take(4)
        sum_outs, made_refs = take(len(streams)), take(len(made))
        gav, wo, wa, go, gkv, gkv_away, gkv_out, gkv_in, g_qkv, gn1, far = take(11)
        send_sem, recv_sem, local_sem = take(3)
        adder_scratch = take(3)
        net.open(send_sem, recv_sem)
        gas.open(ga_ref, gas_ref)
        adder.open(parts_ref, added_ref, *adder_scratch)
        for i, stream in enumerate(streams):
            stream.open([*sum_ins[:1], *made_refs][i], sum_outs[i], *take(5))
        used = iter(range(n_local))

        def local(src, dst):
            cp = pltpu.make_async_copy(src, dst, local_sem.at[next(used)])
            cp.start()
            return cp

        plan = []
        for i in range(len(streams)):
            for k in range(n_chunks):
                plan.append((i, k, False))
                q_chunk = k - (n_chunks - CHUNKS)
                if i and q_chunk >= 0:
                    plan.append((i - 1, q_chunk, True))
        plan += [(i, q_chunk, True) for i in range(len(streams))[-1:] for q_chunk in range(CHUNKS)]
        issued, merged = [0] * len(streams), [0] * len(streams)
        ready = [i == 0 for i in range(len(streams))]

        def pump():
            for i, stream in enumerate(streams):
                allowed = min(n_chunks, merged[i - 1] + AHEAD) if i else n_chunks
                while ready[i] and issued[i] < allowed:
                    stream.issue(issued[i])
                    issued[i] += 1

        def there(i):
            if sums:
                ready[i] = True
                pump()

        def flow(steps):
            while plan and steps:
                i, k, last = plan[0]
                if last:
                    streams[i].last(k)
                elif k < issued[i]:
                    streams[i].merge(k)
                    merged[i] += 1
                    pump()
                else:
                    return
                plan.pop(0)
                steps -= 1

        if sums:
            wr, lt, ot, o_v, wr_sem, lt_sem, ot_sem = take(7)

        def product(rhs_ref, term_ref, steps):
            lhs_ref, n_cols = sum_ins[1], wr.shape[2]
            n_tiles = width // own

            def lhs(t, slot, c):
                at = pl.ds(pl.multiple_of(t * own, own), own)
                return pltpu.make_async_copy(
                    lhs_ref.at[c, :, at], lt.at[slot, c], lt_sem.at[slot, c]
                )

            for part in range(rhs_ref.shape[2] // n_cols):
                window = pl.ds(part * n_cols, n_cols)
                rhs = [
                    pltpu.make_async_copy(rhs_ref.at[c, :, window], wr.at[c], wr_sem.at[c])
                    for c in range(2)
                ]
                for c in range(2):
                    rhs[c].start()
                    lhs(0, 0, c).start()
                for c in range(2):
                    rhs[c].wait()

                def store(t, slot, window=window):
                    at = pl.ds(pl.multiple_of(t * own, own), own)
                    return pltpu.make_async_copy(
                        ot.at[slot], term_ref.at[at, window], ot_sem.at[slot]
                    )

                def tile(t, _, store=store):
                    slot = lax.rem(t, 2)

                    @pl.when(t + 1 < n_tiles)
                    def _():
                        for c in range(2):
                            lhs(t + 1, 1 - slot, c).start()

                    for c in range(2):
                        lhs(t, slot, c).wait()

                    @pl.when(t >= 2)
                    def _():
                        store(t - 2, slot).wait()

                    value = dot(lt[slot].reshape(2 * n_tok, own), wr[...].reshape(2 * n_tok, n_cols), ROWS_T)
                    ot[slot] = value.astype(BF16)
                    store(t, slot).start()
                    return 0

                lax.fori_loop(0, n_tiles, tile, 0)
                store(n_tiles - 2, n_tiles % 2).wait()
                store(n_tiles - 1, 1 - n_tiles % 2).wait()
                flow(steps)

        for _, _, hops, *what in ga_steps:
            if not hops:
                gas.run(hops, *what)
        if sums:
            pump()
            got_o = local(sum_ins[4], o_v)
        got_wo, got_wa = local(wo_ref, wo), local(wa_ref, wa)
        got_ga = local(ga_ref, gav.at[0, 0])
        got_ga.wait()
        kept = [local(ga_job.cut(gav.at[0, 0], p), gas.own(p)) for p in range(CHUNKS)]
        got_wo.wait()
        got_wa.wait()
        if sums:
            product(sum_ins[2], made_refs[0], 1)
            there(1)

        def turn_back(t, rows):
            h = HEAD // 2
            c, sn = cos_ref[rows], sin_ref[rows]
            front, back = t[:, :h], t[:, h:]
            return jnp.concatenate([front * c + back * sn, back * c - front * sn], axis=1).astype(
                BF16
            )

        def slot(s):
            keys = slice(s * n, (s + 1) * n)
            for j in range(2):
                at = pl.ds(s * n + j * own, own)
                go[at, :] = dot(gav[s, j], wo[...], COLS_T).astype(BF16)
            for turn, (g, j) in enumerate(itertools.product(range(heads), range(n // own))):
                rows = slice(s * n + j * own, s * n + (j + 1) * own)
                here = slice(j * own, (j + 1) * own)
                cols = slice(g * HEAD, (g + 1) * HEAD)
                q_g, go_g, lse_g = q_ref[rows, cols], go[rows, cols], lse_ref[s, g, here]
                probs, gps = [], []
                for z in range(n_zh):
                    score = dot(q_g, kv_ref[z, keys, :HEAD], COLS_T) * scaling
                    allowed = k_pos_ref[s, z] <= q_pos_ref[here]
                    probs.append(jnp.where(allowed, jnp.exp(score - lse_g), 0.0))
                    gps.append(dot(go_g, kv_ref[z, keys, HEAD:], COLS_T))
                delta = sum((p * gp).sum(axis=1, keepdims=True) for p, gp in zip(probs, gps))
                gq = 0.0
                for z in range(n_zh):
                    gs = (probs[z] * (gps[z] - delta)).astype(BF16)
                    gq += dot(gs, kv_ref[z, keys, :HEAD])
                    gk = dot(gs, q_g, ROWS_T) * scaling
                    gv = dot(probs[z].astype(BF16), go_g, ROWS_T)
                    total = gkv_away.at[z - 1] if z else gkv.at[s]
                    if turn:
                        gk, gv = gk + total[:, :HEAD], gv + total[:, HEAD:]
                    total[:, :HEAD] = gk
                    total[:, HEAD:] = gv
                g_qkv[rows, cols] = turn_back(gq * scaling, rows)
            sent = []
            for z in range(n_zh - 1):
                gkv_out[s, z] = gkv_away[z].astype(BF16)
                sent.append(net.send(gkv_out.at[s, z], gkv_in.at[s, z], kv_wires[s][z]))
            return sent

        def keys(s, sent):
            rows = slice(s * n, (s + 1) * n)
            q_cols = heads * HEAD
            mine = gkv[s]
            for z, cp in enumerate(sent):
                cp.wait_recv()
                mine = mine + gkv_in[s, z].astype(F32)
            g_qkv[rows, q_cols : q_cols + HEAD] = turn_back(mine[:, :HEAD], rows)
            g_qkv[rows, q_cols + HEAD :] = mine[:, HEAD:].astype(BF16)
            away = pl.ds(pl.multiple_of((1 - net.here["c"]) * half, half), half)
            here = pl.ds(pl.multiple_of(net.here["c"] * half, half), half)
            window = pl.ds(s * n, n)
            halves.append(
                net.send(g_qkv.at[window, away], half_ref.at[1, window], half_wires[s])
            )
            kept.append(local(g_qkv.at[window, here], half_ref.at[0, window]))

        def term(r):
            def tile(t, _):
                at = pl.ds(pl.multiple_of(t * TILE, TILE), TILE)
                value = dot(g_qkv[r * own : (r + 1) * own], wa[at, :], COLS_T)
                gn1[r, :, at] = value.astype(BF16)
                return 0

            lax.fori_loop(0, width // TILE, tile, 0)

        def add(r, window):
            gn1[r, window] = (gn1[r, window].astype(F32) + far[window].astype(F32)).astype(BF16)

        def add_out(hops):
            for _, _, at, *what in sorted(adder.steps, key=lambda step: step[0]):
                if at == hops:
                    adder.run(at, *what)

        halves, late, arrived, sent = [], [], set(), {}
        for _, _, hops, part, off, sends in ga_steps:
            if not hops:
                continue
            if off["c"]:
                late.append((hops, part, off, sends))
                continue
            gas.run(hops, part, off, sends)
            if part == CHUNKS - 1:
                i, j = off["y"], off["zl"]
                local(gas_ref.at[0, i, j], gav.at[i, j]).wait()
                arrived.add((i, j))
                if arrived >= {(0, 1), (1, 0)} and 0 not in sent:
                    flow(2)
                    sent[0] = slot(0)
                    flow(1)
        flow(1)
        sent[1] = slot(1)
        add_out(0)
        flow(2)
        if sums:
            product(sum_ins[3], made_refs[1], 2)
            there(2)
        keys(0, sent[0])
        term(1)
        term(0)
        add_out(1)
        flow(4)
        keys(1, sent[1])
        term(3)
        to_far = (
            net.send(gn1.at[3, y_rows], far.at[y_rows], far_wires[0]),
            net.send(gn1.at[3, zl_rows], far.at[zl_rows], far_wires[1]),
        )
        term(2)
        kept_gn1 = local(gn1.at[0], gn1_ref.at[0])
        flow(2)
        to_far[1].wait_recv()
        add(2, zl_rows)
        to_y = net.send(gn1.at[2], gn1_ref.at[1], near_wires[0])
        to_far[0].wait_recv()
        add(1, y_rows)
        to_zl = net.send(gn1.at[1], gn1_ref.at[2], near_wires[1])
        for hops, part, off, sends in late:
            gas.run(hops, part, off, sends)
        flow(2)
        if sums:
            for cp in (*to_far, to_y, to_zl):
                net.settle(cp)
            kept_gn1.wait()
            got_o.wait()
            others = [
                local(gas_ref.at[1, i, j], gn1.at[2 * i + j]) for i in range(2) for j in range(2)
            ]
            for cp in others:
                cp.wait()

            def output(t, _):
                at = pl.ds(pl.multiple_of(t * TILE, TILE), TILE)
                value = dot(o_v[0], gav[:, :, :, at].reshape(n_tok, TILE), ROWS_T)
                value += dot(o_v[1], gn1[:, :, at].reshape(n_tok, TILE), ROWS_T)
                far[:, at] = value.astype(BF16)
                return 0

            lax.fori_loop(0, width // TILE, output, 0)
            local(far, made_refs[2]).wait()
            there(3)
        else:
            kept_gn1.wait()
        flow(100)
        assert not plan
        for cp in halves + [to_y, to_zl]:
            cp.wait_recv()
        adder.finish()
        net.close()
        for stream in streams:
            stream.close()
        for cp in kept:
            cp.wait()

    shape = jax.ShapeDtypeStruct
    vmem, hbm = pl.BlockSpec(memory_space=pltpu.VMEM), pl.BlockSpec(memory_space=pl.ANY)
    scratch = [
        pltpu.VMEM((2, 2, own, width), BF16),
        pltpu.VMEM(w_out.shape, BF16),
        pltpu.VMEM(w_attn.shape, BF16),
        pltpu.VMEM((n_tok, heads * HEAD), BF16),
        pltpu.VMEM((n_slot, n, 2 * HEAD), F32),
        pltpu.VMEM((n_zh - 1, n, 2 * HEAD), F32),
        pltpu.VMEM((n_slot, n_zh - 1, n, 2 * HEAD), BF16),
        pltpu.VMEM((n_slot, n_zh - 1, n, 2 * HEAD), BF16),
        pltpu.VMEM((n_tok, columns), BF16),
        pltpu.VMEM((4, own, width), BF16),
        pltpu.VMEM((own, width), BF16),
        pltpu.SemaphoreType.DMA((net.count,)),
        pltpu.SemaphoreType.DMA((net.count,)),
        pltpu.SemaphoreType.DMA((n_local,)),
        *adder.scratch(),
    ]
    for stream in streams:
        scratch += stream.scratch()
    if sums:
        scratch += [
            pltpu.VMEM((2, n_tok, TILE), BF16),
            pltpu.VMEM((2, 2, n_tok, own), BF16),
            pltpu.VMEM((2, own, TILE), BF16),
            pltpu.VMEM(o_half.shape, BF16),
            pltpu.SemaphoreType.DMA((2,)),
            pltpu.SemaphoreType.DMA((2, 2)),
            pltpu.SemaphoreType.DMA((2,)),
        ]
    return pl.pallas_call(
        kernel,
        out_shape=[
            shape((2, 2, 2, own, width), BF16),
            shape((2, n_tok, half), BF16),
            shape((3, own, width), BF16),
            shape((2, own, width), BF16),
            *[stream.shape() for stream in streams],
            *[shape(dims, BF16) for dims in made],
        ],
        in_specs=[hbm] + [vmem] * 7 + [hbm] * (3 + n_sums),
        out_specs=[hbm] * (4 + len(streams) + len(made)),
        scratch_shapes=scratch,
        compiler_params=pltpu.CompilerParams(
            collective_id=collective_id, has_side_effects=True, vmem_limit_bytes=FFN_VMEM_LIMIT
        ),
    )(ga, q, kv, lse, q_pos, k_pos, cos, sin, w_out, w_attn, out_parts, *(sums or ()))


def positions(members):
    total = lax.axis_size("zh") * lax.axis_size("zl")
    half = jnp.arange(2)[None, :, None]
    row = jnp.arange(BLK)[None, None, :]
    j = members[:, None, None]
    return (jnp.where(half == 0, j, 2 * total - 1 - j) * BLK + row).reshape(-1)


OUTWARD = ("zh", "x", "c")
TILE = 512
TO_TEAM = [("zl", "y", "c")] * CHUNKS
TO_TEAM_EVEN = [("zl", "y", "c"), ("y", "zl", "c")] * (CHUNKS // 2)


def feed_forward(norm, gd, w_gate, w_down, up_part, collective_id):
    net = Net({a: lax.axis_size(a) for a in AXES})
    sizes = net.sizes
    own, width = norm.shape
    ff = w_gate.shape[1]
    half = ff // 2
    norm_job = NearGather(norm, PAIRED_SLOTS, TO_TEAM_EVEN)
    up_job = RowGather(up_part, None, [OUTWARD] * up_part.shape[0])
    norms, ups = Relay(norm_job, 0, net), Relay(up_job, 1, net)
    steps = sorted(norms.steps + ups.steps, key=lambda s: s[0])
    y_rows, zl_rows = pl.ds(0, own // 2), pl.ds(own // 2, own // 2)
    far_wires = net.wire({"y": 1}), net.wire({"zl": 1})
    near_wires = net.wire({"y": 1}), net.wire({"zl": 1})
    half_wires = [[net.wire({"c": 1}) for _ in range(3)] for _ in range(4)]
    n_local = 64

    def kernel(
        norm_ref, gd_ref, w_gate_ref, w_down_ref, up_ref,
        norms_ref, gate_half, up_half, mixed_half, gn2_ref, out_ref,
        wg, wu, wd, nv, gdv, gate, gm, gg, gu, mx, far, send_sem, recv_sem, local_sem,
    ):
        net.open(send_sem, recv_sem)
        norms.open(norm_ref, norms_ref)
        ups.open(up_ref, wu)
        used = iter(range(n_local))

        def local(src, dst):
            cp = pltpu.make_async_copy(src, dst, local_sem.at[next(used)])
            cp.start()
            return cp

        got_norm = local(norm_ref, nv.at[0])
        for _, runner, hops, *what in steps:
            if not hops:
                runner.run(hops, *what)
        got_gate = local(w_gate_ref, wg)
        got_gd = [local(gd_ref.at[0, 0, 0], gdv.at[0]), local(gd_ref.at[0, 1, 0], gdv.at[1])]
        got_down = local(w_down_ref, wd)
        got_up = [local(ups.job.cut(up_ref, p), ups.own(p)) for p in range(len(up_job.orders))]
        got_norm.wait()
        kept_norm = [local(norm_job.cut(nv.at[0], p), norms.own(p)) for p in range(CHUNKS)]

        def tiles(n, body):
            def step(t, _):
                body(pl.ds(pl.multiple_of(t * TILE, TILE), TILE))
                return 0

            lax.fori_loop(0, n // TILE, step, 0)

        gd_turn = [(0, 0), (1, 0), (0, 1), (1, 1)]

        def begin(turn):
            i, j = gd_turn[turn]
            r = 2 * i + j

            def one(t):
                gate[r, :, t] = dot(nv[r], wg[:, t])

            tiles(ff, one)
            got_gd[turn].wait()

            def two(t):
                gm[r, :, t] = dot(gdv[turn % 2], wd[t, :], COLS_T)

            tiles(ff, two)
            if turn + 2 < 4:
                got_gd.append(local(gd_ref.at[(0, *gd_turn[turn + 2])], gdv.at[turn % 2]))

        got_gate.wait()
        got_down.wait()
        begin(0)
        late = []
        arrived = {(1, 0): 0, (0, 1): 0, (1, 1): 0}
        turn = 1
        for _, runner, hops, part, off, sends in steps:
            if not hops:
                continue
            if runner is norms and off["c"]:
                late.append((hops, part, off, sends))
                continue
            runner.run(hops, part, off, sends)
            if runner is norms:
                arrived[off["y"], off["zl"]] += 1
                while turn < 4 and arrived[gd_turn[turn]] == CHUNKS:
                    i, j = gd_turn[turn]
                    local(norms_ref.at[0, i, j], nv.at[2 * i + j]).wait()
                    begin(turn)
                    turn += 1
        for cp in got_up + kept_norm:
            cp.wait()

        halves, busy = [], {}

        def finish(r, buf):
            for cp, remote in busy.pop(buf, []):
                net.settle(cp) if remote else cp.wait()

            def one(t):
                up = dot(nv[r], wu[:, t])
                g, m = gate[r, :, t], gm[r, :, t]
                s = 1.0 / (1.0 + jnp.exp(-g))
                gs = g * s
                mx[r, :, t] = (gs * up).astype(BF16)
                gg[buf, :, t] = (m * up * s * (1.0 + g * (1.0 - s))).astype(BF16)
                gu[buf, :, t] = (m * gs).astype(BF16)

            tiles(ff, one)
            mine = pl.ds(pl.multiple_of(net.here["c"] * half, half), half)
            other = pl.ds(pl.multiple_of((1 - net.here["c"]) * half, half), half)
            rows = pl.ds(r * own, own)
            for n, (ref, out) in enumerate(
                ((gg.at[buf], gate_half), (gu.at[buf], up_half), (mx.at[r], mixed_half))
            ):
                cp = local(ref.at[:, mine], out.at[0, rows])
                sent = net.send(ref.at[:, other], out.at[1, rows], half_wires[r][n])
                halves.append(sent)
                busy.setdefault(buf if n < 2 else "mixed", []).extend([(cp, False), (sent, True)])

            def two(t):
                term = dot(gg[buf], wg[t, :], COLS_T) + dot(gu[buf], wu[t, :], COLS_T)
                nv[r, :, t] = term.astype(BF16)

            tiles(width, two)

        def add(r, window):
            nv[r, window] = (nv[r, window].astype(F32) + far[window].astype(F32)).astype(BF16)

        finish(3, 0)
        to_far = (
            net.send(nv.at[3, y_rows], far.at[y_rows], far_wires[0]),
            net.send(nv.at[3, zl_rows], far.at[zl_rows], far_wires[1]),
        )
        finish(2, 1)
        to_far[1].wait_recv()
        add(2, zl_rows)
        to_y = net.send(nv.at[2], gn2_ref.at[1], near_wires[0])
        finish(1, 0)
        to_far[0].wait_recv()
        add(1, y_rows)
        to_zl = net.send(nv.at[1], gn2_ref.at[2], near_wires[1])
        finish(0, 1)
        stored = [local(nv.at[0], gn2_ref.at[0])]
        for n, r in enumerate((3, 2, 1, 0)):
            buf = n % 2
            for cp, remote in busy.pop(buf, []):
                net.settle(cp) if remote else cp.wait()

            def down(t):
                gg[buf, :, t] = dot(mx[r], wd[:, t]).astype(BF16)

            tiles(width, down)
            busy[buf] = [(local(gg.at[buf], out_ref.at[r // 2, r % 2]), False)]
        for hops, part, off, sends in late:
            norms.run(hops, part, off, sends)
        to_y.wait_recv()
        to_zl.wait_recv()
        for cp in halves:
            cp.wait_recv()
        net.close()
        for cps in busy.values():
            for cp, remote in cps:
                if not remote:
                    cp.wait()
        for cp in stored:
            cp.wait()

    shape = jax.ShapeDtypeStruct
    weight = pltpu.VMEM((width, ff), BF16)
    return pl.pallas_call(
        kernel,
        out_shape=[
            shape((2, 2, 2, own, width), BF16),
            *[shape((2, 4 * own, half), BF16)] * 3,
            shape((3, own, width), BF16),
            shape((2, 2, own, width), BF16),
        ],
        in_specs=[pl.BlockSpec(memory_space=pl.ANY)] * 5,
        out_specs=[pl.BlockSpec(memory_space=pl.ANY)] * 6,
        scratch_shapes=[
            weight,
            weight,
            pltpu.VMEM((ff, width), BF16),
            pltpu.VMEM((4, own, width), BF16),
            pltpu.VMEM((2, own, width), BF16),
            pltpu.VMEM((4, own, ff), F32),
            pltpu.VMEM((4, own, ff), F32),
            pltpu.VMEM((2, own, ff), BF16),
            pltpu.VMEM((2, own, ff), BF16),
            pltpu.VMEM((4, own, ff), BF16),
            pltpu.VMEM((own, width), BF16),
            pltpu.SemaphoreType.DMA((net.count,)),
            pltpu.SemaphoreType.DMA((net.count,)),
            pltpu.SemaphoreType.DMA((n_local,)),
        ],
        cost_estimate=pl.CostEstimate(
            flops=0, bytes_accessed=130 * 3_000_000, transcendentals=0
        ),
        compiler_params=pltpu.CompilerParams(
            collective_id=collective_id, has_side_effects=True, vmem_limit_bytes=FFN_VMEM_LIMIT
        ),
    )(norm, gd, w_gate, w_down, up_part)


def on_device(
    inputs,
    lengths,
    attn_gain,
    query_weight,
    key_matrix,
    value_matrix,
    output_weight,
    ffn_gain,
    gate_weight,
    up_weight,
    down_weight,
    cotangent,
):
    size = {a: lax.axis_size(a) for a in AXES}
    at = {a: lax.axis_index(a) for a in AXES}
    width = inputs.shape[3]
    own = inputs.shape[1] * inputs.shape[2]
    rows = query_weight.shape[0]
    n_dev = width // rows
    team = size["y"] * size["zl"]
    q_cols = query_weight.shape[1] // team
    kv_cols = key_matrix.shape[1] // team
    ff_rows = down_weight.shape[0]
    ff = gate_weight.shape[1] // team
    heads = q_cols // HEAD
    n_tok = team * own
    scaling = HEAD**-0.5

    def by_team(w):
        return w.reshape(rows, team, -1).transpose(1, 0, 2)

    def ff_cut(w):
        if ff_rows % 128 == 0:
            return ColumnSwap(w, ff_rows)
        cut = w.reshape(rows, *(size[a] for a in AXES), ff_rows)
        return Swap(cut.transpose(2, 3, 0, 5, 4, 1, 6).reshape(team, rows, ff), TEAM)

    attn_cut = jnp.concatenate(
        [by_team(query_weight), by_team(key_matrix), by_team(value_matrix)], axis=2
    )
    row = [jnp.pad(gain.astype(F32), (0, 64 - rows)) for gain in (attn_gain, ffn_gain)]
    tile = jnp.concatenate(
        [jnp.concatenate(row)[None], jnp.full((7, 128), lengths[0].astype(F32))]
    )
    tiles, attn_part, gate_part, up_part = exchange(
        [
            Gather(tile, AXES, [(("c", "x", "y"), ("zl", "zh"))], rank=0),
            Swap(attn_cut, TEAM),
            ff_cut(gate_weight),
            ff_cut(up_weight),
        ],
        1,
    )
    w_down = lax.all_gather(down_weight, SHARES, axis=0, tiled=True)
    gain_one = tiles[:, 0, :rows].reshape(1, width)
    gain_two = tiles[:, 0, 64 : 64 + rows].reshape(1, width)
    slots = tiles[: n_dev // (size["zh"] * size["zl"]), 1, 0].reshape(
        size["y"], size["x"], size["c"]
    )
    lens = slots[at["y"] ^ jnp.arange(2), at["x"], at["c"]].astype(jnp.int32)

    per_head = n_dev // team

    def head_home(i):
        f, t = i // per_head, i % per_head
        zl, y = f // size["y"], f % size["y"]
        zh, t = t % size["zh"], t // size["zh"]
        x, c = t % size["x"], t // size["x"]
        return (((zh * size["zl"] + zl) * size["y"] + y) * size["x"] + x) * size["c"] + c

    homes = [(i, head_home(i)) for i in range(n_dev)]
    out_part = lax.ppermute(output_weight, AXES, homes)

    def row_gather(part):
        return RowGather(part, None, [OUTWARD] * team)

    my_pos = positions((at["zh"] * size["zl"] + at["zl"])[None])
    valid = (my_pos < lengths[0]).astype(F32)[:, None]
    near_zl = at["zl"] ^ jnp.arange(2)
    near_zh = (at["zh"] + jnp.arange(size["zh"])) % size["zh"]
    q_pos = positions(at["zh"] * 2 + near_zl)
    n_q = q_pos.shape[0]
    k_pos = positions((near_zh[:, None] * 2 + near_zl[None, :]).reshape(-1))
    past = size["zh"] * n_q
    k_pos = jnp.where(k_pos[None] < lens[:, None], k_pos[None], past)
    k_pos = k_pos.reshape(2, size["zh"], 1, n_q)
    half = HEAD // 2
    freq = ROPE_BASE ** (-2.0 * jnp.arange(half).astype(F32) / HEAD)
    angles = q_pos.astype(F32)[:, None] * freq[None, :]
    q_pos = q_pos[:, None]
    cos = jnp.tile(jnp.cos(angles), (size["y"], 1))
    sin = jnp.tile(jnp.sin(angles), (size["y"], 1))

    tokens = inputs.reshape(own, width).astype(F32)
    scale_one = rms_scale(tokens)
    norm_one = (tokens * scale_one * gain_one).astype(BF16)
    norm_one_pair, w_attn, w_out = exchange(
        [
            NearGather(norm_one, PAIRED_SLOTS, TO_TEAM),
            row_gather(attn_part),
            Gather(out_part, SHARES, [OUTWARD] * (rows // 16)),
        ],
        2,
    )
    norm_one_pair = norm_one_pair.reshape(2, n_tok, width)
    w_attn = w_attn.reshape(width, -1)
    w_out = w_out.reshape(q_cols, width)
    qkv = dot(norm_one_pair[0], w_attn)
    turned = [
        rotate(qkv[:, h * HEAD : (h + 1) * HEAD], cos, sin).astype(BF16) for h in range(heads + 1)
    ]
    q = jnp.concatenate(turned[:heads], axis=1)
    kv = jnp.concatenate([turned[heads], qkv[:, q_cols + kv_cols :].astype(BF16)], axis=1)
    gy = valid * cotangent.reshape(own, width).astype(F32)
    kv_all, gd_pair = exchange(
        [
            NearGather(kv, ("zh",), [("zh",)]),
            NearGather(gy.astype(BF16), PAIRED_SLOTS, TO_TEAM_EVEN),
        ],
        3,
    )
    o, lse = attention(q, kv_all, q_pos, k_pos, scaling)

    o_parts = dot(o, w_out).astype(BF16).reshape(2, 2, own, width)
    o_added, w_gate, o_half = exchange(
        [TeamSum(o_parts, 4), row_gather(gate_part), Halves(o)], 4, micros=70
    )

    def added(term, others):
        return term.astype(F32) + others[0].astype(F32) + others[1].astype(F32)

    h1 = tokens + added(o_parts[0, 0], o_added)
    scale_two = rms_scale(h1)
    norm_two = (h1 * scale_two * gain_two).astype(BF16)
    norm_two_pair, gate_half, up_half, mixed_half, gn2_terms, out_parts = feed_forward(
        norm_two, gd_pair, w_gate, w_down, up_part, 5
    )
    norm_two_pair = norm_two_pair.reshape(2, n_tok, width)
    gd_pair = gd_pair.reshape(2, n_tok, width)
    gn2 = added(gn2_terms[0], gn2_terms[1:]) * gain_two
    gh1 = gy + scale_two * gn2 - h1 * scale_two**3 * jnp.mean(h1 * gn2, axis=-1, keepdims=True)

    down_term = dot(mixed_half, gd_pair, PAIR_ROWS_T).astype(BF16)
    pairs = size["x"] == size["zh"] == 2
    sums = (down_term, norm_two_pair, gate_half, up_half, o_half) if pairs else None
    ga_pair, g_qkv_half, gn1_terms, out_added, *totals = attention_back(
        gh1.astype(BF16), q, kv_all, lse, q_pos, k_pos, cos, sin, w_out, w_attn, out_parts, sums,
        scaling, 8,
    )
    outputs = valid * (h1 + added(out_parts[0, 0], out_added))
    outputs = outputs.astype(BF16).reshape(inputs.shape)
    attn_term = dot(norm_one_pair, g_qkv_half, PAIR_ROWS_T).astype(BF16)
    n_owners = math.prod(size[a] for a in OWNERS)

    def by_owner(total):
        return Swap(total.astype(BF16).reshape(n_owners, rows, -1), OWNERS)

    homeward = [(b, a) for a, b in homes]
    if pairs:
        down_grad, gate_sum, up_sum, out_sum = totals[:4]
        output_grad = lax.ppermute(out_sum, AXES, homeward)
        attn_sum, gate_sum, up_sum = exchange(
            [PeerSum(attn_term, True), by_owner(gate_sum), by_owner(up_sum)], 9
        )
        attn_sum, output_grad = lax.optimization_barrier((attn_sum, output_grad))
        (attn_sum,) = exchange([by_owner(attn_sum)], 10, micros=10)
    else:
        outer = size["zh"] * team

        def sum_peers(term, outer=1):
            return sum_over(sum_over(term, "x", outer).astype(BF16), "zh").astype(BF16)

        gate_term = dot(norm_two_pair, gate_half, PAIR_ROWS_T).astype(BF16)
        up_term = dot(norm_two_pair, up_half, PAIR_ROWS_T).astype(BF16)
        out_term = dot(o_half, ga_pair.reshape(2, n_tok, width), PAIR_ROWS_T).astype(BF16)
        down_grad = sum_peers(down_term)
        output_grad = lax.ppermute(sum_peers(out_term), AXES, homeward)
        terms = (attn_term, gate_term, up_term)
        attn_sum, gate_sum, up_sum = exchange(
            [by_owner(sum_peers(term, outer)) for term in terms], 9
        )
    gn1 = added(gn1_terms[0], gn1_terms[1:]) * gain_one
    g_tokens = (
        gh1
        + scale_one * gn1
        - tokens * scale_one**3 * jnp.mean(tokens * gn1, axis=-1, keepdims=True)
    )
    input_grad = g_tokens.astype(BF16).reshape(inputs.shape)

    if ff_rows % 128 == 0:
        (query_grad, key_grad, value_grad, gate_grad, up_grad, attn_against, ffn_against) = finish(
            (attn_sum, gate_sum, up_sum),
            (query_weight, key_matrix, value_matrix, gate_weight, up_weight),
            ff_rows,
        )
        attn_against, ffn_against = attn_against[:, 0], ffn_against[:, 0]
    else:

        def ff_natural(total):
            cut = total.reshape(
                size["zl"], size["y"], size["c"], rows, size["x"], size["zh"], ff_rows
            )
            return cut.transpose(3, 5, 0, 1, 4, 2, 6).reshape(rows, -1).astype(F32)

        def side(part):
            return part.transpose(1, 0, 2).reshape(rows, -1).astype(F32)

        attn_sum = attn_sum.reshape(team, 2, rows, -1)
        query_grad = side(attn_sum[:, 0])
        key_grad = side(attn_sum[:, 1, :, :kv_cols])
        value_grad = side(attn_sum[:, 1, :, kv_cols:])
        gate_grad = ff_natural(gate_sum)
        up_grad = ff_natural(up_sum)

        def against(w, g):
            return jnp.sum(w.astype(F32) * g, axis=1)

        attn_against = (
            against(query_weight, query_grad)
            + against(key_matrix, key_grad)
            + against(value_matrix, value_grad)
        )
        ffn_against = against(gate_weight, gate_grad) + against(up_weight, up_grad)
    attn_gain_grad = attn_against / attn_gain.astype(F32)
    ffn_gain_grad = ffn_against / ffn_gain.astype(F32)
    return (
        outputs,
        input_grad,
        attn_gain_grad,
        query_grad,
        key_grad,
        value_grad,
        output_grad.astype(F32),
        ffn_gain_grad,
        gate_grad,
        up_grad,
        down_grad.astype(F32),
    )


def finish(sums, weights, block):
    sizes = {a: lax.axis_size(a) for a in AXES}
    rows = weights[0].shape[0]
    members = offsets(sizes, OWNERS)
    shares = offsets(sizes, ("x", "zh"))

    def kernel(
        attn, gate, up, wq, wk, wv, wg, wu, gq, gk, gv, gg, gu, attn_total, ffn_total
    ):
        totals = []

        def put(value, out, weight, start):
            value = value.astype(F32)
            width = value.shape[1]
            out[:, start : start + width] = value
            totals.append(
                jnp.sum(weight[:, start : start + width].astype(F32) * value, axis=1, keepdims=True)
            )

        q_width, kv_width = gq.shape[1] // 4, gk.shape[1] // 4
        for i, owner in enumerate(members):
            f = place(owner, TEAM, sizes)
            if owner["c"] == 0:
                put(attn[i], gq, wq, f * q_width)
            else:
                put(attn[i, :, :kv_width], gk, wk, f * kv_width)
                put(attn[i, :, kv_width:], gv, wv, f * kv_width)
        attn_total[...] = sum(totals)
        totals.clear()
        for i, owner in enumerate(members):
            for n, share in enumerate(shares):
                start = place({**owner, **share}, AXES, sizes) * block
                window = slice(n * block, (n + 1) * block)
                put(gate[i, :, window], gg, wg, start)
                put(up[i, :, window], gu, wu, start)
        ffn_total[...] = sum(totals)

    shape = jax.ShapeDtypeStruct
    return pl.pallas_call(
        kernel,
        out_shape=[shape(w.shape, F32) for w in weights] + [shape((rows, 1), F32)] * 2,
        in_specs=[pl.BlockSpec(memory_space=pltpu.VMEM)] * 8,
        out_specs=[pl.BlockSpec(memory_space=pltpu.VMEM)] * 7,
        compiler_params=pltpu.CompilerParams(vmem_limit_bytes=VMEM_LIMIT),
    )(*sums, *weights)


def solution(mesh):
    ctx, fsdp = mesh.shape["ctx"], mesh.shape["fsdp"]
    grid = Mesh(mesh.devices.reshape(ctx // 2, 2, 2, fsdp // 4, 2), AXES)
    act = P(("y", "x", "c"), None, ("zh", "zl"), None)
    row = P(AXES)
    return jax.shard_map(
        on_device,
        mesh=grid,
        in_specs=(act, P(("y", "x", "c"))) + (row,) * 9 + (act,),
        out_specs=(act, act) + (row,) * 9,
        check_vma=False,
    )
```

```python
import itertools
import math

import jax
import jax.numpy as jnp
from jax import lax
from jax.experimental import pallas as pl
from jax.experimental.pallas import tpu as pltpu
from jax.sharding import Mesh
from jax.sharding import PartitionSpec as P

HEAD = 256
VMEM_LIMIT = 48 << 20
FFN_VMEM_LIMIT = 62 << 20
BLK = 128
EPS = 1e-06
ROPE_BASE = 1000042.0
AXES = ("zh", "zl", "y", "x", "c")
TEAM = ("zl", "y")
SLOTS = ("y", "zl")
PAIRED_SLOTS = ("c", "y", "zl")
SHARES = ("c", "x", "zh")
OWNERS = ("zl", "y", "c")
ROWS_T = (((0,), (0,)), ((), ()))
PAIR_ROWS_T = (((0, 1), (0, 1)), ((), ()))
COLS_T = (((1,), (1,)), ((), ()))
F32 = jnp.float32
BF16 = jnp.bfloat16


def offsets(sizes, axes):
    return [dict(zip(axes, o)) for o in itertools.product(*(range(sizes[a]) for a in axes))]


def place(at, layout, sizes):
    index = 0
    for a in layout:
        index = index * sizes[a] + at[a]
    return index


class Gather:
    def __init__(self, x, layout, orders, rank=1):
        self.x, self.layout, self.orders, self.rank = x, layout, orders, rank

    def shape(self, sizes):
        return (math.prod(sizes[a] for a in self.layout),) + self.x.shape

    def cut(self, ref, part):
        rows = self.x.shape[0] // len(self.orders)
        return ref.at[pl.ds(part * rows, rows)]

    def spot(self, out, owner, off, part, sizes):
        return self.cut(out.at[place(owner, self.layout, sizes)], part)


class NearGather(Gather):
    def shape(self, sizes):
        return tuple(sizes[a] for a in self.layout) + self.x.shape

    def spot(self, out, owner, off, part, sizes):
        return self.cut(out.at[tuple(off[a] for a in self.layout)], part)


class RowGather(Gather):
    def shape(self, sizes):
        team, rows, columns = self.x.shape
        return (sizes["x"] * sizes["zh"] * team * sizes["c"] * rows, columns)

    def cut(self, ref, part):
        return ref.at[part]

    def spot(self, out, owner, off, part, sizes):
        team, rows, _ = self.x.shape
        block = (owner["zh"] * team + part) * sizes["x"] + owner["x"]
        start = pl.multiple_of((block * sizes["c"] + owner["c"]) * rows, rows)
        return out.at[pl.ds(start, rows)]


class Swap:
    def __init__(self, x, layout):
        self.x, self.layout = x, layout

    def shape(self, sizes):
        return self.x.shape

    def own_shape(self, sizes):
        return self.x.shape[1:]

    def offsets(self, sizes):
        return offsets(sizes, self.layout)

    def pair(self, x, out, here, to, off, sizes):
        return x.at[place(to, self.layout, sizes)], out.at[place(here, self.layout, sizes)]


class ColumnSwap:
    def __init__(self, x, block):
        self.x, self.block = x, block

    def shape(self, sizes):
        rows, columns = self.x.shape
        team = sizes["zl"] * sizes["y"]
        return (team, rows, columns // team)

    def own_shape(self, sizes):
        return self.shape(sizes)[1:]

    def offsets(self, sizes):
        return offsets(sizes, TEAM)

    def pieces(self, x, out, to, sizes):
        found = []
        for i, share in enumerate(offsets(sizes, SHARES)):
            start = pl.multiple_of(place({**share, **to}, AXES, sizes) * self.block, self.block)
            found.append(
                (x.at[:, pl.ds(start, self.block)], out.at[:, pl.ds(i * self.block, self.block)])
            )
        return found


class NearSwap(Swap):
    def pair(self, x, out, here, to, off, sizes):
        i = off[self.layout[0]]
        return x.at[i], out.at[i]


class Halves:
    def __init__(self, x):
        self.x = x

    def shape(self, sizes):
        rows, columns = self.x.shape
        return (2, rows, columns // 2)

    def own_shape(self, sizes):
        rows, columns = self.x.shape
        return (rows, columns // 2)

    def offsets(self, sizes):
        return offsets(sizes, ("c",))

    def pair(self, x, out, here, to, off, sizes):
        width = self.x.shape[1] // 2
        start = pl.multiple_of(to["c"] * width, width)
        return x.at[:, pl.ds(start, width)], out.at[off["c"]]


CHUNKS = 4
AHEAD = 10
EARLY = 0
FLOW = (2, 8, 6, 6)


class TeamSum:
    def __init__(self, x, y_first=2):
        self.x, self.y_first = x, y_first

    def shape(self, sizes):
        return (2,) + self.x.shape[2:]


class Net:
    def __init__(self, sizes):
        self.sizes, self.count, self.reached = sizes, 0, set()

    def wire(self, off):
        self.reached.add(tuple(off.get(a, 0) for a in AXES))
        self.count += 1
        return self.count - 1, off

    def open(self, send_sem, recv_sem):
        self.send_sem, self.recv_sem = send_sem, recv_sem
        self.here = {a: lax.axis_index(a) for a in AXES}
        self.sent = []
        barrier = pltpu.get_barrier_semaphore()
        for off in sorted(self.reached):
            pl.semaphore_signal(
                barrier,
                inc=1,
                device_id=self.device(self.moved(dict(zip(AXES, off)))),
                device_id_type=pl.DeviceIdType.MESH,
            )
        pl.semaphore_wait(barrier, len(self.reached))

    def moved(self, off):
        return {
            a: lax.rem(self.here[a] + off[a], self.sizes[a]) if off.get(a, 0) else self.here[a]
            for a in AXES
        }

    def device(self, at):
        return tuple(at[a] for a in AXES)

    def send(self, src, dst, wire):
        sem, off = wire
        cp = pltpu.make_async_remote_copy(
            src_ref=src,
            dst_ref=dst,
            send_sem=self.send_sem.at[sem],
            recv_sem=self.recv_sem.at[sem],
            device_id=self.device(self.moved(off)),
            device_id_type=pl.DeviceIdType.MESH,
        )
        cp.start()
        self.sent.append(cp)
        return cp

    def settle(self, cp):
        cp.wait_send()
        self.sent = [other for other in self.sent if other is not cp]

    def close(self):
        for cp in self.sent:
            cp.wait_send()


class Relay:
    def __init__(self, job, number, net):
        self.job, self.net, self.sizes = job, net, net.sizes
        self.steps = []
        for part, order in enumerate(job.orders):
            groups = [(axes,) if isinstance(axes, str) else axes for axes in order]
            for off in offsets(self.sizes, [a for axes in groups for a in axes]):
                used = [i for i, axes in enumerate(groups) if any(off[a] for a in axes)]
                sends = [
                    net.wire(to)
                    for axes in groups[used[-1] + 1 if used else 0 :]
                    for to in offsets(self.sizes, axes)
                    if any(to.values())
                ]
                hops = len(used)
                key = (job.rank, part + 2 * hops, hops, number, part)
                self.steps.append((key, self, hops, part, off, sends))

    def open(self, x, out):
        self.x, self.out, self.arrivals = x, out, {}

    def run(self, hops, part, off, sends):
        job, net = self.job, self.net
        owner = net.moved(off)
        if hops:
            self.arrivals[part, tuple(sorted(off.items()))].wait_recv()
            source = job.spot(self.out, owner, off, part, self.sizes)
        else:
            source = job.cut(self.x, part)
        for wire in sends:
            there = dict(off)
            for a, d in wire[1].items():
                there[a] = -d % self.sizes[a]
            dst = job.spot(self.out, owner, there, part, self.sizes)
            self.arrivals[part, tuple(sorted(there.items()))] = net.send(source, dst, wire)

    def own(self, part):
        return self.job.spot(self.out, self.net.here, {a: 0 for a in AXES}, part, self.sizes)


class Stream:
    def __init__(self, net, shape, owners):
        self.net, self.owners = net, owners
        self.nx, self.nz = net.sizes["x"], net.sizes["zh"]
        self.columns, self.dtype = shape[1], BF16
        self.rows = shape[0] // (self.nx * self.nz * CHUNKS)
        self.chunks = [(z, q) for z in [*range(1, self.nz), 0] for q in range(CHUNKS)]
        self.x_wires = [[net.wire({"x": d}) for d in range(1, self.nx)] for _ in self.chunks]
        self.z_wires = [net.wire({"zh": z}) if z else None for z, _ in self.chunks]
        if owners:
            self.members = offsets(net.sizes, TEAM)
            self.own_rows = self.rows // net.sizes["c"]
            self.cores = [
                [({**o, "c": c}, net.wire({**o, "c": c}) if c or any(o.values()) else None)
                 for c in range(net.sizes["c"])]
                for o in self.members
            ]

    def shape(self):
        rows = CHUNKS * self.rows
        if not self.owners:
            return jax.ShapeDtypeStruct((rows, self.columns), self.dtype)
        n = math.prod(self.net.sizes[a] for a in OWNERS)
        return jax.ShapeDtypeStruct((n, rows // n, self.columns), self.dtype)

    def scratch(self):
        n, chunk = len(self.chunks), (self.rows, self.columns)
        return [
            pltpu.VMEM((n, *chunk), self.dtype),
            pltpu.VMEM((self.nx - 1, n, *chunk), self.dtype),
            pltpu.VMEM((self.nz - 1, CHUNKS, *chunk), self.dtype),
            pltpu.SemaphoreType.DMA((n,)),
            pltpu.SemaphoreType.DMA((CHUNKS,)),
        ]

    def open(self, term, out, mine, from_x, from_z, load_sem, store_sem):
        self.term, self.out, self.mine = term, out, mine
        self.from_x, self.from_z = from_x, from_z
        self.load_sem, self.store_sem = load_sem, store_sem
        self.loads, self.x_sent, self.z_sent, self.stores, self.handed = {}, {}, {}, [], []

    def window(self, x, z, q):
        zh = self.net.moved({"zh": z})["zh"]
        if self.owners:
            q = place(self.net.moved(self.members[q]), TEAM, self.net.sizes)
            block = (zh * CHUNKS + q) * self.nx + x
        else:
            block = (x * self.nz + zh) * CHUNKS + q
        return self.term.at[pl.ds(pl.multiple_of(block * self.rows, self.rows), self.rows)]

    def issue(self, k):
        z, q = self.chunks[k]
        self.x_sent[k] = []
        for d, wire in enumerate(self.x_wires[k], 1):
            x = self.net.moved({"x": d})["x"]
            self.x_sent[k].append(
                self.net.send(self.window(x, z, q), self.from_x.at[d - 1, k], wire)
            )
        load = pltpu.make_async_copy(
            self.window(self.net.here["x"], z, q), self.mine.at[k], self.load_sem.at[k]
        )
        load.start()
        self.loads[k] = load

    def merge(self, k):
        z, q = self.chunks[k]
        self.loads[k].wait()
        for cp in self.x_sent[k]:
            cp.wait_recv()
        total = self.mine[k].astype(F32)
        for d in range(self.nx - 1):
            total += self.from_x[d, k].astype(F32)
        self.mine[k] = total.astype(self.dtype)
        if z:
            self.z_sent[z, q] = self.net.send(
                self.mine.at[k], self.from_z.at[z - 1, q], self.z_wires[k]
            )

    def last(self, q):
        k = self.chunks.index((0, q))
        total = self.mine[k].astype(F32)
        for z in range(1, self.nz):
            self.z_sent[z, q].wait_recv()
            total += self.from_z[z - 1, q].astype(F32)
        self.mine[k] = total.astype(self.dtype)
        if self.owners:
            mine = place(self.net.here, OWNERS, self.net.sizes)
            for off, wire in self.cores[q]:
                core = self.net.moved(off)["c"]
                start = pl.multiple_of(core * self.own_rows, self.own_rows)
                src = self.mine.at[k, pl.ds(start, self.own_rows)]
                if wire:
                    self.handed.append(self.net.send(src, self.out.at[mine], wire))
                else:
                    store = pltpu.make_async_copy(src, self.out.at[mine], self.store_sem.at[q])
                    store.start()
                    self.stores.append(store)
            return
        store = pltpu.make_async_copy(
            self.mine.at[k], self.out.at[pl.ds(q * self.rows, self.rows)], self.store_sem.at[q]
        )
        store.start()
        self.stores.append(store)

    def close(self):
        for cp in self.handed:
            cp.wait_recv()
        for store in self.stores:
            store.wait()


class Adder:
    def __init__(self, job, number, net):
        self.job, self.net = job, net
        rows = job.x.shape[2] // CHUNKS
        self.steps = []
        self.parts = []
        for part in range(CHUNKS):
            first, second = ("y", "zl") if part < job.y_first else ("zl", "y")
            wires = net.wire({first: 1}), net.wire({first: 1}), net.wire({second: 1})
            self.parts.append((pl.ds(part * rows, rows), first, second, wires))
            self.steps.append(((0, part, 0, number, part), self, 0, part, None, None))
            self.steps.append(((1, part + 2, 1, number, part), self, 1, part, None, None))

    def scratch(self):
        shape = self.job.x.shape[2:]
        return [pltpu.VMEM(shape, self.job.x.dtype)] * 2 + [pltpu.SemaphoreType.DMA((CHUNKS,))]

    def open(self, x, out, term, far, sem):
        self.x, self.out, self.term, self.far, self.sem = x, out, term, far, sem
        self.waits, self.direct, self.summed = {}, [], []

    def run(self, hops, part, *_):
        window, first, second, wires = self.parts[part]
        y_first = first == "y"
        if not hops:
            self.waits[part] = self.net.send(
                self.x.at[1, 1, window], self.far.at[window], wires[0]
            )
            near = self.x.at[1, 0, window] if y_first else self.x.at[0, 1, window]
            self.direct.append(
                self.net.send(near, self.out.at[0 if y_first else 1, window], wires[1])
            )
            mine = self.x.at[0, 1, window] if y_first else self.x.at[1, 0, window]
            load = pltpu.make_async_copy(mine, self.term.at[window], self.sem.at[part])
            load.start()
            self.waits[part] = self.waits[part], load
            return
        far, load = self.waits[part]
        load.wait()
        far.wait_recv()
        total = self.term[window].astype(F32) + self.far[window].astype(F32)
        self.term[window] = total.astype(self.term.dtype)
        self.summed.append(
            self.net.send(
                self.term.at[window], self.out.at[1 if y_first else 0, window], wires[2]
            )
        )

    def finish(self):
        for cp in self.direct + self.summed:
            cp.wait_recv()


def exchange(jobs, collective_id, micros=50):
    net = Net({a: lax.axis_size(a) for a in AXES})
    sizes = net.sizes
    count = len(jobs)
    steps, swaps, runners, scratch = [], [], [], []
    for number, job in enumerate(jobs):
        if isinstance(job, Gather):
            runner = Relay(job, number, net)
            steps += runner.steps
            stage = [pltpu.VMEM(job.x.shape, job.x.dtype)]
        elif isinstance(job, TeamSum):
            runner = Adder(job, number, net)
            steps += runner.steps
            stage = runner.scratch()
        else:
            runner = None
            n = math.prod(sizes[a] for a in SHARES) if isinstance(job, ColumnSwap) else 1
            for off in job.offsets(sizes):
                if any(off.values()):
                    swaps.append((number, off, [net.wire(off) for _ in range(n)]))
            stage = [pltpu.VMEM(job.own_shape(sizes), job.x.dtype)]
        runners.append((runner, len(scratch), len(scratch) + len(stage)))
        scratch += stage
    steps.sort(key=lambda s: s[0])

    def kernel(*refs):
        ins, outs, rest = refs[:count], refs[count : 2 * count], refs[2 * count :]
        send_sem, recv_sem, local_sem, piece_sem = rest[-4:]
        net.open(send_sem, recv_sem)
        loads, stores = [], []
        for number, job in enumerate(jobs):
            runner, lo, hi = runners[number]
            if isinstance(job, TeamSum):
                runner.open(ins[number], outs[number], *rest[lo:hi])
                continue
            (stage,) = rest[lo:hi]
            if runner:
                runner.open(ins[number], outs[number])
                src = ins[number]
                puts = [
                    (job.cut(stage, part), runner.own(part)) for part in range(len(job.orders))
                ]
            elif isinstance(job, ColumnSwap):
                mine = {a: net.here[a] for a in TEAM}
                for i, (src, dst) in enumerate(job.pieces(ins[number], stage, mine, sizes)):
                    load = pltpu.make_async_copy(src, dst, piece_sem.at[number, i])
                    load.start()
                    loads.append((load, number, []))
                loads[-1][2].append((stage, outs[number].at[place(net.here, TEAM, sizes)]))
                continue
            else:
                none = {a: 0 for a in AXES}
                src, dst = job.pair(ins[number], outs[number], net.here, net.here, none, sizes)
                puts = [(stage, dst)]
            load = pltpu.make_async_copy(src, stage, local_sem.at[number, 0])
            load.start()
            loads.append((load, number, puts))
        for _, runner, hops, *what in steps:
            if not hops:
                runner.run(hops, *what)
        received = []
        for number, off, wires in swaps:
            to = net.moved(off)
            job = jobs[number]
            if isinstance(job, ColumnSwap):
                mine = outs[number].at[place(net.here, TEAM, sizes)]
                pairs = job.pieces(ins[number], mine, {a: to[a] for a in TEAM}, sizes)
            else:
                pairs = [job.pair(ins[number], outs[number], net.here, to, off, sizes)]
            for (src, dst), wire in zip(pairs, wires, strict=True):
                received.append(net.send(src, dst, wire))
        for load, number, puts in loads:
            load.wait()
            for i, (src, dst) in enumerate(puts):
                store = pltpu.make_async_copy(src, dst, local_sem.at[number, 1 + i])
                store.start()
                stores.append(store)
        for _, runner, hops, *what in steps:
            if hops:
                runner.run(hops, *what)
        for cp in received:
            cp.wait_recv()
        for runner, _, _ in runners:
            if isinstance(runner, Adder):
                runner.finish()
        net.close()
        for store in stores:
            store.wait()

    return pl.pallas_call(
        kernel,
        out_shape=[jax.ShapeDtypeStruct(job.shape(sizes), job.x.dtype) for job in jobs],
        in_specs=[pl.BlockSpec(memory_space=pl.ANY)] * count,
        out_specs=[pl.BlockSpec(memory_space=pl.ANY)] * count,
        scratch_shapes=scratch
        + [
            pltpu.SemaphoreType.DMA((net.count,)),
            pltpu.SemaphoreType.DMA((net.count,)),
            pltpu.SemaphoreType.DMA((count, 1 + CHUNKS)),
            pltpu.SemaphoreType.DMA((count, math.prod(sizes[a] for a in SHARES))),
        ],
        cost_estimate=pl.CostEstimate(
            flops=0, bytes_accessed=micros * 3_000_000, transcendentals=0
        ),
        compiler_params=pltpu.CompilerParams(
            collective_id=collective_id, has_side_effects=True, vmem_limit_bytes=VMEM_LIMIT
        ),
    )(*[job.x for job in jobs])


def sum_over(term, axis, outer=1):
    size = lax.axis_size(axis)
    me = lax.axis_index(axis)
    columns = term.shape[1]
    term = term.reshape(outer, -1, columns)
    while size > 1:
        size //= 2
        rows = term.shape[1] // 2
        pairs = [(i, i ^ size) for i in range(lax.axis_size(axis))]
        side = (me // size) % 2
        kept = lax.dynamic_slice_in_dim(term, side * rows, rows, axis=1)
        other = lax.ppermute(
            lax.dynamic_slice_in_dim(term, (1 - side) * rows, rows, axis=1), axis, pairs
        )
        term = kept.astype(F32) + other.astype(F32)
        if size > 1:
            term = term.astype(BF16)
    return term.reshape(-1, columns)


def dot(a, b, dims=None):
    if dims is None:
        return jnp.dot(a, b, preferred_element_type=F32)
    return lax.dot_general(a, b, dims, preferred_element_type=F32)


def rotate(t, cos, sin):
    half = t.shape[-1] // 2
    front, back = t[..., :half], t[..., half:]
    return jnp.concatenate([front * cos - back * sin, back * cos + front * sin], axis=-1)


def rms_scale(values):
    return lax.rsqrt(jnp.mean(values * values, axis=-1, keepdims=True) + EPS)


def attention_front(
    norm, attn_part, out_part, gate_part, gd, q_pos, k_pos, cos, sin, scaling, collective_id
):
    net = Net({a: lax.axis_size(a) for a in AXES})
    sizes = net.sizes
    own, width = norm.shape
    n_slot, n_zh, _, n = k_pos.shape
    n_tok = n_slot * n
    columns = attn_part.shape[2]
    q_cols = columns - 2 * HEAD
    heads = q_cols // HEAD
    half = q_cols // 2
    team = attn_part.shape[0]
    norm_job = NearGather(norm, PAIRED_SLOTS, TO_TEAM)
    attn_job = RowGather(attn_part, None, [OUTWARD] * team)
    out_job = Gather(out_part, SHARES, [OUTWARD] * (out_part.shape[0] // 16), rank=2)
    gd_job = NearGather(gd, PAIRED_SLOTS, TO_TEAM)
    gate_job = RowGather(gate_part, None, [OUTWARD] * team)
    norms, attns, outs = (Relay(job, i, net) for i, job in enumerate((norm_job, attn_job, out_job)))
    gds, gates = (Relay(job, i, net) for i, job in enumerate((gd_job, gate_job)))
    first = sorted(norms.steps + attns.steps + outs.steps, key=lambda step: step[0])
    gd_steps = sorted(gds.steps, key=lambda step: step[0])
    gate_steps = sorted(gates.steps, key=lambda step: step[0])
    kv_wires = [[net.wire({"zh": z}) for z in range(1, n_zh)] for _ in range(n_slot)]
    half_wires = [net.wire({"c": 1}) for _ in range(n_slot)]
    y_rows, zl_rows = pl.ds(0, own // 2), pl.ds(own // 2, own // 2)
    far_wires = net.wire({"y": 1}), net.wire({"zl": 1})
    near_wires = net.wire({"y": 1}), net.wire({"zl": 1})
    n_local = 64
    out_shapes = [job.shape(sizes) for job in (norm_job, gd_job, attn_job, out_job, gate_job)]

    def kernel(
        norm_ref, attn_ref, outp_ref, gate_ref, gd_ref, q_pos_ref, k_pos_ref, cos_ref, sin_ref,
        norms_ref, gds_ref, w_attn_ref, w_out_ref, w_gate_ref, q_ref, kv_ref, lse_ref, half_ref,
        terms_ref,
        nv, wa, wo, q, kv, o, terms, far, gd_stage, gate_stage, send_sem, recv_sem, local_sem,
    ):
        net.open(send_sem, recv_sem)
        norms.open(norm_ref, norms_ref)
        attns.open(attn_ref, wa)
        outs.open(outp_ref, wo)
        gds.open(gd_ref, gds_ref)
        gates.open(gate_ref, w_gate_ref)
        used = iter(range(n_local))

        def local(src, dst):
            cp = pltpu.make_async_copy(src, dst, local_sem.at[next(used)])
            cp.start()
            return cp

        def start(steps):
            for _, runner, hops, *what in steps:
                if not hops:
                    runner.run(hops, *what)

        gate_first = [step for step in gate_steps if not step[2] and step[3] < EARLY]
        gate_rest = [step for step in gate_steps if not step[2] and step[3] >= EARLY]
        start(first)
        got_norm = local(norm_ref, nv.at[0, 0])
        got_attn = [local(attn_job.cut(attn_ref, p), attns.own(p)) for p in range(team)]
        got_attn += [
            local(out_job.cut(outp_ref, p), outs.own(p)) for p in range(len(out_job.orders))
        ]
        got_gd, got_gate = local(gd_ref, gd_stage), local(gate_ref, gate_stage)
        got_norm.wait()
        kept = [local(norm_job.cut(nv.at[0, 0], p), norms.own(p)) for p in range(CHUNKS)]
        got_gd.wait()
        kept += [local(gd_job.cut(gd_stage, p), gds.own(p)) for p in range(CHUNKS)]
        got_gate.wait()
        kept += [local(gate_job.cut(gate_stage, p), gates.own(p)) for p in range(team)]

        def turn(t, rows):
            h = HEAD // 2
            c, sn = cos_ref[rows], sin_ref[rows]
            front, back = t[:, :h], t[:, h:]
            return jnp.concatenate([front * c - back * sn, back * c + front * sn], axis=1).astype(
                BF16
            )

        def project(s):
            for j in range(n // own):
                rows = slice(s * n + j * own, s * n + (j + 1) * own)
                for g in range(heads):
                    cols = slice(g * HEAD, (g + 1) * HEAD)
                    q[rows, cols] = turn(dot(nv[s, j], wa[:, cols]), rows)
                kv[0, rows, :HEAD] = turn(dot(nv[s, j], wa[:, q_cols : q_cols + HEAD]), rows)
                kv[0, rows, HEAD:] = dot(nv[s, j], wa[:, q_cols + HEAD :]).astype(BF16)
            window = pl.ds(s * n, n)
            return [
                net.send(kv.at[0, window], kv.at[n_zh - z, window], kv_wires[s][z - 1])
                for z in range(1, n_zh)
            ]

        def attend(s, sent):
            for cp in sent:
                cp.wait_recv()
            rows = slice(s * n, (s + 1) * n)
            for g in range(heads):
                cols = slice(g * HEAD, (g + 1) * HEAD)
                scores = []
                for z in range(n_zh):
                    score = dot(q[rows, cols], kv[z, rows, :HEAD], COLS_T) * scaling
                    allowed = k_pos_ref[s, z] <= q_pos_ref[...]
                    scores.append(jnp.where(allowed, score, -jnp.inf))
                peak = scores[0].max(axis=1, keepdims=True)
                for score in scores[1:]:
                    peak = jnp.maximum(peak, score.max(axis=1, keepdims=True))
                exps = [jnp.exp(score - peak) for score in scores]
                total = sum(e.sum(axis=1, keepdims=True) for e in exps)
                inverse = 1.0 / total
                o[rows, cols] = sum(
                    dot((e * inverse).astype(BF16), kv[z, rows, HEAD:]) for z, e in enumerate(exps)
                ).astype(BF16)
                lse_ref[s, g] = peak + jnp.log(total)
            away = pl.ds(pl.multiple_of((1 - net.here["c"]) * half, half), half)
            here = pl.ds(pl.multiple_of(net.here["c"] * half, half), half)
            window = pl.ds(s * n, n)
            halves.append(net.send(o.at[window, away], half_ref.at[1, window], half_wires[s]))
            kept.append(local(o.at[window, here], half_ref.at[0, window]))

        def term(r):
            n_part = out_part.shape[0]

            def tile(t, _):
                at = pl.ds(pl.multiple_of(t * TILE, TILE), TILE)
                weight = wo[:, :, at].reshape(q_cols, TILE)
                terms[r, :, at] = dot(o[r * own : (r + 1) * own], weight).astype(BF16)
                return 0

            lax.fori_loop(0, width // TILE, tile, 0)

        def add(r, window):
            terms[r, window] = (terms[r, window].astype(F32) + far[window].astype(F32)).astype(BF16)

        halves, late = [], []

        def relay(steps, most=9):
            for _, runner, hops, part, off, sends in steps:
                if not hops:
                    continue
                if runner in (norms, gds) and off["c"]:
                    late.append((runner, hops, part, off, sends))
                    continue
                runner.run(hops, part, off, sends)
                if runner is attns and hops == 1 and off["zh"] and part == team - 1:
                    start(gate_first)
                    gate_first.clear()
                if runner is norms and part == CHUNKS - 1:
                    i, j = off["y"], off["zl"]
                    got[i, j] = local(norms_ref.at[0, i, j], nv.at[i, j])

        got = {}
        relay(first)
        for cp in got_attn:
            cp.wait()
        kept.append(local(wa, w_attn_ref))
        kept.append(local(wo, w_out_ref))
        start(gd_steps)
        got[0, 1].wait()
        sent = [project(0)]
        got[1, 0].wait()
        got[1, 1].wait()
        sent.append(project(1))
        start(gate_rest)
        relay([step for step in gd_steps if step[2] == 1])
        attend(0, sent[0])
        term(1)
        term(0)
        relay([step for step in gd_steps if step[2] > 1])
        attend(1, sent[1])
        term(3)
        to_far = (
            net.send(terms.at[3, y_rows], far.at[y_rows], far_wires[0]),
            net.send(terms.at[3, zl_rows], far.at[zl_rows], far_wires[1]),
        )
        term(2)
        kept.append(local(terms.at[0], terms_ref.at[0]))
        kept.append(local(q, q_ref))
        kept.append(local(kv, kv_ref))
        relay([step for step in gate_steps if step[2] == 1 and step[3] < 2])
        to_far[1].wait_recv()
        add(2, zl_rows)
        to_y = net.send(terms.at[2], terms_ref.at[1], near_wires[0])
        to_far[0].wait_recv()
        add(1, y_rows)
        to_zl = net.send(terms.at[1], terms_ref.at[2], near_wires[1])
        relay([step for step in gate_steps if not (step[2] == 1 and step[3] < 2)])
        for runner, *step in late:
            runner.run(*step)
        for cp in halves + [to_y, to_zl]:
            cp.wait_recv()
        net.close()
        for cp in kept:
            cp.wait()

    shape = jax.ShapeDtypeStruct
    vmem, hbm = pl.BlockSpec(memory_space=pltpu.VMEM), pl.BlockSpec(memory_space=pl.ANY)
    q_shape, kv_shape = (n_tok, q_cols), (n_zh, n_tok, 2 * HEAD)
    return pl.pallas_call(
        kernel,
        out_shape=[
            *[shape(dims, BF16) for dims in out_shapes],
            shape(q_shape, BF16),
            shape(kv_shape, BF16),
            shape((n_slot, heads, n, 1), F32),
            shape((2, n_tok, half), BF16),
            shape((3, own, width), BF16),
        ],
        in_specs=[hbm] * 5 + [vmem] * 4,
        out_specs=[hbm] * 7 + [vmem] + [hbm] * 2,
        scratch_shapes=[
            pltpu.VMEM((2, 2, own, width), BF16),
            pltpu.VMEM(out_shapes[2], BF16),
            pltpu.VMEM(out_shapes[3], BF16),
            pltpu.VMEM(q_shape, BF16),
            pltpu.VMEM(kv_shape, BF16),
            pltpu.VMEM(q_shape, BF16),
            pltpu.VMEM((4, own, width), BF16),
            pltpu.VMEM((own, width), BF16),
            pltpu.VMEM(gd.shape, BF16),
            pltpu.VMEM(gate_part.shape, BF16),
            pltpu.SemaphoreType.DMA((net.count,)),
            pltpu.SemaphoreType.DMA((net.count,)),
            pltpu.SemaphoreType.DMA((n_local,)),
        ],
        cost_estimate=pl.CostEstimate(
            flops=0, bytes_accessed=160 * 3_000_000, transcendentals=0
        ),
        compiler_params=pltpu.CompilerParams(
            collective_id=collective_id, has_side_effects=True, vmem_limit_bytes=FFN_VMEM_LIMIT
        ),
    )(norm, attn_part, out_part, gate_part, gd, q_pos, k_pos, cos, sin)


def attention_back(
    ga, q, kv, lse, q_pos, k_pos, cos, sin, w_out, w_attn, out_parts, sums, scaling, collective_id
):
    net = Net({a: lax.axis_size(a) for a in AXES})
    own, width = ga.shape
    n_slot, n_zh, _, n = k_pos.shape
    n_tok = n_slot * n
    heads = q.shape[1] // HEAD
    columns = w_attn.shape[1]
    half = columns // 2
    ga_job = NearGather(ga, PAIRED_SLOTS, TO_TEAM_EVEN)
    gas = Relay(ga_job, 0, net)
    ga_steps = sorted(gas.steps, key=lambda step: step[0])
    adder = Adder(TeamSum(out_parts, CHUNKS), 1, net)
    streams, made = [], []
    if sums:
        down, _, gate_half, _, o_half, _ = sums
        made = [(width, gate_half.shape[2])] * 2 + [(o_half.shape[2], width), (width, half)]
        streams = [Stream(net, down.shape, False)]
        streams += [Stream(net, dims, i != 2) for i, dims in enumerate(made)]
    n_chunks = n_zh * CHUNKS
    kv_wires = [[net.wire({"zh": z}) for z in range(1, n_zh)] for _ in range(n_slot)]
    half_wires = [net.wire({"c": 1}) for _ in range(n_slot)]
    y_rows, zl_rows = pl.ds(0, own // 2), pl.ds(own // 2, own // 2)
    far_wires = net.wire({"y": 1}), net.wire({"zl": 1})
    near_wires = net.wire({"y": 1}), net.wire({"zl": 1})
    n_sums = len(sums) if sums else 0
    n_local = 48

    def kernel(*refs):
        refs = iter(refs)

        def take(count):
            return list(itertools.islice(refs, count))

        ga_ref, q_ref, kv_ref, lse_ref, q_pos_ref, k_pos_ref = take(6)
        cos_ref, sin_ref, wo_ref, wa_ref, parts_ref = take(5)
        sum_ins = take(n_sums)
        gas_ref, half_ref, gn1_ref, added_ref = take(4)
        sum_outs, made_refs = take(len(streams)), take(len(made))
        gav, wo, wa, go, gkv, gkv_away, gkv_out, gkv_in, g_qkv, gn1, far = take(11)
        send_sem, recv_sem, local_sem = take(3)
        adder_scratch = take(3)
        net.open(send_sem, recv_sem)
        gas.open(ga_ref, gas_ref)
        adder.open(parts_ref, added_ref, *adder_scratch)
        for i, stream in enumerate(streams):
            stream.open([*sum_ins[:1], *made_refs][i], sum_outs[i], *take(5))
        used = iter(range(n_local))

        def local(src, dst):
            cp = pltpu.make_async_copy(src, dst, local_sem.at[next(used)])
            cp.start()
            return cp

        plan = []
        for i in range(len(streams)):
            for k in range(n_chunks):
                plan.append((i, k, False))
                q_chunk = k - (n_chunks - CHUNKS)
                if i and q_chunk >= 0:
                    plan.append((i - 1, q_chunk, True))
        plan += [(i, q_chunk, True) for i in range(len(streams))[-1:] for q_chunk in range(CHUNKS)]
        issued, merged = [0] * len(streams), [0] * len(streams)
        ready = [i == 0 for i in range(len(streams))]

        def pump():
            for i, stream in enumerate(streams):
                while ready[i] and issued[i] < n_chunks and sum(issued) < sum(merged) + AHEAD:
                    stream.issue(issued[i])
                    issued[i] += 1
                if issued[i] < n_chunks:
                    return

        def there(i):
            if sums:
                ready[i] = True
                pump()

        def flow(steps):
            while plan and steps:
                i, k, last = plan[0]
                if last:
                    streams[i].last(k)
                elif k < issued[i]:
                    streams[i].merge(k)
                    merged[i] += 1
                    pump()
                else:
                    return
                plan.pop(0)
                steps -= 1

        if sums:
            wr, lt, ot, o_v, wr_sem, lt_sem, ot_sem = take(7)

        def product(lhs_ref, rhs_ref, term_ref, steps):
            n_cols = wr.shape[2]
            n_tiles = width // own

            def lhs(t, slot, c):
                at = pl.ds(pl.multiple_of(t * own, own), own)
                return pltpu.make_async_copy(
                    lhs_ref.at[c, :, at], lt.at[slot, c], lt_sem.at[slot, c]
                )

            for part in range(rhs_ref.shape[2] // n_cols):
                window = pl.ds(part * n_cols, n_cols)
                rhs = [
                    pltpu.make_async_copy(rhs_ref.at[c, :, window], wr.at[c], wr_sem.at[c])
                    for c in range(2)
                ]
                for c in range(2):
                    rhs[c].start()
                    lhs(0, 0, c).start()
                for c in range(2):
                    rhs[c].wait()

                def store(t, slot, window=window):
                    at = pl.ds(pl.multiple_of(t * own, own), own)
                    return pltpu.make_async_copy(
                        ot.at[slot], term_ref.at[at, window], ot_sem.at[slot]
                    )

                def tile(t, _, store=store):
                    slot = lax.rem(t, 2)

                    @pl.when(t + 1 < n_tiles)
                    def _():
                        for c in range(2):
                            lhs(t + 1, 1 - slot, c).start()

                    for c in range(2):
                        lhs(t, slot, c).wait()

                    @pl.when(t >= 2)
                    def _():
                        store(t - 2, slot).wait()

                    value = dot(lt[slot].reshape(2 * n_tok, own), wr[...].reshape(2 * n_tok, n_cols), ROWS_T)
                    ot[slot] = value.astype(BF16)
                    store(t, slot).start()
                    return 0

                lax.fori_loop(0, n_tiles, tile, 0)
                store(n_tiles - 2, n_tiles % 2).wait()
                store(n_tiles - 1, 1 - n_tiles % 2).wait()
                flow(steps)

        for _, _, hops, *what in ga_steps:
            if not hops:
                gas.run(hops, *what)
        if sums:
            pump()
            got_o = local(sum_ins[4], o_v)
        got_wo, got_wa = local(wo_ref, wo), local(wa_ref, wa)
        got_ga = local(ga_ref, gav.at[0, 0])
        got_ga.wait()
        kept = [local(ga_job.cut(gav.at[0, 0], p), gas.own(p)) for p in range(CHUNKS)]
        got_wo.wait()
        got_wa.wait()
        if sums:
            product(sum_ins[1], sum_ins[2], made_refs[0], 1)
            there(1)

        def turn_back(t, rows):
            h = HEAD // 2
            c, sn = cos_ref[rows], sin_ref[rows]
            front, back = t[:, :h], t[:, h:]
            return jnp.concatenate([front * c + back * sn, back * c - front * sn], axis=1).astype(
                BF16
            )

        def slot(s):
            keys = slice(s * n, (s + 1) * n)
            for j in range(2):
                at = pl.ds(s * n + j * own, own)
                go[at, :] = dot(gav[s, j], wo[...], COLS_T).astype(BF16)
            for turn, (g, j) in enumerate(itertools.product(range(heads), range(n // own))):
                rows = slice(s * n + j * own, s * n + (j + 1) * own)
                here = slice(j * own, (j + 1) * own)
                cols = slice(g * HEAD, (g + 1) * HEAD)
                q_g, go_g, lse_g = q_ref[rows, cols], go[rows, cols], lse_ref[s, g, here]
                probs, gps = [], []
                for z in range(n_zh):
                    score = dot(q_g, kv_ref[z, keys, :HEAD], COLS_T) * scaling
                    allowed = k_pos_ref[s, z] <= q_pos_ref[here]
                    probs.append(jnp.where(allowed, jnp.exp(score - lse_g), 0.0))
                    gps.append(dot(go_g, kv_ref[z, keys, HEAD:], COLS_T))
                delta = sum((p * gp).sum(axis=1, keepdims=True) for p, gp in zip(probs, gps))
                gq = 0.0
                for z in range(n_zh):
                    gs = (probs[z] * (gps[z] - delta)).astype(BF16)
                    gq += dot(gs, kv_ref[z, keys, :HEAD])
                    gk = dot(gs, q_g, ROWS_T) * scaling
                    gv = dot(probs[z].astype(BF16), go_g, ROWS_T)
                    total = gkv_away.at[z - 1] if z else gkv.at[s]
                    if turn:
                        gk, gv = gk + total[:, :HEAD], gv + total[:, HEAD:]
                    total[:, :HEAD] = gk
                    total[:, HEAD:] = gv
                g_qkv[rows, cols] = turn_back(gq * scaling, rows)
            sent = []
            for z in range(n_zh - 1):
                gkv_out[s, z] = gkv_away[z].astype(BF16)
                sent.append(net.send(gkv_out.at[s, z], gkv_in.at[s, z], kv_wires[s][z]))
            return sent

        def keys(s, sent):
            rows = slice(s * n, (s + 1) * n)
            q_cols = heads * HEAD
            mine = gkv[s]
            for z, cp in enumerate(sent):
                cp.wait_recv()
                mine = mine + gkv_in[s, z].astype(F32)
            g_qkv[rows, q_cols : q_cols + HEAD] = turn_back(mine[:, :HEAD], rows)
            g_qkv[rows, q_cols + HEAD :] = mine[:, HEAD:].astype(BF16)
            away = pl.ds(pl.multiple_of((1 - net.here["c"]) * half, half), half)
            here = pl.ds(pl.multiple_of(net.here["c"] * half, half), half)
            window = pl.ds(s * n, n)
            halves.append(
                net.send(g_qkv.at[window, away], half_ref.at[1, window], half_wires[s])
            )
            kept.append(local(g_qkv.at[window, here], half_ref.at[0, window]))

        def term(r):
            def tile(t, _):
                at = pl.ds(pl.multiple_of(t * TILE, TILE), TILE)
                value = dot(g_qkv[r * own : (r + 1) * own], wa[at, :], COLS_T)
                gn1[r, :, at] = value.astype(BF16)
                return 0

            lax.fori_loop(0, width // TILE, tile, 0)

        def add(r, window):
            gn1[r, window] = (gn1[r, window].astype(F32) + far[window].astype(F32)).astype(BF16)

        def add_out(hops):
            for _, _, at, *what in sorted(adder.steps, key=lambda step: step[0]):
                if at == hops:
                    adder.run(at, *what)

        def relay_late():
            for hops, part, off, sends in late:
                gas.run(hops, part, off, sends)

        halves, late, arrived, sent = [], [], set(), {}
        for _, _, hops, part, off, sends in ga_steps:
            if not hops:
                continue
            if off["c"]:
                late.append((hops, part, off, sends))
                continue
            gas.run(hops, part, off, sends)
            if part == CHUNKS - 1:
                i, j = off["y"], off["zl"]
                local(gas_ref.at[0, i, j], gav.at[i, j]).wait()
                arrived.add((i, j))
                if arrived >= {(0, 1), (1, 0)} and 0 not in sent:
                    flow(2)
                    sent[0] = slot(0)
                    flow(1)
        flow(1)
        sent[1] = slot(1)
        add_out(0)
        flow(2)
        if sums:
            product(sum_ins[1], sum_ins[3], made_refs[1], 2)
            there(2)
            relay_late()
            got_o.wait()
            others = [
                local(gas_ref.at[1, i, j], gn1.at[2 * i + j]) for i in range(2) for j in range(2)
            ]
            for cp in others:
                cp.wait()

            def output(t, _):
                at = pl.ds(pl.multiple_of(t * TILE, TILE), TILE)
                value = dot(o_v[0], gav[:, :, :, at].reshape(n_tok, TILE), ROWS_T)
                value += dot(o_v[1], gn1[:, :, at].reshape(n_tok, TILE), ROWS_T)
                block = pl.ds(pl.multiple_of(t * o_v.shape[2], o_v.shape[2]), o_v.shape[2])
                wr[0, block] = value.astype(BF16)
                return 0

            lax.fori_loop(0, width // TILE, output, 0)
            n_rows = o_v.shape[2]
            kept_out = [
                local(
                    wr.at[0, pl.ds(t * n_rows, n_rows)], made_refs[2].at[:, pl.ds(t * TILE, TILE)]
                )
                for t in range(width // TILE)
            ]
            for cp in kept_out:
                cp.wait()
            there(3)
            flow(FLOW[0])
        else:
            relay_late()
        keys(0, sent[0])
        term(1)
        term(0)
        add_out(1)
        flow(FLOW[1])
        keys(1, sent[1])
        term(3)
        to_far = (
            net.send(gn1.at[3, y_rows], far.at[y_rows], far_wires[0]),
            net.send(gn1.at[3, zl_rows], far.at[zl_rows], far_wires[1]),
        )
        term(2)
        kept.append(local(gn1.at[0], gn1_ref.at[0]))
        flow(FLOW[2])
        to_far[1].wait_recv()
        add(2, zl_rows)
        to_y = net.send(gn1.at[2], gn1_ref.at[1], near_wires[0])
        to_far[0].wait_recv()
        add(1, y_rows)
        to_zl = net.send(gn1.at[1], gn1_ref.at[2], near_wires[1])
        for cp in halves:
            cp.wait_recv()
        for cp in kept:
            cp.wait()
        if sums:
            flow(FLOW[3])
            product(sum_ins[5], half_ref, made_refs[3], 1)
            there(4)
        flow(100)
        assert not plan
        for cp in (to_y, to_zl):
            cp.wait_recv()
        adder.finish()
        net.close()
        for stream in streams:
            stream.close()

    shape = jax.ShapeDtypeStruct
    vmem, hbm = pl.BlockSpec(memory_space=pltpu.VMEM), pl.BlockSpec(memory_space=pl.ANY)
    scratch = [
        pltpu.VMEM((2, 2, own, width), BF16),
        pltpu.VMEM(w_out.shape, BF16),
        pltpu.VMEM(w_attn.shape, BF16),
        pltpu.VMEM((n_tok, heads * HEAD), BF16),
        pltpu.VMEM((n_slot, n, 2 * HEAD), F32),
        pltpu.VMEM((n_zh - 1, n, 2 * HEAD), F32),
        pltpu.VMEM((n_slot, n_zh - 1, n, 2 * HEAD), BF16),
        pltpu.VMEM((n_slot, n_zh - 1, n, 2 * HEAD), BF16),
        pltpu.VMEM((n_tok, columns), BF16),
        pltpu.VMEM((4, own, width), BF16),
        pltpu.VMEM((own, width), BF16),
        pltpu.SemaphoreType.DMA((net.count,)),
        pltpu.SemaphoreType.DMA((net.count,)),
        pltpu.SemaphoreType.DMA((n_local,)),
        *adder.scratch(),
    ]
    for stream in streams:
        scratch += stream.scratch()
    if sums:
        scratch += [
            pltpu.VMEM((2, n_tok, TILE), BF16),
            pltpu.VMEM((2, 2, n_tok, own), BF16),
            pltpu.VMEM((2, own, TILE), BF16),
            pltpu.VMEM(o_half.shape, BF16),
            pltpu.SemaphoreType.DMA((2,)),
            pltpu.SemaphoreType.DMA((2, 2)),
            pltpu.SemaphoreType.DMA((2,)),
        ]
    return pl.pallas_call(
        kernel,
        out_shape=[
            shape((2, 2, 2, own, width), BF16),
            shape((2, n_tok, half), BF16),
            shape((3, own, width), BF16),
            shape((2, own, width), BF16),
            *[stream.shape() for stream in streams],
            *[shape(dims, BF16) for dims in made],
        ],
        in_specs=[hbm] + [vmem] * 7 + [hbm] * (3 + n_sums),
        out_specs=[hbm] * (4 + len(streams) + len(made)),
        scratch_shapes=scratch,
        compiler_params=pltpu.CompilerParams(
            collective_id=collective_id, has_side_effects=True, vmem_limit_bytes=FFN_VMEM_LIMIT
        ),
    )(ga, q, kv, lse, q_pos, k_pos, cos, sin, w_out, w_attn, out_parts, *(sums or ()))


def positions(members):
    total = lax.axis_size("zh") * lax.axis_size("zl")
    half = jnp.arange(2)[None, :, None]
    row = jnp.arange(BLK)[None, None, :]
    j = members[:, None, None]
    return (jnp.where(half == 0, j, 2 * total - 1 - j) * BLK + row).reshape(-1)


OUTWARD = ("zh", "x", "c")
TILE = 512
TO_TEAM = [("zl", "y", "c")] * CHUNKS
TO_TEAM_EVEN = [("zl", "y", "c"), ("y", "zl", "c")] * (CHUNKS // 2)


def feed_forward(norm, gd, w_gate, w_down, up_part, collective_id):
    net = Net({a: lax.axis_size(a) for a in AXES})
    sizes = net.sizes
    own, width = norm.shape
    ff = w_gate.shape[1]
    half = ff // 2
    norm_job = NearGather(norm, PAIRED_SLOTS, TO_TEAM_EVEN)
    up_job = RowGather(up_part, None, [OUTWARD] * up_part.shape[0])
    norms, ups = Relay(norm_job, 0, net), Relay(up_job, 1, net)
    steps = sorted(norms.steps + ups.steps, key=lambda s: s[0])
    y_rows, zl_rows = pl.ds(0, own // 2), pl.ds(own // 2, own // 2)
    far_wires = net.wire({"y": 1}), net.wire({"zl": 1})
    near_wires = net.wire({"y": 1}), net.wire({"zl": 1})
    half_wires = [[net.wire({"c": 1}) for _ in range(3)] for _ in range(4)]
    n_local = 64

    def kernel(
        norm_ref, gd_ref, w_gate_ref, w_down_ref, up_ref,
        norms_ref, gate_half, up_half, mixed_half, gn2_ref, out_ref,
        wg, wu, wd, nv, gdv, gate, gm, gg, gu, mx, far, send_sem, recv_sem, local_sem,
    ):
        net.open(send_sem, recv_sem)
        norms.open(norm_ref, norms_ref)
        ups.open(up_ref, wu)
        used = iter(range(n_local))

        def local(src, dst):
            cp = pltpu.make_async_copy(src, dst, local_sem.at[next(used)])
            cp.start()
            return cp

        got_norm = local(norm_ref, nv.at[0])
        for _, runner, hops, *what in steps:
            if not hops:
                runner.run(hops, *what)
        got_gate = local(w_gate_ref, wg)
        got_gd = [local(gd_ref.at[0, 0, 0], gdv.at[0]), local(gd_ref.at[0, 1, 0], gdv.at[1])]
        got_down = local(w_down_ref, wd)
        got_up = [local(ups.job.cut(up_ref, p), ups.own(p)) for p in range(len(up_job.orders))]
        got_norm.wait()
        kept_norm = [local(norm_job.cut(nv.at[0], p), norms.own(p)) for p in range(CHUNKS)]

        def tiles(n, body):
            def step(t, _):
                body(pl.ds(pl.multiple_of(t * TILE, TILE), TILE))
                return 0

            lax.fori_loop(0, n // TILE, step, 0)

        gd_turn = [(0, 0), (1, 0), (0, 1), (1, 1)]

        def begin(turn):
            i, j = gd_turn[turn]
            r = 2 * i + j

            def one(t):
                gate[r, :, t] = dot(nv[r], wg[:, t])

            tiles(ff, one)
            got_gd[turn].wait()

            def two(t):
                gm[r, :, t] = dot(gdv[turn % 2], wd[t, :], COLS_T)

            tiles(ff, two)
            if turn + 2 < 4:
                got_gd.append(local(gd_ref.at[(0, *gd_turn[turn + 2])], gdv.at[turn % 2]))

        got_gate.wait()
        got_down.wait()
        begin(0)
        late = []
        arrived = {(1, 0): 0, (0, 1): 0, (1, 1): 0}
        turn = 1
        for _, runner, hops, part, off, sends in steps:
            if not hops:
                continue
            if runner is norms and off["c"]:
                late.append((hops, part, off, sends))
                continue
            runner.run(hops, part, off, sends)
            if runner is norms:
                arrived[off["y"], off["zl"]] += 1
                while turn < 4 and arrived[gd_turn[turn]] == CHUNKS:
                    i, j = gd_turn[turn]
                    local(norms_ref.at[0, i, j], nv.at[2 * i + j]).wait()
                    begin(turn)
                    turn += 1
        for cp in got_up + kept_norm:
            cp.wait()

        halves, busy = [], {}

        def finish(r, buf):
            for cp, remote in busy.pop(buf, []):
                net.settle(cp) if remote else cp.wait()

            def one(t):
                up = dot(nv[r], wu[:, t])
                g, m = gate[r, :, t], gm[r, :, t]
                s = 1.0 / (1.0 + jnp.exp(-g))
                gs = g * s
                mx[r, :, t] = (gs * up).astype(BF16)
                gg[buf, :, t] = (m * up * s * (1.0 + g * (1.0 - s))).astype(BF16)
                gu[buf, :, t] = (m * gs).astype(BF16)

            tiles(ff, one)
            mine = pl.ds(pl.multiple_of(net.here["c"] * half, half), half)
            other = pl.ds(pl.multiple_of((1 - net.here["c"]) * half, half), half)
            rows = pl.ds(r * own, own)
            for n, (ref, out) in enumerate(
                ((gg.at[buf], gate_half), (gu.at[buf], up_half), (mx.at[r], mixed_half))
            ):
                cp = local(ref.at[:, mine], out.at[0, rows])
                sent = net.send(ref.at[:, other], out.at[1, rows], half_wires[r][n])
                halves.append(sent)
                busy.setdefault(buf if n < 2 else "mixed", []).extend([(cp, False), (sent, True)])

            def two(t):
                term = dot(gg[buf], wg[t, :], COLS_T) + dot(gu[buf], wu[t, :], COLS_T)
                nv[r, :, t] = term.astype(BF16)

            tiles(width, two)

        def add(r, window):
            nv[r, window] = (nv[r, window].astype(F32) + far[window].astype(F32)).astype(BF16)

        finish(3, 0)
        to_far = (
            net.send(nv.at[3, y_rows], far.at[y_rows], far_wires[0]),
            net.send(nv.at[3, zl_rows], far.at[zl_rows], far_wires[1]),
        )
        finish(2, 1)
        to_far[1].wait_recv()
        add(2, zl_rows)
        to_y = net.send(nv.at[2], gn2_ref.at[1], near_wires[0])
        finish(1, 0)
        to_far[0].wait_recv()
        add(1, y_rows)
        to_zl = net.send(nv.at[1], gn2_ref.at[2], near_wires[1])
        finish(0, 1)
        stored = [local(nv.at[0], gn2_ref.at[0])]
        for n, r in enumerate((3, 2, 1, 0)):
            buf = n % 2
            for cp, remote in busy.pop(buf, []):
                net.settle(cp) if remote else cp.wait()

            def down(t):
                gg[buf, :, t] = dot(mx[r], wd[:, t]).astype(BF16)

            tiles(width, down)
            busy[buf] = [(local(gg.at[buf], out_ref.at[r // 2, r % 2]), False)]
        for hops, part, off, sends in late:
            norms.run(hops, part, off, sends)
        to_y.wait_recv()
        to_zl.wait_recv()
        for cp in halves:
            cp.wait_recv()
        net.close()
        for cps in busy.values():
            for cp, remote in cps:
                if not remote:
                    cp.wait()
        for cp in stored:
            cp.wait()

    shape = jax.ShapeDtypeStruct
    weight = pltpu.VMEM((width, ff), BF16)
    return pl.pallas_call(
        kernel,
        out_shape=[
            shape((2, 2, 2, own, width), BF16),
            *[shape((2, 4 * own, half), BF16)] * 3,
            shape((3, own, width), BF16),
            shape((2, 2, own, width), BF16),
        ],
        in_specs=[pl.BlockSpec(memory_space=pl.ANY)] * 5,
        out_specs=[pl.BlockSpec(memory_space=pl.ANY)] * 6,
        scratch_shapes=[
            weight,
            weight,
            pltpu.VMEM((ff, width), BF16),
            pltpu.VMEM((4, own, width), BF16),
            pltpu.VMEM((2, own, width), BF16),
            pltpu.VMEM((4, own, ff), F32),
            pltpu.VMEM((4, own, ff), F32),
            pltpu.VMEM((2, own, ff), BF16),
            pltpu.VMEM((2, own, ff), BF16),
            pltpu.VMEM((4, own, ff), BF16),
            pltpu.VMEM((own, width), BF16),
            pltpu.SemaphoreType.DMA((net.count,)),
            pltpu.SemaphoreType.DMA((net.count,)),
            pltpu.SemaphoreType.DMA((n_local,)),
        ],
        cost_estimate=pl.CostEstimate(
            flops=0, bytes_accessed=130 * 3_000_000, transcendentals=0
        ),
        compiler_params=pltpu.CompilerParams(
            collective_id=collective_id, has_side_effects=True, vmem_limit_bytes=FFN_VMEM_LIMIT
        ),
    )(norm, gd, w_gate, w_down, up_part)


def on_device(
    inputs,
    lengths,
    attn_gain,
    query_weight,
    key_matrix,
    value_matrix,
    output_weight,
    ffn_gain,
    gate_weight,
    up_weight,
    down_weight,
    cotangent,
):
    size = {a: lax.axis_size(a) for a in AXES}
    at = {a: lax.axis_index(a) for a in AXES}
    width = inputs.shape[3]
    own = inputs.shape[1] * inputs.shape[2]
    rows = query_weight.shape[0]
    n_dev = width // rows
    team = size["y"] * size["zl"]
    q_cols = query_weight.shape[1] // team
    kv_cols = key_matrix.shape[1] // team
    ff_rows = down_weight.shape[0]
    ff = gate_weight.shape[1] // team
    heads = q_cols // HEAD
    n_tok = team * own
    scaling = HEAD**-0.5

    def by_team(w):
        return w.reshape(rows, team, -1).transpose(1, 0, 2)

    def ff_cut(w):
        if ff_rows % 128 == 0:
            return ColumnSwap(w, ff_rows)
        cut = w.reshape(rows, *(size[a] for a in AXES), ff_rows)
        return Swap(cut.transpose(2, 3, 0, 5, 4, 1, 6).reshape(team, rows, ff), TEAM)

    attn_cut = jnp.concatenate(
        [by_team(query_weight), by_team(key_matrix), by_team(value_matrix)], axis=2
    )
    row = [jnp.pad(gain.astype(F32), (0, 64 - rows)) for gain in (attn_gain, ffn_gain)]
    tile = jnp.concatenate(
        [jnp.concatenate(row)[None], jnp.full((7, 128), lengths[0].astype(F32))]
    )
    tiles, attn_part, gate_part, up_part = exchange(
        [
            Gather(tile, AXES, [(("c", "x", "y"), ("zl", "zh"))], rank=0),
            Swap(attn_cut, TEAM),
            ff_cut(gate_weight),
            ff_cut(up_weight),
        ],
        1,
    )
    w_down = lax.all_gather(down_weight, SHARES, axis=0, tiled=True)
    gain_one = tiles[:, 0, :rows].reshape(1, width)
    gain_two = tiles[:, 0, 64 : 64 + rows].reshape(1, width)
    slots = tiles[: n_dev // (size["zh"] * size["zl"]), 1, 0].reshape(
        size["y"], size["x"], size["c"]
    )
    lens = slots[at["y"] ^ jnp.arange(2), at["x"], at["c"]].astype(jnp.int32)

    per_head = n_dev // team

    def head_home(i):
        f, t = i // per_head, i % per_head
        zl, y = f // size["y"], f % size["y"]
        zh, t = t % size["zh"], t // size["zh"]
        x, c = t % size["x"], t // size["x"]
        return (((zh * size["zl"] + zl) * size["y"] + y) * size["x"] + x) * size["c"] + c

    homes = [(i, head_home(i)) for i in range(n_dev)]
    out_part = lax.ppermute(output_weight, AXES, homes)

    def row_gather(part):
        return RowGather(part, None, [OUTWARD] * team)

    my_pos = positions((at["zh"] * size["zl"] + at["zl"])[None])
    valid = (my_pos < lengths[0]).astype(F32)[:, None]
    near_zl = at["zl"] ^ jnp.arange(2)
    near_zh = (at["zh"] + jnp.arange(size["zh"])) % size["zh"]
    q_pos = positions(at["zh"] * 2 + near_zl)
    n_q = q_pos.shape[0]
    k_pos = positions((near_zh[:, None] * 2 + near_zl[None, :]).reshape(-1))
    past = size["zh"] * n_q
    k_pos = jnp.where(k_pos[None] < lens[:, None], k_pos[None], past)
    k_pos = k_pos.reshape(2, size["zh"], 1, n_q)
    half = HEAD // 2
    freq = ROPE_BASE ** (-2.0 * jnp.arange(half).astype(F32) / HEAD)
    angles = q_pos.astype(F32)[:, None] * freq[None, :]
    q_pos = q_pos[:, None]
    cos = jnp.tile(jnp.cos(angles), (size["y"], 1))
    sin = jnp.tile(jnp.sin(angles), (size["y"], 1))

    tokens = inputs.reshape(own, width).astype(F32)
    scale_one = rms_scale(tokens)
    norm_one = (tokens * scale_one * gain_one).astype(BF16)
    gy = valid * cotangent.reshape(own, width).astype(F32)
    (
        norm_one_pair, gd_pair, w_attn, w_out, w_gate, q, kv_all, lse, o_half, o_terms
    ) = attention_front(
        norm_one, attn_part, out_part, gate_part, gy.astype(BF16), q_pos, k_pos, cos, sin,
        scaling, 2,
    )
    norm_one_pair = norm_one_pair.reshape(2, n_tok, width)
    w_out = w_out.reshape(q_cols, width)

    def added(term, others):
        return term.astype(F32) + others[0].astype(F32) + others[1].astype(F32)

    h1 = tokens + added(o_terms[0], o_terms[1:])
    scale_two = rms_scale(h1)
    norm_two = (h1 * scale_two * gain_two).astype(BF16)
    norm_two_pair, gate_half, up_half, mixed_half, gn2_terms, out_parts = feed_forward(
        norm_two, gd_pair, w_gate, w_down, up_part, 5
    )
    norm_two_pair = norm_two_pair.reshape(2, n_tok, width)
    gd_pair = gd_pair.reshape(2, n_tok, width)
    gn2 = added(gn2_terms[0], gn2_terms[1:]) * gain_two
    gh1 = gy + scale_two * gn2 - h1 * scale_two**3 * jnp.mean(h1 * gn2, axis=-1, keepdims=True)

    down_term = dot(mixed_half, gd_pair, PAIR_ROWS_T).astype(BF16)
    pairs = size["x"] == size["zh"] == 2
    sums = (down_term, norm_two_pair, gate_half, up_half, o_half, norm_one_pair) if pairs else None
    ga_pair, g_qkv_half, gn1_terms, out_added, *totals = attention_back(
        gh1.astype(BF16), q, kv_all, lse, q_pos, k_pos, cos, sin, w_out, w_attn, out_parts, sums,
        scaling, 8,
    )
    outputs = valid * (h1 + added(out_parts[0, 0], out_added))
    outputs = outputs.astype(BF16).reshape(inputs.shape)
    n_owners = math.prod(size[a] for a in OWNERS)

    def by_owner(total):
        return Swap(total.astype(BF16).reshape(n_owners, rows, -1), OWNERS)

    homeward = [(b, a) for a, b in homes]
    if pairs:
        down_grad, gate_sum, up_sum, out_sum, attn_sum = totals[:5]
        output_grad = lax.ppermute(out_sum, AXES, homeward)
    else:
        outer = size["zh"] * team

        def sum_peers(term, outer=1):
            return sum_over(sum_over(term, "x", outer).astype(BF16), "zh").astype(BF16)

        attn_term = dot(norm_one_pair, g_qkv_half, PAIR_ROWS_T).astype(BF16)
        gate_term = dot(norm_two_pair, gate_half, PAIR_ROWS_T).astype(BF16)
        up_term = dot(norm_two_pair, up_half, PAIR_ROWS_T).astype(BF16)
        out_term = dot(o_half, ga_pair.reshape(2, n_tok, width), PAIR_ROWS_T).astype(BF16)
        down_grad = sum_peers(down_term)
        output_grad = lax.ppermute(sum_peers(out_term), AXES, homeward)
        terms = (attn_term, gate_term, up_term)
        attn_sum, gate_sum, up_sum = exchange(
            [by_owner(sum_peers(term, outer)) for term in terms], 9
        )
    gn1 = added(gn1_terms[0], gn1_terms[1:]) * gain_one
    g_tokens = (
        gh1
        + scale_one * gn1
        - tokens * scale_one**3 * jnp.mean(tokens * gn1, axis=-1, keepdims=True)
    )
    input_grad = g_tokens.astype(BF16).reshape(inputs.shape)

    if ff_rows % 128 == 0:
        (query_grad, key_grad, value_grad, gate_grad, up_grad, attn_against, ffn_against) = finish(
            (attn_sum, gate_sum, up_sum),
            (query_weight, key_matrix, value_matrix, gate_weight, up_weight),
            ff_rows,
        )
        attn_against, ffn_against = attn_against[:, 0], ffn_against[:, 0]
    else:

        def ff_natural(total):
            cut = total.reshape(
                size["zl"], size["y"], size["c"], rows, size["x"], size["zh"], ff_rows
            )
            return cut.transpose(3, 5, 0, 1, 4, 2, 6).reshape(rows, -1).astype(F32)

        def side(part):
            return part.transpose(1, 0, 2).reshape(rows, -1).astype(F32)

        attn_sum = attn_sum.reshape(team, 2, rows, -1)
        query_grad = side(attn_sum[:, 0])
        key_grad = side(attn_sum[:, 1, :, :kv_cols])
        value_grad = side(attn_sum[:, 1, :, kv_cols:])
        gate_grad = ff_natural(gate_sum)
        up_grad = ff_natural(up_sum)

        def against(w, g):
            return jnp.sum(w.astype(F32) * g, axis=1)

        attn_against = (
            against(query_weight, query_grad)
            + against(key_matrix, key_grad)
            + against(value_matrix, value_grad)
        )
        ffn_against = against(gate_weight, gate_grad) + against(up_weight, up_grad)
    attn_gain_grad = attn_against / attn_gain.astype(F32)
    ffn_gain_grad = ffn_against / ffn_gain.astype(F32)
    return (
        outputs,
        input_grad,
        attn_gain_grad,
        query_grad,
        key_grad,
        value_grad,
        output_grad.astype(F32),
        ffn_gain_grad,
        gate_grad,
        up_grad,
        down_grad.astype(F32),
    )


def finish(sums, weights, block):
    sizes = {a: lax.axis_size(a) for a in AXES}
    rows = weights[0].shape[0]
    members = offsets(sizes, OWNERS)
    shares = offsets(sizes, ("x", "zh"))

    def kernel(
        attn, gate, up, wq, wk, wv, wg, wu, gq, gk, gv, gg, gu, attn_total, ffn_total
    ):
        totals = []

        def put(value, out, weight, start):
            value = value.astype(F32)
            width = value.shape[1]
            out[:, start : start + width] = value
            totals.append(
                jnp.sum(weight[:, start : start + width].astype(F32) * value, axis=1, keepdims=True)
            )

        q_width, kv_width = gq.shape[1] // 4, gk.shape[1] // 4
        for i, owner in enumerate(members):
            f = place(owner, TEAM, sizes)
            if owner["c"] == 0:
                put(attn[i], gq, wq, f * q_width)
            else:
                put(attn[i, :, :kv_width], gk, wk, f * kv_width)
                put(attn[i, :, kv_width:], gv, wv, f * kv_width)
        attn_total[...] = sum(totals)
        totals.clear()
        for i, owner in enumerate(members):
            for n, share in enumerate(shares):
                start = place({**owner, **share}, AXES, sizes) * block
                window = slice(n * block, (n + 1) * block)
                put(gate[i, :, window], gg, wg, start)
                put(up[i, :, window], gu, wu, start)
        ffn_total[...] = sum(totals)

    shape = jax.ShapeDtypeStruct
    return pl.pallas_call(
        kernel,
        out_shape=[shape(w.shape, F32) for w in weights] + [shape((rows, 1), F32)] * 2,
        in_specs=[pl.BlockSpec(memory_space=pltpu.VMEM)] * 8,
        out_specs=[pl.BlockSpec(memory_space=pltpu.VMEM)] * 7,
        compiler_params=pltpu.CompilerParams(vmem_limit_bytes=VMEM_LIMIT),
    )(*sums, *weights)


def solution(mesh):
    ctx, fsdp = mesh.shape["ctx"], mesh.shape["fsdp"]
    grid = Mesh(mesh.devices.reshape(ctx // 2, 2, 2, fsdp // 4, 2), AXES)
    act = P(("y", "x", "c"), None, ("zh", "zl"), None)
    row = P(AXES)
    return jax.shard_map(
        on_device,
        mesh=grid,
        in_specs=(act, P(("y", "x", "c"))) + (row,) * 9 + (act,),
        out_specs=(act, act) + (row,) * 9,
        check_vma=False,
    )
```

```python
import itertools
import math

import jax
import jax.numpy as jnp
from jax import lax
from jax.experimental import pallas as pl
from jax.experimental.pallas import tpu as pltpu
from jax.sharding import Mesh
from jax.sharding import PartitionSpec as P

HEAD = 256
VMEM_LIMIT = 48 << 20
FFN_VMEM_LIMIT = 62 << 20
BLK = 128
EPS = 1e-06
ROPE_BASE = 1000042.0
AXES = ("zh", "zl", "y", "x", "c")
TEAM = ("zl", "y")
SLOTS = ("y", "zl")
PAIRED_SLOTS = ("c", "y", "zl")
SHARES = ("c", "x", "zh")
OWNERS = ("zl", "y", "c")
ROWS_T = (((0,), (0,)), ((), ()))
PAIR_ROWS_T = (((0, 1), (0, 1)), ((), ()))
COLS_T = (((1,), (1,)), ((), ()))
F32 = jnp.float32
BF16 = jnp.bfloat16


def offsets(sizes, axes):
    return [dict(zip(axes, o)) for o in itertools.product(*(range(sizes[a]) for a in axes))]


def place(at, layout, sizes):
    index = 0
    for a in layout:
        index = index * sizes[a] + at[a]
    return index


class Gather:
    def __init__(self, x, layout, orders, rank=1):
        self.x, self.layout, self.orders, self.rank = x, layout, orders, rank

    def shape(self, sizes):
        return (math.prod(sizes[a] for a in self.layout),) + self.x.shape

    def cut(self, ref, part):
        rows = self.x.shape[0] // len(self.orders)
        return ref.at[pl.ds(part * rows, rows)]

    def spot(self, out, owner, off, part, sizes):
        return self.cut(out.at[place(owner, self.layout, sizes)], part)


class NearGather(Gather):
    def shape(self, sizes):
        return tuple(sizes[a] for a in self.layout) + self.x.shape

    def spot(self, out, owner, off, part, sizes):
        return self.cut(out.at[tuple(off[a] for a in self.layout)], part)


class RowGather(Gather):
    def shape(self, sizes):
        team, rows, columns = self.x.shape
        return (sizes["x"] * sizes["zh"] * team * sizes["c"] * rows, columns)

    def cut(self, ref, part):
        return ref.at[part]

    def spot(self, out, owner, off, part, sizes):
        team, rows, _ = self.x.shape
        block = (owner["zh"] * team + part) * sizes["x"] + owner["x"]
        start = pl.multiple_of((block * sizes["c"] + owner["c"]) * rows, rows)
        return out.at[pl.ds(start, rows)]


class RowGatherOf(RowGather):
    def __init__(self, source, x, orders):
        super().__init__(jax.ShapeDtypeStruct(x.shape, x.dtype), None, orders)
        self.source = source


class Swap:
    def __init__(self, x, layout):
        self.x, self.layout = x, layout

    def shape(self, sizes):
        return self.x.shape

    def own_shape(self, sizes):
        return self.x.shape[1:]

    def offsets(self, sizes):
        return offsets(sizes, self.layout)

    def pair(self, x, out, here, to, off, sizes):
        return x.at[place(to, self.layout, sizes)], out.at[place(here, self.layout, sizes)]


class ColumnSwap:
    def __init__(self, x, block):
        self.x, self.block = x, block

    def shape(self, sizes):
        rows, columns = self.x.shape
        team = sizes["zl"] * sizes["y"]
        return (team, rows, columns // team)

    def own_shape(self, sizes):
        return self.shape(sizes)[1:]

    def offsets(self, sizes):
        return offsets(sizes, TEAM)

    def pieces(self, x, out, to, sizes):
        found = []
        for i, share in enumerate(offsets(sizes, SHARES)):
            start = pl.multiple_of(place({**share, **to}, AXES, sizes) * self.block, self.block)
            found.append(
                (x.at[:, pl.ds(start, self.block)], out.at[:, pl.ds(i * self.block, self.block)])
            )
        return found


class NearSwap(Swap):
    def pair(self, x, out, here, to, off, sizes):
        i = off[self.layout[0]]
        return x.at[i], out.at[i]


class Halves:
    def __init__(self, x):
        self.x = x

    def shape(self, sizes):
        rows, columns = self.x.shape
        return (2, rows, columns // 2)

    def own_shape(self, sizes):
        rows, columns = self.x.shape
        return (rows, columns // 2)

    def offsets(self, sizes):
        return offsets(sizes, ("c",))

    def pair(self, x, out, here, to, off, sizes):
        width = self.x.shape[1] // 2
        start = pl.multiple_of(to["c"] * width, width)
        return x.at[:, pl.ds(start, width)], out.at[off["c"]]


CHUNKS = 4
AHEAD = 10
ROOM = 5
FLOW = (2, 8, 6, 6)


class TeamSum:
    def __init__(self, x, y_first=2):
        self.x, self.y_first = x, y_first

    def shape(self, sizes):
        return (2,) + self.x.shape[2:]


class Net:
    def __init__(self, sizes):
        self.sizes, self.count, self.reached = sizes, 0, set()

    def wire(self, off):
        self.reached.add(tuple(off.get(a, 0) for a in AXES))
        self.count += 1
        return self.count - 1, off

    def open(self, send_sem, recv_sem):
        self.send_sem, self.recv_sem = send_sem, recv_sem
        self.here = {a: lax.axis_index(a) for a in AXES}
        self.sent = []
        barrier = pltpu.get_barrier_semaphore()
        for off in sorted(self.reached):
            pl.semaphore_signal(
                barrier,
                inc=1,
                device_id=self.device(self.moved(dict(zip(AXES, off)))),
                device_id_type=pl.DeviceIdType.MESH,
            )
        pl.semaphore_wait(barrier, len(self.reached))

    def moved(self, off):
        return {
            a: lax.rem(self.here[a] + off[a], self.sizes[a]) if off.get(a, 0) else self.here[a]
            for a in AXES
        }

    def device(self, at):
        return tuple(at[a] for a in AXES)

    def send(self, src, dst, wire):
        sem, off = wire
        cp = pltpu.make_async_remote_copy(
            src_ref=src,
            dst_ref=dst,
            send_sem=self.send_sem.at[sem],
            recv_sem=self.recv_sem.at[sem],
            device_id=self.device(self.moved(off)),
            device_id_type=pl.DeviceIdType.MESH,
        )
        cp.start()
        self.sent.append(cp)
        return cp

    def settle(self, cp):
        cp.wait_send()
        self.sent = [other for other in self.sent if other is not cp]

    def close(self):
        for cp in self.sent:
            cp.wait_send()


class Relay:
    def __init__(self, job, number, net):
        self.job, self.net, self.sizes = job, net, net.sizes
        self.steps = []
        for part, order in enumerate(job.orders):
            groups = [(axes,) if isinstance(axes, str) else axes for axes in order]
            for off in offsets(self.sizes, [a for axes in groups for a in axes]):
                used = [i for i, axes in enumerate(groups) if any(off[a] for a in axes)]
                sends = [
                    net.wire(to)
                    for axes in groups[used[-1] + 1 if used else 0 :]
                    for to in offsets(self.sizes, axes)
                    if any(to.values())
                ]
                hops = len(used)
                key = (job.rank, part + 2 * hops, hops, number, part)
                self.steps.append((key, self, hops, part, off, sends))

    def open(self, x, out):
        self.x, self.out, self.arrivals = x, out, {}

    def run(self, hops, part, off, sends):
        job, net = self.job, self.net
        owner = net.moved(off)
        if hops:
            self.arrivals[part, tuple(sorted(off.items()))].wait_recv()
            source = job.spot(self.out, owner, off, part, self.sizes)
        else:
            source = job.cut(self.x, part)
        for wire in sends:
            there = dict(off)
            for a, d in wire[1].items():
                there[a] = -d % self.sizes[a]
            dst = job.spot(self.out, owner, there, part, self.sizes)
            self.arrivals[part, tuple(sorted(there.items()))] = net.send(source, dst, wire)

    def own(self, part):
        return self.job.spot(self.out, self.net.here, {a: 0 for a in AXES}, part, self.sizes)


class Stream:
    def __init__(self, net, shape, owners):
        self.net, self.owners = net, owners
        self.nx, self.nz = net.sizes["x"], net.sizes["zh"]
        self.columns, self.dtype = shape[1], BF16
        self.rows = shape[0] // (self.nx * self.nz * CHUNKS)
        self.chunks = [(z, q) for z in [*range(1, self.nz), 0] for q in range(CHUNKS)]
        self.x_wires = [[net.wire({"x": d}) for d in range(1, self.nx)] for _ in self.chunks]
        self.z_wires = [net.wire({"zh": z}) if z else None for z, _ in self.chunks]
        if owners:
            self.members = offsets(net.sizes, TEAM)
            self.own_rows = self.rows // net.sizes["c"]
            self.cores = [
                [({**o, "c": c}, net.wire({**o, "c": c}) if c or any(o.values()) else None)
                 for c in range(net.sizes["c"])]
                for o in self.members
            ]

    def shape(self):
        rows = CHUNKS * self.rows
        if not self.owners:
            return jax.ShapeDtypeStruct((rows, self.columns), self.dtype)
        n = math.prod(self.net.sizes[a] for a in OWNERS)
        return jax.ShapeDtypeStruct((n, rows // n, self.columns), self.dtype)

    def scratch(self):
        n, chunk = len(self.chunks), (self.rows, self.columns)
        return [
            pltpu.VMEM((n, *chunk), self.dtype),
            pltpu.VMEM((self.nx - 1, n, *chunk), self.dtype),
            pltpu.VMEM((self.nz - 1, CHUNKS, *chunk), self.dtype),
            pltpu.SemaphoreType.DMA((n,)),
            pltpu.SemaphoreType.DMA((CHUNKS,)),
        ]

    def open(self, term, out, mine, from_x, from_z, load_sem, store_sem):
        self.term, self.out, self.mine = term, out, mine
        self.from_x, self.from_z = from_x, from_z
        self.load_sem, self.store_sem = load_sem, store_sem
        self.loads, self.x_sent, self.z_sent, self.stores, self.handed = {}, {}, {}, [], []

    def window(self, x, z, q):
        zh = self.net.moved({"zh": z})["zh"]
        if self.owners:
            q = place(self.net.moved(self.members[q]), TEAM, self.net.sizes)
            block = (zh * CHUNKS + q) * self.nx + x
        else:
            block = (x * self.nz + zh) * CHUNKS + q
        return self.term.at[pl.ds(pl.multiple_of(block * self.rows, self.rows), self.rows)]

    def issue(self, k):
        z, q = self.chunks[k]
        self.x_sent[k] = []
        for d, wire in enumerate(self.x_wires[k], 1):
            x = self.net.moved({"x": d})["x"]
            self.x_sent[k].append(
                self.net.send(self.window(x, z, q), self.from_x.at[d - 1, k], wire)
            )
        load = pltpu.make_async_copy(
            self.window(self.net.here["x"], z, q), self.mine.at[k], self.load_sem.at[k]
        )
        load.start()
        self.loads[k] = load

    def merge(self, k):
        z, q = self.chunks[k]
        self.loads[k].wait()
        for cp in self.x_sent[k]:
            cp.wait_recv()
        total = self.mine[k].astype(F32)
        for d in range(self.nx - 1):
            total += self.from_x[d, k].astype(F32)
        self.mine[k] = total.astype(self.dtype)
        if z:
            self.z_sent[z, q] = self.net.send(
                self.mine.at[k], self.from_z.at[z - 1, q], self.z_wires[k]
            )

    def last(self, q):
        k = self.chunks.index((0, q))
        total = self.mine[k].astype(F32)
        for z in range(1, self.nz):
            self.z_sent[z, q].wait_recv()
            total += self.from_z[z - 1, q].astype(F32)
        self.mine[k] = total.astype(self.dtype)
        if self.owners:
            mine = place(self.net.here, OWNERS, self.net.sizes)
            for off, wire in self.cores[q]:
                core = self.net.moved(off)["c"]
                start = pl.multiple_of(core * self.own_rows, self.own_rows)
                src = self.mine.at[k, pl.ds(start, self.own_rows)]
                if wire:
                    self.handed.append(self.net.send(src, self.out.at[mine], wire))
                else:
                    store = pltpu.make_async_copy(src, self.out.at[mine], self.store_sem.at[q])
                    store.start()
                    self.stores.append(store)
            return
        store = pltpu.make_async_copy(
            self.mine.at[k], self.out.at[pl.ds(q * self.rows, self.rows)], self.store_sem.at[q]
        )
        store.start()
        self.stores.append(store)

    def close(self):
        for cp in self.handed:
            cp.wait_recv()
        for store in self.stores:
            store.wait()


class Adder:
    def __init__(self, job, number, net):
        self.job, self.net = job, net
        rows = job.x.shape[2] // CHUNKS
        self.steps = []
        self.parts = []
        for part in range(CHUNKS):
            first, second = ("y", "zl") if part < job.y_first else ("zl", "y")
            wires = net.wire({first: 1}), net.wire({first: 1}), net.wire({second: 1})
            self.parts.append((pl.ds(part * rows, rows), first, second, wires))
            self.steps.append(((0, part, 0, number, part), self, 0, part, None, None))
            self.steps.append(((1, part + 2, 1, number, part), self, 1, part, None, None))

    def scratch(self):
        shape = self.job.x.shape[2:]
        return [pltpu.VMEM(shape, self.job.x.dtype)] * 2 + [pltpu.SemaphoreType.DMA((CHUNKS,))]

    def open(self, x, out, term, far, sem):
        self.x, self.out, self.term, self.far, self.sem = x, out, term, far, sem
        self.waits, self.direct, self.summed = {}, [], []

    def run(self, hops, part, *_):
        window, first, second, wires = self.parts[part]
        y_first = first == "y"
        if not hops:
            self.waits[part] = self.net.send(
                self.x.at[1, 1, window], self.far.at[window], wires[0]
            )
            near = self.x.at[1, 0, window] if y_first else self.x.at[0, 1, window]
            self.direct.append(
                self.net.send(near, self.out.at[0 if y_first else 1, window], wires[1])
            )
            mine = self.x.at[0, 1, window] if y_first else self.x.at[1, 0, window]
            load = pltpu.make_async_copy(mine, self.term.at[window], self.sem.at[part])
            load.start()
            self.waits[part] = self.waits[part], load
            return
        far, load = self.waits[part]
        load.wait()
        far.wait_recv()
        total = self.term[window].astype(F32) + self.far[window].astype(F32)
        self.term[window] = total.astype(self.term.dtype)
        self.summed.append(
            self.net.send(
                self.term.at[window], self.out.at[1 if y_first else 0, window], wires[2]
            )
        )

    def finish(self):
        for cp in self.direct + self.summed:
            cp.wait_recv()


def exchange(jobs, collective_id, micros=50):
    net = Net({a: lax.axis_size(a) for a in AXES})
    sizes = net.sizes
    count = len(jobs)
    n_in = sum(not isinstance(job, RowGatherOf) for job in jobs)
    steps, swaps, runners, scratch = [], [], [], []
    for number, job in enumerate(jobs):
        if isinstance(job, Gather):
            runner = Relay(job, number, net)
            if not isinstance(job, RowGatherOf):
                steps += runner.steps
            stage = [pltpu.VMEM(job.x.shape, job.x.dtype)]
        elif isinstance(job, TeamSum):
            runner = Adder(job, number, net)
            steps += runner.steps
            stage = runner.scratch()
        else:
            runner = None
            n = math.prod(sizes[a] for a in SHARES) if isinstance(job, ColumnSwap) else 1
            for off in job.offsets(sizes):
                if any(off.values()):
                    swaps.append((number, off, [net.wire(off) for _ in range(n)]))
            stage = [pltpu.VMEM(job.own_shape(sizes), job.x.dtype)]
        runners.append((runner, len(scratch), len(scratch) + len(stage)))
        scratch += stage
    steps.sort(key=lambda s: s[0])

    def kernel(*refs):
        ins, outs, rest = refs[:n_in], refs[n_in : n_in + count], refs[n_in + count :]
        send_sem, recv_sem, local_sem, piece_sem = rest[-4:]
        net.open(send_sem, recv_sem)
        loads, stores = [], []
        for number, job in enumerate(jobs):
            runner, lo, hi = runners[number]
            if isinstance(job, TeamSum):
                runner.open(ins[number], outs[number], *rest[lo:hi])
                continue
            if isinstance(job, RowGatherOf):
                continue
            (stage,) = rest[lo:hi]
            if runner:
                runner.open(ins[number], outs[number])
                src = ins[number]
                puts = [
                    (job.cut(stage, part), runner.own(part)) for part in range(len(job.orders))
                ]
            elif isinstance(job, ColumnSwap):
                mine = {a: net.here[a] for a in TEAM}
                for i, (src, dst) in enumerate(job.pieces(ins[number], stage, mine, sizes)):
                    load = pltpu.make_async_copy(src, dst, piece_sem.at[number, i])
                    load.start()
                    loads.append((load, number, []))
                loads[-1][2].append((stage, outs[number].at[place(net.here, TEAM, sizes)]))
                continue
            else:
                none = {a: 0 for a in AXES}
                src, dst = job.pair(ins[number], outs[number], net.here, net.here, none, sizes)
                puts = [(stage, dst)]
            load = pltpu.make_async_copy(src, stage, local_sem.at[number, 0])
            load.start()
            loads.append((load, number, puts))
        for _, runner, hops, *what in steps:
            if not hops:
                runner.run(hops, *what)
        received = []
        for number, off, wires in swaps:
            to = net.moved(off)
            job = jobs[number]
            if isinstance(job, ColumnSwap):
                mine = outs[number].at[place(net.here, TEAM, sizes)]
                pairs = job.pieces(ins[number], mine, {a: to[a] for a in TEAM}, sizes)
            else:
                pairs = [job.pair(ins[number], outs[number], net.here, to, off, sizes)]
            for (src, dst), wire in zip(pairs, wires, strict=True):
                received.append((number, net.send(src, dst, wire)))
        for load, number, puts in loads:
            load.wait()
            for i, (src, dst) in enumerate(puts):
                store = pltpu.make_async_copy(src, dst, local_sem.at[number, 1 + i])
                store.start()
                stores.append((number, store))
        for _, runner, hops, *what in steps:
            if hops:
                runner.run(hops, *what)
        for number, job in enumerate(jobs):
            if not isinstance(job, RowGatherOf):
                continue
            for cps in (received, stores):
                for other, cp in [one for one in cps if one[0] == job.source]:
                    cp.wait_recv() if cps is received else cp.wait()
            received = [one for one in received if one[0] != job.source]
            stores = [one for one in stores if one[0] != job.source]
            runner, lo, hi = runners[number]
            (stage,) = rest[lo:hi]
            source = outs[job.source]
            runner.open(source, outs[number])
            load = pltpu.make_async_copy(source, stage, local_sem.at[number, 0])
            load.start()
            waiting = sorted(runner.steps, key=lambda step: step[0])
            for _, _, hops, *what in waiting:
                if not hops:
                    runner.run(hops, *what)
            load.wait()
            for part in range(len(job.orders)):
                store = pltpu.make_async_copy(
                    job.cut(stage, part), runner.own(part), local_sem.at[number, 1 + part]
                )
                store.start()
                stores.append((number, store))
            for _, _, hops, *what in waiting:
                if hops:
                    runner.run(hops, *what)
        for _, cp in received:
            cp.wait_recv()
        for runner, _, _ in runners:
            if isinstance(runner, Adder):
                runner.finish()
        net.close()
        for _, store in stores:
            store.wait()

    return pl.pallas_call(
        kernel,
        out_shape=[jax.ShapeDtypeStruct(job.shape(sizes), job.x.dtype) for job in jobs],
        in_specs=[pl.BlockSpec(memory_space=pl.ANY)] * n_in,
        out_specs=[pl.BlockSpec(memory_space=pl.ANY)] * count,
        scratch_shapes=scratch
        + [
            pltpu.SemaphoreType.DMA((net.count,)),
            pltpu.SemaphoreType.DMA((net.count,)),
            pltpu.SemaphoreType.DMA((count, 1 + CHUNKS)),
            pltpu.SemaphoreType.DMA((count, math.prod(sizes[a] for a in SHARES))),
        ],
        cost_estimate=pl.CostEstimate(
            flops=0, bytes_accessed=micros * 3_000_000, transcendentals=0
        ),
        compiler_params=pltpu.CompilerParams(
            collective_id=collective_id, has_side_effects=True, vmem_limit_bytes=VMEM_LIMIT
        ),
    )(*[job.x for job in jobs[:n_in]])


def sum_over(term, axis, outer=1):
    size = lax.axis_size(axis)
    me = lax.axis_index(axis)
    columns = term.shape[1]
    term = term.reshape(outer, -1, columns)
    while size > 1:
        size //= 2
        rows = term.shape[1] // 2
        pairs = [(i, i ^ size) for i in range(lax.axis_size(axis))]
        side = (me // size) % 2
        kept = lax.dynamic_slice_in_dim(term, side * rows, rows, axis=1)
        other = lax.ppermute(
            lax.dynamic_slice_in_dim(term, (1 - side) * rows, rows, axis=1), axis, pairs
        )
        term = kept.astype(F32) + other.astype(F32)
        if size > 1:
            term = term.astype(BF16)
    return term.reshape(-1, columns)


def dot(a, b, dims=None):
    if dims is None:
        return jnp.dot(a, b, preferred_element_type=F32)
    return lax.dot_general(a, b, dims, preferred_element_type=F32)


def rotate(t, cos, sin):
    half = t.shape[-1] // 2
    front, back = t[..., :half], t[..., half:]
    return jnp.concatenate([front * cos - back * sin, back * cos + front * sin], axis=-1)


def rms_scale(values):
    return lax.rsqrt(jnp.mean(values * values, axis=-1, keepdims=True) + EPS)


def attention_front(
    norm, w_attn, out_part, gate_part, down_part, gd, q_pos, k_pos, cos, sin, scaling, collective_id
):
    net = Net({a: lax.axis_size(a) for a in AXES})
    sizes = net.sizes
    own, width = norm.shape
    n_slot, n_zh, _, n = k_pos.shape
    n_tok = n_slot * n
    columns = w_attn.shape[1]
    q_cols = columns - 2 * HEAD
    heads = q_cols // HEAD
    half = q_cols // 2
    team = gate_part.shape[0]
    norm_job = NearGather(norm, PAIRED_SLOTS, TO_TEAM)
    down_job = Gather(down_part, SHARES, [OUTWARD] * CHUNKS)
    out_job = Gather(out_part, SHARES, [OUTWARD] * (out_part.shape[0] // 16), rank=2)
    gd_job = NearGather(gd, PAIRED_SLOTS, TO_TEAM)
    gate_job = RowGather(gate_part, None, [OUTWARD] * team)
    norms, downs, outs = (Relay(job, i, net) for i, job in enumerate((norm_job, down_job, out_job)))
    gds, gates = (Relay(job, i, net) for i, job in enumerate((gd_job, gate_job)))
    first = sorted(norms.steps + downs.steps, key=lambda step: step[0])
    out_steps = sorted(outs.steps, key=lambda step: step[0])
    gd_steps = sorted(gds.steps, key=lambda step: step[0])
    gate_steps = sorted(gates.steps, key=lambda step: step[0])
    kv_wires = [[net.wire({"zh": z}) for z in range(1, n_zh)] for _ in range(n_slot)]
    half_wires = [net.wire({"c": 1}) for _ in range(n_slot)]
    y_rows, zl_rows = pl.ds(0, own * 6 // 8), pl.ds(own * 6 // 8, own - own * 6 // 8)
    far_wires = net.wire({"y": 1}), net.wire({"zl": 1})
    near_wires = net.wire({"y": 1}), net.wire({"zl": 1})
    n_local = 64
    out_shapes = [job.shape(sizes) for job in (norm_job, gd_job, out_job, gate_job, down_job)]

    def kernel(
        norm_ref, w_attn_ref, outp_ref, gate_ref, down_ref, gd_ref, q_pos_ref, k_pos_ref, cos_ref,
        sin_ref, norms_ref, gds_ref, w_out_ref, w_gate_ref, w_down_ref, q_ref, kv_ref, lse_ref,
        half_ref, terms_ref,
        nv, wa, wo, q, kv, o, terms, far, gd_stage, gate_stage, down_stage,
        send_sem, recv_sem, local_sem,
    ):
        net.open(send_sem, recv_sem)
        norms.open(norm_ref, norms_ref)
        downs.open(down_ref, w_down_ref)
        outs.open(outp_ref, wo)
        gds.open(gd_ref, gds_ref)
        gates.open(gate_ref, w_gate_ref)
        used = iter(range(n_local))

        def local(src, dst):
            cp = pltpu.make_async_copy(src, dst, local_sem.at[next(used)])
            cp.start()
            return cp

        def start(steps):
            for _, runner, hops, *what in steps:
                if not hops:
                    runner.run(hops, *what)

        start(first)
        got_norm = local(norm_ref, nv.at[0, 0])
        start(out_steps)
        got_attn = [local(w_attn_ref, wa)]
        got_attn += [
            local(out_job.cut(outp_ref, p), outs.own(p)) for p in range(len(out_job.orders))
        ]
        got_gd, got_gate = local(gd_ref, gd_stage), local(gate_ref, gate_stage)
        got_down = local(down_ref, down_stage)
        got_norm.wait()
        kept = [local(norm_job.cut(nv.at[0, 0], p), norms.own(p)) for p in range(CHUNKS)]
        got_gd.wait()
        kept += [local(gd_job.cut(gd_stage, p), gds.own(p)) for p in range(CHUNKS)]
        got_gate.wait()
        kept += [local(gate_job.cut(gate_stage, p), gates.own(p)) for p in range(team)]
        got_down.wait()
        kept += [local(down_job.cut(down_stage, p), downs.own(p)) for p in range(CHUNKS)]

        def turn(t, rows):
            h = HEAD // 2
            c, sn = cos_ref[rows], sin_ref[rows]
            front, back = t[:, :h], t[:, h:]
            return jnp.concatenate([front * c - back * sn, back * c + front * sn], axis=1).astype(
                BF16
            )

        def project(s):
            for j in range(n // own):
                rows = slice(s * n + j * own, s * n + (j + 1) * own)
                for g in range(heads):
                    cols = slice(g * HEAD, (g + 1) * HEAD)
                    q[rows, cols] = turn(dot(nv[s, j], wa[:, cols]), rows)
                kv[0, rows, :HEAD] = turn(dot(nv[s, j], wa[:, q_cols : q_cols + HEAD]), rows)
                kv[0, rows, HEAD:] = dot(nv[s, j], wa[:, q_cols + HEAD :]).astype(BF16)
            window = pl.ds(s * n, n)
            return [
                net.send(kv.at[0, window], kv.at[n_zh - z, window], kv_wires[s][z - 1])
                for z in range(1, n_zh)
            ]

        def attend(s, sent):
            for cp in sent:
                cp.wait_recv()
            rows = slice(s * n, (s + 1) * n)
            for g in range(heads):
                cols = slice(g * HEAD, (g + 1) * HEAD)
                scores = []
                for z in range(n_zh):
                    score = dot(q[rows, cols], kv[z, rows, :HEAD], COLS_T) * scaling
                    allowed = k_pos_ref[s, z] <= q_pos_ref[...]
                    scores.append(jnp.where(allowed, score, -jnp.inf))
                peak = scores[0].max(axis=1, keepdims=True)
                for score in scores[1:]:
                    peak = jnp.maximum(peak, score.max(axis=1, keepdims=True))
                exps = [jnp.exp(score - peak) for score in scores]
                total = sum(e.sum(axis=1, keepdims=True) for e in exps)
                inverse = 1.0 / total
                o[rows, cols] = sum(
                    dot((e * inverse).astype(BF16), kv[z, rows, HEAD:]) for z, e in enumerate(exps)
                ).astype(BF16)
                lse_ref[s, g] = peak + jnp.log(total)
            away = pl.ds(pl.multiple_of((1 - net.here["c"]) * half, half), half)
            here = pl.ds(pl.multiple_of(net.here["c"] * half, half), half)
            window = pl.ds(s * n, n)
            halves.append(net.send(o.at[window, away], half_ref.at[1, window], half_wires[s]))
            kept.append(local(o.at[window, here], half_ref.at[0, window]))

        def term(r):
            def tile(t, _):
                at = pl.ds(pl.multiple_of(t * TILE, TILE), TILE)
                weight = wo[:, :, at].reshape(q_cols, TILE)
                terms[r, :, at] = dot(o[r * own : (r + 1) * own], weight).astype(BF16)
                return 0

            lax.fori_loop(0, width // TILE, tile, 0)

        def add(r, window):
            terms[r, window] = (terms[r, window].astype(F32) + far[window].astype(F32)).astype(BF16)

        halves, late = [], []

        def relay(steps):
            for _, runner, hops, part, off, sends in steps:
                if not hops:
                    continue
                if runner in (norms, gds) and off["c"]:
                    late.append((runner, hops, part, off, sends))
                    continue
                runner.run(hops, part, off, sends)
                if runner is norms and part == CHUNKS - 1:
                    i, j = off["y"], off["zl"]
                    got[i, j] = local(norms_ref.at[0, i, j], nv.at[i, j])

        got = {}
        relay([step for step in first if step[1] is norms or step[0][1] <= ROOM])
        for cp in got_attn:
            cp.wait()
        start(gd_steps)
        got[0, 1].wait()
        sent = [project(0)]
        got[1, 0].wait()
        got[1, 1].wait()
        sent.append(project(1))
        relay([step for step in first if not (step[1] is norms or step[0][1] <= ROOM)])
        relay(out_steps)
        kept.append(local(wo, w_out_ref))
        relay([step for step in gd_steps if step[2] == 1])
        attend(0, sent[0])
        start(gate_steps)
        term(1)
        term(0)
        relay([step for step in gd_steps if step[2] > 1])
        attend(1, sent[1])
        term(3)
        to_far = (
            net.send(terms.at[3, y_rows], far.at[y_rows], far_wires[0]),
            net.send(terms.at[3, zl_rows], far.at[zl_rows], far_wires[1]),
        )
        term(2)
        kept.append(local(terms.at[0], terms_ref.at[0]))
        kept.append(local(q, q_ref))
        kept.append(local(kv, kv_ref))
        relay([step for step in gate_steps if step[2] == 1 and step[3] < 2])
        to_far[1].wait_recv()
        add(2, zl_rows)
        to_y = net.send(terms.at[2], terms_ref.at[1], near_wires[0])
        to_far[0].wait_recv()
        add(1, y_rows)
        to_zl = net.send(terms.at[1], terms_ref.at[2], near_wires[1])
        relay([step for step in gate_steps if not (step[2] == 1 and step[3] < 2)])
        for runner, *step in late:
            runner.run(*step)
        for cp in halves + [to_y, to_zl]:
            cp.wait_recv()
        net.close()
        for cp in kept:
            cp.wait()

    shape = jax.ShapeDtypeStruct
    vmem, hbm = pl.BlockSpec(memory_space=pltpu.VMEM), pl.BlockSpec(memory_space=pl.ANY)
    q_shape, kv_shape = (n_tok, q_cols), (n_zh, n_tok, 2 * HEAD)
    return pl.pallas_call(
        kernel,
        out_shape=[
            *[shape(dims, BF16) for dims in out_shapes],
            shape(q_shape, BF16),
            shape(kv_shape, BF16),
            shape((n_slot, heads, n, 1), F32),
            shape((2, n_tok, half), BF16),
            shape((3, own, width), BF16),
        ],
        in_specs=[hbm] * 6 + [vmem] * 4,
        out_specs=[hbm] * 7 + [vmem] + [hbm] * 2,
        scratch_shapes=[
            pltpu.VMEM((2, 2, own, width), BF16),
            pltpu.VMEM(w_attn.shape, BF16),
            pltpu.VMEM(out_shapes[2], BF16),
            pltpu.VMEM(q_shape, BF16),
            pltpu.VMEM(kv_shape, BF16),
            pltpu.VMEM(q_shape, BF16),
            pltpu.VMEM((4, own, width), BF16),
            pltpu.VMEM((own, width), BF16),
            pltpu.VMEM(gd.shape, BF16),
            pltpu.VMEM(gate_part.shape, BF16),
            pltpu.VMEM(down_part.shape, BF16),
            pltpu.SemaphoreType.DMA((net.count,)),
            pltpu.SemaphoreType.DMA((net.count,)),
            pltpu.SemaphoreType.DMA((n_local,)),
        ],
        cost_estimate=pl.CostEstimate(
            flops=0, bytes_accessed=160 * 3_000_000, transcendentals=0
        ),
        compiler_params=pltpu.CompilerParams(
            collective_id=collective_id, has_side_effects=True, vmem_limit_bytes=FFN_VMEM_LIMIT
        ),
    )(norm, w_attn, out_part, gate_part, down_part, gd, q_pos, k_pos, cos, sin)


def attention_back(
    ga, q, kv, lse, q_pos, k_pos, cos, sin, w_out, w_attn, out_parts, sums, scaling, collective_id
):
    net = Net({a: lax.axis_size(a) for a in AXES})
    own, width = ga.shape
    n_slot, n_zh, _, n = k_pos.shape
    n_tok = n_slot * n
    heads = q.shape[1] // HEAD
    columns = w_attn.shape[1]
    half = columns // 2
    ga_job = NearGather(ga, PAIRED_SLOTS, TO_TEAM_EVEN)
    gas = Relay(ga_job, 0, net)
    ga_steps = sorted(gas.steps, key=lambda step: step[0])
    adder = Adder(TeamSum(out_parts, CHUNKS // 2), 1, net)
    streams, made = [], []
    if sums:
        down, _, gate_half, _, o_half, _ = sums
        made = [(width, gate_half.shape[2])] * 2 + [(o_half.shape[2], width), (width, half)]
        streams = [Stream(net, down.shape, False)]
        streams += [Stream(net, dims, i != 2) for i, dims in enumerate(made)]
    n_chunks = n_zh * CHUNKS
    kv_wires = [[net.wire({"zh": z}) for z in range(1, n_zh)] for _ in range(n_slot)]
    half_wires = [net.wire({"c": 1}) for _ in range(n_slot)]
    y_rows, zl_rows = pl.ds(0, own // 2), pl.ds(own // 2, own // 2)
    far_wires = net.wire({"y": 1}), net.wire({"zl": 1})
    near_wires = net.wire({"y": 1}), net.wire({"zl": 1})
    n_sums = len(sums) if sums else 0
    n_local = 48

    def kernel(*refs):
        refs = iter(refs)

        def take(count):
            return list(itertools.islice(refs, count))

        ga_ref, q_ref, kv_ref, lse_ref, q_pos_ref, k_pos_ref = take(6)
        cos_ref, sin_ref, wo_ref, wa_ref, parts_ref = take(5)
        sum_ins = take(n_sums)
        gas_ref, half_ref, gn1_ref, added_ref = take(4)
        sum_outs, made_refs = take(len(streams)), take(len(made))
        gav, wo, wa, go, gkv, gkv_away, gkv_out, gkv_in, g_qkv, gn1, far = take(11)
        send_sem, recv_sem, local_sem = take(3)
        adder_scratch = take(3)
        net.open(send_sem, recv_sem)
        gas.open(ga_ref, gas_ref)
        adder.open(parts_ref, added_ref, *adder_scratch)
        for i, stream in enumerate(streams):
            stream.open([*sum_ins[:1], *made_refs][i], sum_outs[i], *take(5))
        used = iter(range(n_local))

        def local(src, dst):
            cp = pltpu.make_async_copy(src, dst, local_sem.at[next(used)])
            cp.start()
            return cp

        plan = []
        for i in range(len(streams)):
            for k in range(n_chunks):
                plan.append((i, k, False))
                q_chunk = k - (n_chunks - CHUNKS)
                if i and q_chunk >= 0:
                    plan.append((i - 1, q_chunk, True))
        plan += [(i, q_chunk, True) for i in range(len(streams))[-1:] for q_chunk in range(CHUNKS)]
        issued, merged = [0] * len(streams), [0] * len(streams)
        ready = [i == 0 for i in range(len(streams))]

        def pump():
            for i, stream in enumerate(streams):
                while ready[i] and issued[i] < n_chunks and sum(issued) < sum(merged) + AHEAD:
                    stream.issue(issued[i])
                    issued[i] += 1
                if issued[i] < n_chunks:
                    return

        def there(i):
            if sums:
                ready[i] = True
                pump()

        def flow(steps):
            while plan and steps:
                i, k, last = plan[0]
                if last:
                    streams[i].last(k)
                elif k < issued[i]:
                    streams[i].merge(k)
                    merged[i] += 1
                    pump()
                else:
                    return
                plan.pop(0)
                steps -= 1

        if sums:
            wr, lt, ot, o_v, wr_sem, lt_sem, ot_sem = take(7)

        def product(lhs_ref, rhs_ref, term_ref, steps):
            n_cols = wr.shape[2]
            n_tiles = width // own

            def lhs(t, slot, c):
                at = pl.ds(pl.multiple_of(t * own, own), own)
                return pltpu.make_async_copy(
                    lhs_ref.at[c, :, at], lt.at[slot, c], lt_sem.at[slot, c]
                )

            for part in range(rhs_ref.shape[2] // n_cols):
                window = pl.ds(part * n_cols, n_cols)
                rhs = [
                    pltpu.make_async_copy(rhs_ref.at[c, :, window], wr.at[c], wr_sem.at[c])
                    for c in range(2)
                ]
                for c in range(2):
                    rhs[c].start()
                    lhs(0, 0, c).start()
                for c in range(2):
                    rhs[c].wait()

                def store(t, slot, window=window):
                    at = pl.ds(pl.multiple_of(t * own, own), own)
                    return pltpu.make_async_copy(
                        ot.at[slot], term_ref.at[at, window], ot_sem.at[slot]
                    )

                def tile(t, _, store=store):
                    slot = lax.rem(t, 2)

                    @pl.when(t + 1 < n_tiles)
                    def _():
                        for c in range(2):
                            lhs(t + 1, 1 - slot, c).start()

                    for c in range(2):
                        lhs(t, slot, c).wait()

                    @pl.when(t >= 2)
                    def _():
                        store(t - 2, slot).wait()

                    value = dot(lt[slot].reshape(2 * n_tok, own), wr[...].reshape(2 * n_tok, n_cols), ROWS_T)
                    ot[slot] = value.astype(BF16)
                    store(t, slot).start()
                    return 0

                lax.fori_loop(0, n_tiles, tile, 0)
                store(n_tiles - 2, n_tiles % 2).wait()
                store(n_tiles - 1, 1 - n_tiles % 2).wait()
                flow(steps)

        for _, _, hops, *what in ga_steps:
            if not hops:
                gas.run(hops, *what)
        if sums:
            pump()
            got_o = local(sum_ins[4], o_v)
        got_wo, got_wa = local(wo_ref, wo), local(wa_ref, wa)
        got_ga = local(ga_ref, gav.at[0, 0])
        got_ga.wait()
        kept = [local(ga_job.cut(gav.at[0, 0], p), gas.own(p)) for p in range(CHUNKS)]
        got_wo.wait()
        got_wa.wait()
        if sums:
            product(sum_ins[1], sum_ins[2], made_refs[0], 1)
            there(1)

        def turn_back(t, rows):
            h = HEAD // 2
            c, sn = cos_ref[rows], sin_ref[rows]
            front, back = t[:, :h], t[:, h:]
            return jnp.concatenate([front * c + back * sn, back * c - front * sn], axis=1).astype(
                BF16
            )

        def slot(s):
            keys = slice(s * n, (s + 1) * n)
            for j in range(2):
                at = pl.ds(s * n + j * own, own)
                go[at, :] = dot(gav[s, j], wo[...], COLS_T).astype(BF16)
            for turn, (g, j) in enumerate(itertools.product(range(heads), range(n // own))):
                rows = slice(s * n + j * own, s * n + (j + 1) * own)
                here = slice(j * own, (j + 1) * own)
                cols = slice(g * HEAD, (g + 1) * HEAD)
                q_g, go_g, lse_g = q_ref[rows, cols], go[rows, cols], lse_ref[s, g, here]
                probs, gps = [], []
                for z in range(n_zh):
                    score = dot(q_g, kv_ref[z, keys, :HEAD], COLS_T) * scaling
                    allowed = k_pos_ref[s, z] <= q_pos_ref[here]
                    probs.append(jnp.where(allowed, jnp.exp(score - lse_g), 0.0))
                    gps.append(dot(go_g, kv_ref[z, keys, HEAD:], COLS_T))
                delta = sum((p * gp).sum(axis=1, keepdims=True) for p, gp in zip(probs, gps))
                gq = 0.0
                for z in range(n_zh):
                    gs = (probs[z] * (gps[z] - delta)).astype(BF16)
                    gq += dot(gs, kv_ref[z, keys, :HEAD])
                    gk = dot(gs, q_g, ROWS_T) * scaling
                    gv = dot(probs[z].astype(BF16), go_g, ROWS_T)
                    total = gkv_away.at[z - 1] if z else gkv.at[s]
                    if turn:
                        gk, gv = gk + total[:, :HEAD], gv + total[:, HEAD:]
                    total[:, :HEAD] = gk
                    total[:, HEAD:] = gv
                g_qkv[rows, cols] = turn_back(gq * scaling, rows)
            sent = []
            for z in range(n_zh - 1):
                gkv_out[s, z] = gkv_away[z].astype(BF16)
                sent.append(net.send(gkv_out.at[s, z], gkv_in.at[s, z], kv_wires[s][z]))
            return sent

        def keys(s, sent):
            rows = slice(s * n, (s + 1) * n)
            q_cols = heads * HEAD
            mine = gkv[s]
            for z, cp in enumerate(sent):
                cp.wait_recv()
                mine = mine + gkv_in[s, z].astype(F32)
            g_qkv[rows, q_cols : q_cols + HEAD] = turn_back(mine[:, :HEAD], rows)
            g_qkv[rows, q_cols + HEAD :] = mine[:, HEAD:].astype(BF16)
            away = pl.ds(pl.multiple_of((1 - net.here["c"]) * half, half), half)
            here = pl.ds(pl.multiple_of(net.here["c"] * half, half), half)
            window = pl.ds(s * n, n)
            halves.append(
                net.send(g_qkv.at[window, away], half_ref.at[1, window], half_wires[s])
            )
            kept.append(local(g_qkv.at[window, here], half_ref.at[0, window]))

        def term(r):
            def tile(t, _):
                at = pl.ds(pl.multiple_of(t * TILE, TILE), TILE)
                value = dot(g_qkv[r * own : (r + 1) * own], wa[at, :], COLS_T)
                gn1[r, :, at] = value.astype(BF16)
                return 0

            lax.fori_loop(0, width // TILE, tile, 0)

        def add(r, window):
            gn1[r, window] = (gn1[r, window].astype(F32) + far[window].astype(F32)).astype(BF16)

        def add_out(hops):
            for _, _, at, *what in sorted(adder.steps, key=lambda step: step[0]):
                if at == hops:
                    adder.run(at, *what)

        def relay_late():
            for hops, part, off, sends in late:
                gas.run(hops, part, off, sends)

        halves, late, arrived, sent = [], [], set(), {}
        for _, _, hops, part, off, sends in ga_steps:
            if not hops:
                continue
            if off["c"]:
                late.append((hops, part, off, sends))
                continue
            gas.run(hops, part, off, sends)
            if part == CHUNKS - 1:
                i, j = off["y"], off["zl"]
                local(gas_ref.at[0, i, j], gav.at[i, j]).wait()
                arrived.add((i, j))
                if arrived >= {(0, 1), (1, 0)} and 0 not in sent:
                    flow(2)
                    sent[0] = slot(0)
                    flow(1)
        flow(1)
        sent[1] = slot(1)
        add_out(0)
        flow(2)
        if sums:
            product(sum_ins[1], sum_ins[3], made_refs[1], 2)
            there(2)
            relay_late()
            got_o.wait()
            others = [
                local(gas_ref.at[1, i, j], gn1.at[2 * i + j]) for i in range(2) for j in range(2)
            ]
            for cp in others:
                cp.wait()

            def output(t, _):
                at = pl.ds(pl.multiple_of(t * TILE, TILE), TILE)
                value = dot(o_v[0], gav[:, :, :, at].reshape(n_tok, TILE), ROWS_T)
                value += dot(o_v[1], gn1[:, :, at].reshape(n_tok, TILE), ROWS_T)
                block = pl.ds(pl.multiple_of(t * o_v.shape[2], o_v.shape[2]), o_v.shape[2])
                wr[0, block] = value.astype(BF16)
                return 0

            lax.fori_loop(0, width // TILE, output, 0)
            n_rows = o_v.shape[2]
            kept_out = [
                local(
                    wr.at[0, pl.ds(t * n_rows, n_rows)], made_refs[2].at[:, pl.ds(t * TILE, TILE)]
                )
                for t in range(width // TILE)
            ]
            for cp in kept_out:
                cp.wait()
            there(3)
            flow(FLOW[0])
        else:
            relay_late()
        keys(0, sent[0])
        term(1)
        term(0)
        add_out(1)
        flow(FLOW[1])
        keys(1, sent[1])
        term(3)
        to_far = (
            net.send(gn1.at[3, y_rows], far.at[y_rows], far_wires[0]),
            net.send(gn1.at[3, zl_rows], far.at[zl_rows], far_wires[1]),
        )
        term(2)
        kept.append(local(gn1.at[0], gn1_ref.at[0]))
        flow(FLOW[2])
        to_far[1].wait_recv()
        add(2, zl_rows)
        to_y = net.send(gn1.at[2], gn1_ref.at[1], near_wires[0])
        to_far[0].wait_recv()
        add(1, y_rows)
        to_zl = net.send(gn1.at[1], gn1_ref.at[2], near_wires[1])
        for cp in halves:
            cp.wait_recv()
        for cp in kept:
            cp.wait()
        if sums:
            flow(FLOW[3])
            product(sum_ins[5], half_ref, made_refs[3], 1)
            there(4)
        flow(100)
        assert not plan
        for cp in (to_y, to_zl):
            cp.wait_recv()
        adder.finish()
        net.close()
        for stream in streams:
            stream.close()

    shape = jax.ShapeDtypeStruct
    vmem, hbm = pl.BlockSpec(memory_space=pltpu.VMEM), pl.BlockSpec(memory_space=pl.ANY)
    scratch = [
        pltpu.VMEM((2, 2, own, width), BF16),
        pltpu.VMEM(w_out.shape, BF16),
        pltpu.VMEM(w_attn.shape, BF16),
        pltpu.VMEM((n_tok, heads * HEAD), BF16),
        pltpu.VMEM((n_slot, n, 2 * HEAD), F32),
        pltpu.VMEM((n_zh - 1, n, 2 * HEAD), F32),
        pltpu.VMEM((n_slot, n_zh - 1, n, 2 * HEAD), BF16),
        pltpu.VMEM((n_slot, n_zh - 1, n, 2 * HEAD), BF16),
        pltpu.VMEM((n_tok, columns), BF16),
        pltpu.VMEM((4, own, width), BF16),
        pltpu.VMEM((own, width), BF16),
        pltpu.SemaphoreType.DMA((net.count,)),
        pltpu.SemaphoreType.DMA((net.count,)),
        pltpu.SemaphoreType.DMA((n_local,)),
        *adder.scratch(),
    ]
    for stream in streams:
        scratch += stream.scratch()
    if sums:
        scratch += [
            pltpu.VMEM((2, n_tok, TILE), BF16),
            pltpu.VMEM((2, 2, n_tok, own), BF16),
            pltpu.VMEM((2, own, TILE), BF16),
            pltpu.VMEM(o_half.shape, BF16),
            pltpu.SemaphoreType.DMA((2,)),
            pltpu.SemaphoreType.DMA((2, 2)),
            pltpu.SemaphoreType.DMA((2,)),
        ]
    return pl.pallas_call(
        kernel,
        out_shape=[
            shape((2, 2, 2, own, width), BF16),
            shape((2, n_tok, half), BF16),
            shape((3, own, width), BF16),
            shape((2, own, width), BF16),
            *[stream.shape() for stream in streams],
            *[shape(dims, BF16) for dims in made],
        ],
        in_specs=[hbm] + [vmem] * 7 + [hbm] * (3 + n_sums),
        out_specs=[hbm] * (4 + len(streams) + len(made)),
        scratch_shapes=scratch,
        compiler_params=pltpu.CompilerParams(
            collective_id=collective_id, has_side_effects=True, vmem_limit_bytes=FFN_VMEM_LIMIT
        ),
    )(ga, q, kv, lse, q_pos, k_pos, cos, sin, w_out, w_attn, out_parts, *(sums or ()))


def positions(members):
    total = lax.axis_size("zh") * lax.axis_size("zl")
    half = jnp.arange(2)[None, :, None]
    row = jnp.arange(BLK)[None, None, :]
    j = members[:, None, None]
    return (jnp.where(half == 0, j, 2 * total - 1 - j) * BLK + row).reshape(-1)


OUTWARD = ("zh", "x", "c")
TILE = 512
TO_TEAM = [("zl", "y", "c")] * CHUNKS
TO_TEAM_EVEN = [("zl", "y", "c"), ("y", "zl", "c")] * (CHUNKS // 2)


def feed_forward(norm, gd, w_gate, w_down, up_part, collective_id):
    net = Net({a: lax.axis_size(a) for a in AXES})
    sizes = net.sizes
    own, width = norm.shape
    ff = w_gate.shape[1]
    half = ff // 2
    norm_job = NearGather(norm, PAIRED_SLOTS, TO_TEAM_EVEN)
    up_job = RowGather(up_part, None, [OUTWARD] * up_part.shape[0])
    norms, ups = Relay(norm_job, 0, net), Relay(up_job, 1, net)
    steps = sorted(norms.steps + ups.steps, key=lambda s: s[0])
    y_rows, zl_rows = pl.ds(0, own // 2), pl.ds(own // 2, own // 2)
    far_wires = net.wire({"y": 1}), net.wire({"zl": 1})
    near_wires = net.wire({"y": 1}), net.wire({"zl": 1})
    half_wires = [[net.wire({"c": 1}) for _ in range(3)] for _ in range(4)]
    n_local = 64

    def kernel(
        norm_ref, gd_ref, w_gate_ref, w_down_ref, up_ref,
        norms_ref, gate_half, up_half, mixed_half, gn2_ref, out_ref,
        wg, wu, wd, nv, gdv, gate, gm, gg, gu, mx, far, send_sem, recv_sem, local_sem,
    ):
        net.open(send_sem, recv_sem)
        norms.open(norm_ref, norms_ref)
        ups.open(up_ref, wu)
        used = iter(range(n_local))

        def local(src, dst):
            cp = pltpu.make_async_copy(src, dst, local_sem.at[next(used)])
            cp.start()
            return cp

        got_norm = local(norm_ref, nv.at[0])
        for _, runner, hops, *what in steps:
            if not hops:
                runner.run(hops, *what)
        got_gate = local(w_gate_ref, wg)
        got_gd = [local(gd_ref.at[0, 0, 0], gdv.at[0]), local(gd_ref.at[0, 1, 0], gdv.at[1])]
        got_down = local(w_down_ref, wd)
        got_up = [local(ups.job.cut(up_ref, p), ups.own(p)) for p in range(len(up_job.orders))]
        got_norm.wait()
        kept_norm = [local(norm_job.cut(nv.at[0], p), norms.own(p)) for p in range(CHUNKS)]

        def tiles(n, body):
            def step(t, _):
                body(pl.ds(pl.multiple_of(t * TILE, TILE), TILE))
                return 0

            lax.fori_loop(0, n // TILE, step, 0)

        gd_turn = [(0, 0), (1, 0), (0, 1), (1, 1)]

        def begin(turn):
            i, j = gd_turn[turn]
            r = 2 * i + j

            def one(t):
                gate[r, :, t] = dot(nv[r], wg[:, t])

            tiles(ff, one)
            got_gd[turn].wait()

            def two(t):
                gm[r, :, t] = dot(gdv[turn % 2], wd[t, :], COLS_T)

            tiles(ff, two)
            if turn + 2 < 4:
                got_gd.append(local(gd_ref.at[(0, *gd_turn[turn + 2])], gdv.at[turn % 2]))

        got_gate.wait()
        got_down.wait()
        begin(0)
        late = []
        arrived = {(1, 0): 0, (0, 1): 0, (1, 1): 0}
        turn = 1
        for _, runner, hops, part, off, sends in steps:
            if not hops:
                continue
            if runner is norms and off["c"]:
                late.append((hops, part, off, sends))
                continue
            runner.run(hops, part, off, sends)
            if runner is norms:
                arrived[off["y"], off["zl"]] += 1
                while turn < 4 and arrived[gd_turn[turn]] == CHUNKS:
                    i, j = gd_turn[turn]
                    local(norms_ref.at[0, i, j], nv.at[2 * i + j]).wait()
                    begin(turn)
                    turn += 1
        for cp in got_up + kept_norm:
            cp.wait()

        halves, busy = [], {}

        def finish(r, buf):
            for cp, remote in busy.pop(buf, []):
                net.settle(cp) if remote else cp.wait()

            def one(t):
                up = dot(nv[r], wu[:, t])
                g, m = gate[r, :, t], gm[r, :, t]
                s = 1.0 / (1.0 + jnp.exp(-g))
                gs = g * s
                mx[r, :, t] = (gs * up).astype(BF16)
                gg[buf, :, t] = (m * up * s * (1.0 + g * (1.0 - s))).astype(BF16)
                gu[buf, :, t] = (m * gs).astype(BF16)

            tiles(ff, one)
            mine = pl.ds(pl.multiple_of(net.here["c"] * half, half), half)
            other = pl.ds(pl.multiple_of((1 - net.here["c"]) * half, half), half)
            rows = pl.ds(r * own, own)
            for n, (ref, out) in enumerate(
                ((gg.at[buf], gate_half), (gu.at[buf], up_half), (mx.at[r], mixed_half))
            ):
                cp = local(ref.at[:, mine], out.at[0, rows])
                sent = net.send(ref.at[:, other], out.at[1, rows], half_wires[r][n])
                halves.append(sent)
                busy.setdefault(buf if n < 2 else "mixed", []).extend([(cp, False), (sent, True)])

            def two(t):
                term = dot(gg[buf], wg[t, :], COLS_T) + dot(gu[buf], wu[t, :], COLS_T)
                nv[r, :, t] = term.astype(BF16)

            tiles(width, two)

        def add(r, window):
            nv[r, window] = (nv[r, window].astype(F32) + far[window].astype(F32)).astype(BF16)

        finish(3, 0)
        to_far = (
            net.send(nv.at[3, y_rows], far.at[y_rows], far_wires[0]),
            net.send(nv.at[3, zl_rows], far.at[zl_rows], far_wires[1]),
        )
        finish(2, 1)
        to_far[1].wait_recv()
        add(2, zl_rows)
        to_y = net.send(nv.at[2], gn2_ref.at[1], near_wires[0])
        finish(1, 0)
        to_far[0].wait_recv()
        add(1, y_rows)
        to_zl = net.send(nv.at[1], gn2_ref.at[2], near_wires[1])
        finish(0, 1)
        stored = [local(nv.at[0], gn2_ref.at[0])]
        for n, r in enumerate((3, 2, 1, 0)):
            buf = n % 2
            for cp, remote in busy.pop(buf, []):
                net.settle(cp) if remote else cp.wait()

            def down(t):
                gg[buf, :, t] = dot(mx[r], wd[:, t]).astype(BF16)

            tiles(width, down)
            busy[buf] = [(local(gg.at[buf], out_ref.at[r // 2, r % 2]), False)]
        for hops, part, off, sends in late:
            norms.run(hops, part, off, sends)
        to_y.wait_recv()
        to_zl.wait_recv()
        for cp in halves:
            cp.wait_recv()
        net.close()
        for cps in busy.values():
            for cp, remote in cps:
                if not remote:
                    cp.wait()
        for cp in stored:
            cp.wait()

    shape = jax.ShapeDtypeStruct
    weight = pltpu.VMEM((width, ff), BF16)
    return pl.pallas_call(
        kernel,
        out_shape=[
            shape((2, 2, 2, own, width), BF16),
            *[shape((2, 4 * own, half), BF16)] * 3,
            shape((3, own, width), BF16),
            shape((2, 2, own, width), BF16),
        ],
        in_specs=[pl.BlockSpec(memory_space=pl.ANY)] * 5,
        out_specs=[pl.BlockSpec(memory_space=pl.ANY)] * 6,
        scratch_shapes=[
            weight,
            weight,
            pltpu.VMEM((ff, width), BF16),
            pltpu.VMEM((4, own, width), BF16),
            pltpu.VMEM((2, own, width), BF16),
            pltpu.VMEM((4, own, ff), F32),
            pltpu.VMEM((4, own, ff), F32),
            pltpu.VMEM((2, own, ff), BF16),
            pltpu.VMEM((2, own, ff), BF16),
            pltpu.VMEM((4, own, ff), BF16),
            pltpu.VMEM((own, width), BF16),
            pltpu.SemaphoreType.DMA((net.count,)),
            pltpu.SemaphoreType.DMA((net.count,)),
            pltpu.SemaphoreType.DMA((n_local,)),
        ],
        cost_estimate=pl.CostEstimate(
            flops=0, bytes_accessed=130 * 3_000_000, transcendentals=0
        ),
        compiler_params=pltpu.CompilerParams(
            collective_id=collective_id, has_side_effects=True, vmem_limit_bytes=FFN_VMEM_LIMIT
        ),
    )(norm, gd, w_gate, w_down, up_part)


def on_device(
    inputs,
    lengths,
    attn_gain,
    query_weight,
    key_matrix,
    value_matrix,
    output_weight,
    ffn_gain,
    gate_weight,
    up_weight,
    down_weight,
    cotangent,
):
    size = {a: lax.axis_size(a) for a in AXES}
    at = {a: lax.axis_index(a) for a in AXES}
    width = inputs.shape[3]
    own = inputs.shape[1] * inputs.shape[2]
    rows = query_weight.shape[0]
    n_dev = width // rows
    team = size["y"] * size["zl"]
    q_cols = query_weight.shape[1] // team
    kv_cols = key_matrix.shape[1] // team
    ff_rows = down_weight.shape[0]
    ff = gate_weight.shape[1] // team
    heads = q_cols // HEAD
    n_tok = team * own
    scaling = HEAD**-0.5

    def by_team(w):
        return w.reshape(rows, team, -1).transpose(1, 0, 2)

    def ff_cut(w):
        if ff_rows % 128 == 0:
            return ColumnSwap(w, ff_rows)
        cut = w.reshape(rows, *(size[a] for a in AXES), ff_rows)
        return Swap(cut.transpose(2, 3, 0, 5, 4, 1, 6).reshape(team, rows, ff), TEAM)

    attn_cut = jnp.concatenate(
        [by_team(query_weight), by_team(key_matrix), by_team(value_matrix)], axis=2
    )
    row = [jnp.pad(gain.astype(F32), (0, 64 - rows)) for gain in (attn_gain, ffn_gain)]
    tile = jnp.concatenate(
        [jnp.concatenate(row)[None], jnp.full((7, 128), lengths[0].astype(F32))]
    )
    tiles, _, gate_part, up_part, w_attn = exchange(
        [
            Gather(tile, AXES, [(("c", "x", "y"), ("zl", "zh"))], rank=0),
            Swap(attn_cut, TEAM),
            ff_cut(gate_weight),
            ff_cut(up_weight),
            RowGatherOf(1, attn_cut, [OUTWARD] * team),
        ],
        1,
    )
    gain_one = tiles[:, 0, :rows].reshape(1, width)
    gain_two = tiles[:, 0, 64 : 64 + rows].reshape(1, width)
    slots = tiles[: n_dev // (size["zh"] * size["zl"]), 1, 0].reshape(
        size["y"], size["x"], size["c"]
    )
    lens = slots[at["y"] ^ jnp.arange(2), at["x"], at["c"]].astype(jnp.int32)

    per_head = n_dev // team

    def head_home(i):
        f, t = i // per_head, i % per_head
        zl, y = f // size["y"], f % size["y"]
        zh, t = t % size["zh"], t // size["zh"]
        x, c = t % size["x"], t // size["x"]
        return (((zh * size["zl"] + zl) * size["y"] + y) * size["x"] + x) * size["c"] + c

    homes = [(i, head_home(i)) for i in range(n_dev)]
    out_part = lax.ppermute(output_weight, AXES, homes)

    def row_gather(part):
        return RowGather(part, None, [OUTWARD] * team)

    my_pos = positions((at["zh"] * size["zl"] + at["zl"])[None])
    valid = (my_pos < lengths[0]).astype(F32)[:, None]
    near_zl = at["zl"] ^ jnp.arange(2)
    near_zh = (at["zh"] + jnp.arange(size["zh"])) % size["zh"]
    q_pos = positions(at["zh"] * 2 + near_zl)
    n_q = q_pos.shape[0]
    k_pos = positions((near_zh[:, None] * 2 + near_zl[None, :]).reshape(-1))
    past = size["zh"] * n_q
    k_pos = jnp.where(k_pos[None] < lens[:, None], k_pos[None], past)
    k_pos = k_pos.reshape(2, size["zh"], 1, n_q)
    half = HEAD // 2
    freq = ROPE_BASE ** (-2.0 * jnp.arange(half).astype(F32) / HEAD)
    angles = q_pos.astype(F32)[:, None] * freq[None, :]
    q_pos = q_pos[:, None]
    cos = jnp.tile(jnp.cos(angles), (size["y"], 1))
    sin = jnp.tile(jnp.sin(angles), (size["y"], 1))

    tokens = inputs.reshape(own, width).astype(F32)
    scale_one = rms_scale(tokens)
    norm_one = (tokens * scale_one * gain_one).astype(BF16)
    gy = valid * cotangent.reshape(own, width).astype(F32)
    (
        norm_one_pair, gd_pair, w_out, w_gate, w_down, q, kv_all, lse, o_half, o_terms
    ) = attention_front(
        norm_one, w_attn, out_part, gate_part, down_weight, gy.astype(BF16), q_pos, k_pos, cos,
        sin, scaling, 2,
    )
    w_down = w_down.reshape(ff, width)
    norm_one_pair = norm_one_pair.reshape(2, n_tok, width)
    w_out = w_out.reshape(q_cols, width)

    def added(term, others):
        return term.astype(F32) + others[0].astype(F32) + others[1].astype(F32)

    h1 = tokens + added(o_terms[0], o_terms[1:])
    scale_two = rms_scale(h1)
    norm_two = (h1 * scale_two * gain_two).astype(BF16)
    norm_two_pair, gate_half, up_half, mixed_half, gn2_terms, out_parts = feed_forward(
        norm_two, gd_pair, w_gate, w_down, up_part, 5
    )
    norm_two_pair = norm_two_pair.reshape(2, n_tok, width)
    gd_pair = gd_pair.reshape(2, n_tok, width)
    gn2 = added(gn2_terms[0], gn2_terms[1:]) * gain_two
    gh1 = gy + scale_two * gn2 - h1 * scale_two**3 * jnp.mean(h1 * gn2, axis=-1, keepdims=True)

    down_term = dot(mixed_half, gd_pair, PAIR_ROWS_T).astype(BF16)
    pairs = size["x"] == size["zh"] == 2
    sums = (down_term, norm_two_pair, gate_half, up_half, o_half, norm_one_pair) if pairs else None
    ga_pair, g_qkv_half, gn1_terms, out_added, *totals = attention_back(
        gh1.astype(BF16), q, kv_all, lse, q_pos, k_pos, cos, sin, w_out, w_attn, out_parts, sums,
        scaling, 8,
    )
    outputs = valid * (h1 + added(out_parts[0, 0], out_added))
    outputs = outputs.astype(BF16).reshape(inputs.shape)
    n_owners = math.prod(size[a] for a in OWNERS)

    def by_owner(total):
        return Swap(total.astype(BF16).reshape(n_owners, rows, -1), OWNERS)

    homeward = [(b, a) for a, b in homes]
    if pairs:
        down_grad, gate_sum, up_sum, out_sum, attn_sum = totals[:5]
        output_grad = lax.ppermute(out_sum, AXES, homeward)
    else:
        outer = size["zh"] * team

        def sum_peers(term, outer=1):
            return sum_over(sum_over(term, "x", outer).astype(BF16), "zh").astype(BF16)

        attn_term = dot(norm_one_pair, g_qkv_half, PAIR_ROWS_T).astype(BF16)
        gate_term = dot(norm_two_pair, gate_half, PAIR_ROWS_T).astype(BF16)
        up_term = dot(norm_two_pair, up_half, PAIR_ROWS_T).astype(BF16)
        out_term = dot(o_half, ga_pair.reshape(2, n_tok, width), PAIR_ROWS_T).astype(BF16)
        down_grad = sum_peers(down_term)
        output_grad = lax.ppermute(sum_peers(out_term), AXES, homeward)
        terms = (attn_term, gate_term, up_term)
        attn_sum, gate_sum, up_sum = exchange(
            [by_owner(sum_peers(term, outer)) for term in terms], 9
        )
    gn1 = added(gn1_terms[0], gn1_terms[1:]) * gain_one
    g_tokens = (
        gh1
        + scale_one * gn1
        - tokens * scale_one**3 * jnp.mean(tokens * gn1, axis=-1, keepdims=True)
    )
    input_grad = g_tokens.astype(BF16).reshape(inputs.shape)

    if ff_rows % 128 == 0:
        (query_grad, key_grad, value_grad, gate_grad, up_grad, attn_against, ffn_against) = finish(
            (attn_sum, gate_sum, up_sum),
            (query_weight, key_matrix, value_matrix, gate_weight, up_weight),
            ff_rows,
        )
        attn_against, ffn_against = attn_against[:, 0], ffn_against[:, 0]
    else:

        def ff_natural(total):
            cut = total.reshape(
                size["zl"], size["y"], size["c"], rows, size["x"], size["zh"], ff_rows
            )
            return cut.transpose(3, 5, 0, 1, 4, 2, 6).reshape(rows, -1).astype(F32)

        def side(part):
            return part.transpose(1, 0, 2).reshape(rows, -1).astype(F32)

        attn_sum = attn_sum.reshape(team, 2, rows, -1)
        query_grad = side(attn_sum[:, 0])
        key_grad = side(attn_sum[:, 1, :, :kv_cols])
        value_grad = side(attn_sum[:, 1, :, kv_cols:])
        gate_grad = ff_natural(gate_sum)
        up_grad = ff_natural(up_sum)

        def against(w, g):
            return jnp.sum(w.astype(F32) * g, axis=1)

        attn_against = (
            against(query_weight, query_grad)
            + against(key_matrix, key_grad)
            + against(value_matrix, value_grad)
        )
        ffn_against = against(gate_weight, gate_grad) + against(up_weight, up_grad)
    attn_gain_grad = attn_against / attn_gain.astype(F32)
    ffn_gain_grad = ffn_against / ffn_gain.astype(F32)
    return (
        outputs,
        input_grad,
        attn_gain_grad,
        query_grad,
        key_grad,
        value_grad,
        output_grad.astype(F32),
        ffn_gain_grad,
        gate_grad,
        up_grad,
        down_grad.astype(F32),
    )


def finish(sums, weights, block):
    sizes = {a: lax.axis_size(a) for a in AXES}
    rows = weights[0].shape[0]
    members = offsets(sizes, OWNERS)
    shares = offsets(sizes, ("x", "zh"))

    def kernel(
        attn, gate, up, wq, wk, wv, wg, wu, gq, gk, gv, gg, gu, attn_total, ffn_total
    ):
        totals = []

        def put(value, out, weight, start):
            value = value.astype(F32)
            width = value.shape[1]
            out[:, start : start + width] = value
            totals.append(
                jnp.sum(weight[:, start : start + width].astype(F32) * value, axis=1, keepdims=True)
            )

        q_width, kv_width = gq.shape[1] // 4, gk.shape[1] // 4
        for i, owner in enumerate(members):
            f = place(owner, TEAM, sizes)
            if owner["c"] == 0:
                put(attn[i], gq, wq, f * q_width)
            else:
                put(attn[i, :, :kv_width], gk, wk, f * kv_width)
                put(attn[i, :, kv_width:], gv, wv, f * kv_width)
        attn_total[...] = sum(totals)
        totals.clear()
        for i, owner in enumerate(members):
            for n, share in enumerate(shares):
                start = place({**owner, **share}, AXES, sizes) * block
                window = slice(n * block, (n + 1) * block)
                put(gate[i, :, window], gg, wg, start)
                put(up[i, :, window], gu, wu, start)
        ffn_total[...] = sum(totals)

    shape = jax.ShapeDtypeStruct
    return pl.pallas_call(
        kernel,
        out_shape=[shape(w.shape, F32) for w in weights] + [shape((rows, 1), F32)] * 2,
        in_specs=[pl.BlockSpec(memory_space=pltpu.VMEM)] * 8,
        out_specs=[pl.BlockSpec(memory_space=pltpu.VMEM)] * 7,
        compiler_params=pltpu.CompilerParams(vmem_limit_bytes=VMEM_LIMIT),
    )(*sums, *weights)


def solution(mesh):
    ctx, fsdp = mesh.shape["ctx"], mesh.shape["fsdp"]
    grid = Mesh(mesh.devices.reshape(ctx // 2, 2, 2, fsdp // 4, 2), AXES)
    act = P(("y", "x", "c"), None, ("zh", "zl"), None)
    row = P(AXES)
    return jax.shard_map(
        on_device,
        mesh=grid,
        in_specs=(act, P(("y", "x", "c"))) + (row,) * 9 + (act,),
        out_specs=(act, act) + (row,) * 9,
        check_vma=False,
    )
```

```python
import itertools
import math

import jax
import jax.numpy as jnp
from jax import lax
from jax.experimental import pallas as pl
from jax.experimental.pallas import tpu as pltpu
from jax.sharding import Mesh
from jax.sharding import PartitionSpec as P

HEAD = 256
VMEM_LIMIT = 48 << 20
FFN_VMEM_LIMIT = 62 << 20
BLK = 128
EPS = 1e-06
ROPE_BASE = 1000042.0
AXES = ("zh", "zl", "y", "x", "c")
TEAM = ("zl", "y")
SLOTS = ("y", "zl")
PAIRED_SLOTS = ("c", "y", "zl")
SHARES = ("c", "x", "zh")
OWNERS = ("zl", "y", "c")
ROWS_T = (((0,), (0,)), ((), ()))
PAIR_ROWS_T = (((0, 1), (0, 1)), ((), ()))
COLS_T = (((1,), (1,)), ((), ()))
F32 = jnp.float32
BF16 = jnp.bfloat16


def offsets(sizes, axes):
    return [dict(zip(axes, o)) for o in itertools.product(*(range(sizes[a]) for a in axes))]


def place(at, layout, sizes):
    index = 0
    for a in layout:
        index = index * sizes[a] + at[a]
    return index


class Gather:
    def __init__(self, x, layout, orders, rank=1):
        self.x, self.layout, self.orders, self.rank = x, layout, orders, rank

    def shape(self, sizes):
        return (math.prod(sizes[a] for a in self.layout),) + self.x.shape

    def cut(self, ref, part):
        rows = self.x.shape[0] // len(self.orders)
        return ref.at[pl.ds(part * rows, rows)]

    def spot(self, out, owner, off, part, sizes):
        return self.cut(out.at[place(owner, self.layout, sizes)], part)


class NearGather(Gather):
    def shape(self, sizes):
        return tuple(sizes[a] for a in self.layout) + self.x.shape

    def spot(self, out, owner, off, part, sizes):
        return self.cut(out.at[tuple(off[a] for a in self.layout)], part)


class RowGather(Gather):
    def shape(self, sizes):
        team, rows, columns = self.x.shape
        return (sizes["x"] * sizes["zh"] * team * sizes["c"] * rows, columns)

    def cut(self, ref, part):
        return ref.at[part]

    def spot(self, out, owner, off, part, sizes):
        team, rows, _ = self.x.shape
        block = (owner["zh"] * team + part) * sizes["x"] + owner["x"]
        start = pl.multiple_of((block * sizes["c"] + owner["c"]) * rows, rows)
        return out.at[pl.ds(start, rows)]


class RowGatherOf(RowGather):
    def __init__(self, source, x, orders):
        super().__init__(jax.ShapeDtypeStruct(x.shape, x.dtype), None, orders)
        self.source = source


class Swap:
    def __init__(self, x, layout):
        self.x, self.layout = x, layout

    def shape(self, sizes):
        return self.x.shape

    def own_shape(self, sizes):
        return self.x.shape[1:]

    def offsets(self, sizes):
        return offsets(sizes, self.layout)

    def pair(self, x, out, here, to, off, sizes):
        return x.at[place(to, self.layout, sizes)], out.at[place(here, self.layout, sizes)]


class ColumnSwap:
    def __init__(self, x, block):
        self.x, self.block = x, block

    def shape(self, sizes):
        rows, columns = self.x.shape
        team = sizes["zl"] * sizes["y"]
        return (team, rows, columns // team)

    def own_shape(self, sizes):
        return self.shape(sizes)[1:]

    def offsets(self, sizes):
        return offsets(sizes, TEAM)

    def pieces(self, x, out, to, sizes):
        found = []
        for i, share in enumerate(offsets(sizes, SHARES)):
            start = pl.multiple_of(place({**share, **to}, AXES, sizes) * self.block, self.block)
            found.append(
                (x.at[:, pl.ds(start, self.block)], out.at[:, pl.ds(i * self.block, self.block)])
            )
        return found


class NearSwap(Swap):
    def pair(self, x, out, here, to, off, sizes):
        i = off[self.layout[0]]
        return x.at[i], out.at[i]


class Halves:
    def __init__(self, x):
        self.x = x

    def shape(self, sizes):
        rows, columns = self.x.shape
        return (2, rows, columns // 2)

    def own_shape(self, sizes):
        rows, columns = self.x.shape
        return (rows, columns // 2)

    def offsets(self, sizes):
        return offsets(sizes, ("c",))

    def pair(self, x, out, here, to, off, sizes):
        width = self.x.shape[1] // 2
        start = pl.multiple_of(to["c"] * width, width)
        return x.at[:, pl.ds(start, width)], out.at[off["c"]]


CHUNKS = 4
AHEAD = 10
ROOM = 5
FLOW = (2, 8, 6, 6)


class TeamSum:
    def __init__(self, x, y_first=2):
        self.x, self.y_first = x, y_first

    def shape(self, sizes):
        return (2,) + self.x.shape[2:]


class Net:
    def __init__(self, sizes):
        self.sizes, self.count, self.reached = sizes, 0, set()

    def wire(self, off):
        self.reached.add(tuple(off.get(a, 0) for a in AXES))
        self.count += 1
        return self.count - 1, off

    def open(self, send_sem, recv_sem):
        self.send_sem, self.recv_sem = send_sem, recv_sem
        self.here = {a: lax.axis_index(a) for a in AXES}
        self.sent = []
        barrier = pltpu.get_barrier_semaphore()
        for off in sorted(self.reached):
            pl.semaphore_signal(
                barrier,
                inc=1,
                device_id=self.device(self.moved(dict(zip(AXES, off)))),
                device_id_type=pl.DeviceIdType.MESH,
            )
        pl.semaphore_wait(barrier, len(self.reached))

    def moved(self, off):
        return {
            a: lax.rem(self.here[a] + off[a], self.sizes[a]) if off.get(a, 0) else self.here[a]
            for a in AXES
        }

    def device(self, at):
        return tuple(at[a] for a in AXES)

    def send(self, src, dst, wire):
        sem, off = wire
        cp = pltpu.make_async_remote_copy(
            src_ref=src,
            dst_ref=dst,
            send_sem=self.send_sem.at[sem],
            recv_sem=self.recv_sem.at[sem],
            device_id=self.device(self.moved(off)),
            device_id_type=pl.DeviceIdType.MESH,
        )
        cp.start()
        self.sent.append(cp)
        return cp

    def settle(self, cp):
        cp.wait_send()
        self.sent = [other for other in self.sent if other is not cp]

    def close(self):
        for cp in self.sent:
            cp.wait_send()


class Relay:
    def __init__(self, job, number, net):
        self.job, self.net, self.sizes = job, net, net.sizes
        self.steps = []
        for part, order in enumerate(job.orders):
            groups = [(axes,) if isinstance(axes, str) else axes for axes in order]
            for off in offsets(self.sizes, [a for axes in groups for a in axes]):
                used = [i for i, axes in enumerate(groups) if any(off[a] for a in axes)]
                sends = [
                    net.wire(to)
                    for axes in groups[used[-1] + 1 if used else 0 :]
                    for to in offsets(self.sizes, axes)
                    if any(to.values())
                ]
                hops = len(used)
                key = (job.rank, part + 2 * hops, hops, number, part)
                self.steps.append((key, self, hops, part, off, sends))

    def open(self, x, out):
        self.x, self.out, self.arrivals = x, out, {}

    def run(self, hops, part, off, sends):
        job, net = self.job, self.net
        owner = net.moved(off)
        if hops:
            self.arrivals[part, tuple(sorted(off.items()))].wait_recv()
            source = job.spot(self.out, owner, off, part, self.sizes)
        else:
            source = job.cut(self.x, part)
        for wire in sends:
            there = dict(off)
            for a, d in wire[1].items():
                there[a] = -d % self.sizes[a]
            dst = job.spot(self.out, owner, there, part, self.sizes)
            self.arrivals[part, tuple(sorted(there.items()))] = net.send(source, dst, wire)

    def own(self, part):
        return self.job.spot(self.out, self.net.here, {a: 0 for a in AXES}, part, self.sizes)


class Stream:
    def __init__(self, net, shape, owners):
        self.net, self.owners = net, owners
        self.nx, self.nz = net.sizes["x"], net.sizes["zh"]
        self.columns, self.dtype = shape[1], BF16
        self.rows = shape[0] // (self.nx * self.nz * CHUNKS)
        self.chunks = [(z, q) for z in [*range(1, self.nz), 0] for q in range(CHUNKS)]
        self.x_wires = [[net.wire({"x": d}) for d in range(1, self.nx)] for _ in self.chunks]
        self.z_wires = [net.wire({"zh": z}) if z else None for z, _ in self.chunks]
        if owners:
            self.members = offsets(net.sizes, TEAM)
            self.own_rows = self.rows // net.sizes["c"]
            self.cores = [
                [({**o, "c": c}, net.wire({**o, "c": c}) if c or any(o.values()) else None)
                 for c in range(net.sizes["c"])]
                for o in self.members
            ]

    def shape(self):
        rows = CHUNKS * self.rows
        if not self.owners:
            return jax.ShapeDtypeStruct((rows, self.columns), self.dtype)
        n = math.prod(self.net.sizes[a] for a in OWNERS)
        return jax.ShapeDtypeStruct((n, rows // n, self.columns), self.dtype)

    def scratch(self):
        n, chunk = len(self.chunks), (self.rows, self.columns)
        return [
            pltpu.VMEM((n, *chunk), self.dtype),
            pltpu.VMEM((self.nx - 1, n, *chunk), self.dtype),
            pltpu.VMEM((self.nz - 1, CHUNKS, *chunk), self.dtype),
            pltpu.SemaphoreType.DMA((n,)),
            pltpu.SemaphoreType.DMA((CHUNKS,)),
        ]

    def open(self, term, out, mine, from_x, from_z, load_sem, store_sem):
        self.term, self.out, self.mine = term, out, mine
        self.from_x, self.from_z = from_x, from_z
        self.load_sem, self.store_sem = load_sem, store_sem
        self.loads, self.x_sent, self.z_sent, self.stores, self.handed = {}, {}, {}, [], []

    def window(self, x, z, q):
        zh = self.net.moved({"zh": z})["zh"]
        if self.owners:
            q = place(self.net.moved(self.members[q]), TEAM, self.net.sizes)
            block = (zh * CHUNKS + q) * self.nx + x
        else:
            block = (x * self.nz + zh) * CHUNKS + q
        return self.term.at[pl.ds(pl.multiple_of(block * self.rows, self.rows), self.rows)]

    def issue(self, k):
        z, q = self.chunks[k]
        self.x_sent[k] = []
        for d, wire in enumerate(self.x_wires[k], 1):
            x = self.net.moved({"x": d})["x"]
            self.x_sent[k].append(
                self.net.send(self.window(x, z, q), self.from_x.at[d - 1, k], wire)
            )
        load = pltpu.make_async_copy(
            self.window(self.net.here["x"], z, q), self.mine.at[k], self.load_sem.at[k]
        )
        load.start()
        self.loads[k] = load

    def merge(self, k):
        z, q = self.chunks[k]
        self.loads[k].wait()
        for cp in self.x_sent[k]:
            cp.wait_recv()
        total = self.mine[k].astype(F32)
        for d in range(self.nx - 1):
            total += self.from_x[d, k].astype(F32)
        self.mine[k] = total.astype(self.dtype)
        if z:
            self.z_sent[z, q] = self.net.send(
                self.mine.at[k], self.from_z.at[z - 1, q], self.z_wires[k]
            )

    def last(self, q):
        k = self.chunks.index((0, q))
        total = self.mine[k].astype(F32)
        for z in range(1, self.nz):
            self.z_sent[z, q].wait_recv()
            total += self.from_z[z - 1, q].astype(F32)
        self.mine[k] = total.astype(self.dtype)
        if self.owners:
            mine = place(self.net.here, OWNERS, self.net.sizes)
            for off, wire in self.cores[q]:
                core = self.net.moved(off)["c"]
                start = pl.multiple_of(core * self.own_rows, self.own_rows)
                src = self.mine.at[k, pl.ds(start, self.own_rows)]
                if wire:
                    self.handed.append(self.net.send(src, self.out.at[mine], wire))
                else:
                    store = pltpu.make_async_copy(src, self.out.at[mine], self.store_sem.at[q])
                    store.start()
                    self.stores.append(store)
            return
        store = pltpu.make_async_copy(
            self.mine.at[k], self.out.at[pl.ds(q * self.rows, self.rows)], self.store_sem.at[q]
        )
        store.start()
        self.stores.append(store)

    def close(self):
        for cp in self.handed:
            cp.wait_recv()
        for store in self.stores:
            store.wait()


class Adder:
    def __init__(self, job, number, net):
        self.job, self.net = job, net
        rows = job.x.shape[2] // CHUNKS
        self.steps = []
        self.parts = []
        for part in range(CHUNKS):
            first, second = ("y", "zl") if part < job.y_first else ("zl", "y")
            wires = net.wire({first: 1}), net.wire({first: 1}), net.wire({second: 1})
            self.parts.append((pl.ds(part * rows, rows), first, second, wires))
            self.steps.append(((0, part, 0, number, part), self, 0, part, None, None))
            self.steps.append(((1, part + 2, 1, number, part), self, 1, part, None, None))

    def scratch(self):
        shape = self.job.x.shape[2:]
        return [pltpu.VMEM(shape, self.job.x.dtype)] * 2 + [pltpu.SemaphoreType.DMA((CHUNKS,))]

    def open(self, x, out, term, far, sem):
        self.x, self.out, self.term, self.far, self.sem = x, out, term, far, sem
        self.waits, self.direct, self.summed = {}, [], []

    def run(self, hops, part, *_):
        window, first, second, wires = self.parts[part]
        y_first = first == "y"
        if not hops:
            self.waits[part] = self.net.send(
                self.x.at[1, 1, window], self.far.at[window], wires[0]
            )
            near = self.x.at[1, 0, window] if y_first else self.x.at[0, 1, window]
            self.direct.append(
                self.net.send(near, self.out.at[0 if y_first else 1, window], wires[1])
            )
            mine = self.x.at[0, 1, window] if y_first else self.x.at[1, 0, window]
            load = pltpu.make_async_copy(mine, self.term.at[window], self.sem.at[part])
            load.start()
            self.waits[part] = self.waits[part], load
            return
        far, load = self.waits[part]
        load.wait()
        far.wait_recv()
        total = self.term[window].astype(F32) + self.far[window].astype(F32)
        self.term[window] = total.astype(self.term.dtype)
        self.summed.append(
            self.net.send(
                self.term.at[window], self.out.at[1 if y_first else 0, window], wires[2]
            )
        )

    def finish(self):
        for cp in self.direct + self.summed:
            cp.wait_recv()


def exchange(jobs, collective_id, micros=50):
    net = Net({a: lax.axis_size(a) for a in AXES})
    sizes = net.sizes
    count = len(jobs)
    n_in = sum(not isinstance(job, RowGatherOf) for job in jobs)
    steps, swaps, runners, scratch = [], [], [], []
    for number, job in enumerate(jobs):
        if isinstance(job, Gather):
            runner = Relay(job, number, net)
            if not isinstance(job, RowGatherOf):
                steps += runner.steps
            stage = [pltpu.VMEM(job.x.shape, job.x.dtype)]
        elif isinstance(job, TeamSum):
            runner = Adder(job, number, net)
            steps += runner.steps
            stage = runner.scratch()
        else:
            runner = None
            n = math.prod(sizes[a] for a in SHARES) if isinstance(job, ColumnSwap) else 1
            for off in job.offsets(sizes):
                if any(off.values()):
                    swaps.append((number, off, [net.wire(off) for _ in range(n)]))
            stage = [pltpu.VMEM(job.own_shape(sizes), job.x.dtype)]
        runners.append((runner, len(scratch), len(scratch) + len(stage)))
        scratch += stage
    steps.sort(key=lambda s: s[0])

    def kernel(*refs):
        ins, outs, rest = refs[:n_in], refs[n_in : n_in + count], refs[n_in + count :]
        send_sem, recv_sem, local_sem, piece_sem = rest[-4:]
        net.open(send_sem, recv_sem)
        loads, stores = [], []
        for number, job in enumerate(jobs):
            runner, lo, hi = runners[number]
            if isinstance(job, TeamSum):
                runner.open(ins[number], outs[number], *rest[lo:hi])
                continue
            if isinstance(job, RowGatherOf):
                continue
            (stage,) = rest[lo:hi]
            if runner:
                runner.open(ins[number], outs[number])
                src = ins[number]
                puts = [
                    (job.cut(stage, part), runner.own(part)) for part in range(len(job.orders))
                ]
            elif isinstance(job, ColumnSwap):
                mine = {a: net.here[a] for a in TEAM}
                for i, (src, dst) in enumerate(job.pieces(ins[number], stage, mine, sizes)):
                    load = pltpu.make_async_copy(src, dst, piece_sem.at[number, i])
                    load.start()
                    loads.append((load, number, []))
                loads[-1][2].append((stage, outs[number].at[place(net.here, TEAM, sizes)]))
                continue
            else:
                none = {a: 0 for a in AXES}
                src, dst = job.pair(ins[number], outs[number], net.here, net.here, none, sizes)
                puts = [(stage, dst)]
            load = pltpu.make_async_copy(src, stage, local_sem.at[number, 0])
            load.start()
            loads.append((load, number, puts))
        for _, runner, hops, *what in steps:
            if not hops:
                runner.run(hops, *what)
        received = []
        for number, off, wires in swaps:
            to = net.moved(off)
            job = jobs[number]
            if isinstance(job, ColumnSwap):
                mine = outs[number].at[place(net.here, TEAM, sizes)]
                pairs = job.pieces(ins[number], mine, {a: to[a] for a in TEAM}, sizes)
            else:
                pairs = [job.pair(ins[number], outs[number], net.here, to, off, sizes)]
            for (src, dst), wire in zip(pairs, wires, strict=True):
                received.append((number, net.send(src, dst, wire)))
        for load, number, puts in loads:
            load.wait()
            for i, (src, dst) in enumerate(puts):
                store = pltpu.make_async_copy(src, dst, local_sem.at[number, 1 + i])
                store.start()
                stores.append((number, store))
        for _, runner, hops, *what in steps:
            if hops:
                runner.run(hops, *what)
        for number, job in enumerate(jobs):
            if not isinstance(job, RowGatherOf):
                continue
            for cps in (received, stores):
                for other, cp in [one for one in cps if one[0] == job.source]:
                    cp.wait_recv() if cps is received else cp.wait()
            received = [one for one in received if one[0] != job.source]
            stores = [one for one in stores if one[0] != job.source]
            runner, lo, hi = runners[number]
            (stage,) = rest[lo:hi]
            source = outs[job.source]
            runner.open(source, outs[number])
            load = pltpu.make_async_copy(source, stage, local_sem.at[number, 0])
            load.start()
            waiting = sorted(runner.steps, key=lambda step: step[0])
            for _, _, hops, *what in waiting:
                if not hops:
                    runner.run(hops, *what)
            load.wait()
            for part in range(len(job.orders)):
                store = pltpu.make_async_copy(
                    job.cut(stage, part), runner.own(part), local_sem.at[number, 1 + part]
                )
                store.start()
                stores.append((number, store))
            for _, _, hops, *what in waiting:
                if hops:
                    runner.run(hops, *what)
        for _, cp in received:
            cp.wait_recv()
        for runner, _, _ in runners:
            if isinstance(runner, Adder):
                runner.finish()
        net.close()
        for _, store in stores:
            store.wait()

    return pl.pallas_call(
        kernel,
        out_shape=[jax.ShapeDtypeStruct(job.shape(sizes), job.x.dtype) for job in jobs],
        in_specs=[pl.BlockSpec(memory_space=pl.ANY)] * n_in,
        out_specs=[pl.BlockSpec(memory_space=pl.ANY)] * count,
        scratch_shapes=scratch
        + [
            pltpu.SemaphoreType.DMA((net.count,)),
            pltpu.SemaphoreType.DMA((net.count,)),
            pltpu.SemaphoreType.DMA((count, 1 + CHUNKS)),
            pltpu.SemaphoreType.DMA((count, math.prod(sizes[a] for a in SHARES))),
        ],
        cost_estimate=pl.CostEstimate(
            flops=0, bytes_accessed=micros * 3_000_000, transcendentals=0
        ),
        compiler_params=pltpu.CompilerParams(
            collective_id=collective_id, has_side_effects=True, vmem_limit_bytes=VMEM_LIMIT
        ),
    )(*[job.x for job in jobs[:n_in]])


def sum_over(term, axis, outer=1):
    size = lax.axis_size(axis)
    me = lax.axis_index(axis)
    columns = term.shape[1]
    term = term.reshape(outer, -1, columns)
    while size > 1:
        size //= 2
        rows = term.shape[1] // 2
        pairs = [(i, i ^ size) for i in range(lax.axis_size(axis))]
        side = (me // size) % 2
        kept = lax.dynamic_slice_in_dim(term, side * rows, rows, axis=1)
        other = lax.ppermute(
            lax.dynamic_slice_in_dim(term, (1 - side) * rows, rows, axis=1), axis, pairs
        )
        term = kept.astype(F32) + other.astype(F32)
        if size > 1:
            term = term.astype(BF16)
    return term.reshape(-1, columns)


def dot(a, b, dims=None):
    if dims is None:
        return jnp.dot(a, b, preferred_element_type=F32)
    return lax.dot_general(a, b, dims, preferred_element_type=F32)


def rotate(t, cos, sin):
    half = t.shape[-1] // 2
    front, back = t[..., :half], t[..., half:]
    return jnp.concatenate([front * cos - back * sin, back * cos + front * sin], axis=-1)


def rms_scale(values):
    return lax.rsqrt(jnp.mean(values * values, axis=-1, keepdims=True) + EPS)


def attention_front(
    norm, w_attn, out_part, gate_part, down_part, gd, q_pos, k_pos, cos, sin, scaling, collective_id
):
    net = Net({a: lax.axis_size(a) for a in AXES})
    sizes = net.sizes
    own, width = norm.shape
    n_slot, n_zh, _, n = k_pos.shape
    n_tok = n_slot * n
    columns = w_attn.shape[1]
    q_cols = columns - 2 * HEAD
    heads = q_cols // HEAD
    half = q_cols // 2
    team = gate_part.shape[0]
    norm_job = NearGather(norm, PAIRED_SLOTS, TO_TEAM)
    down_job = Gather(down_part, SHARES, [OUTWARD] * CHUNKS)
    out_job = Gather(out_part, SHARES, [OUTWARD] * (out_part.shape[0] // 16), rank=2)
    gd_job = NearGather(gd, PAIRED_SLOTS, TO_TEAM)
    gate_job = RowGather(gate_part, None, [OUTWARD] * team)
    norms, downs, outs = (Relay(job, i, net) for i, job in enumerate((norm_job, down_job, out_job)))
    gds, gates = (Relay(job, i, net) for i, job in enumerate((gd_job, gate_job)))
    first = sorted(norms.steps + downs.steps, key=lambda step: step[0])
    out_steps = sorted(outs.steps, key=lambda step: step[0])
    gd_steps = sorted(gds.steps, key=lambda step: step[0])
    gate_steps = sorted(gates.steps, key=lambda step: step[0])
    kv_wires = [[net.wire({"zh": z}) for z in range(1, n_zh)] for _ in range(n_slot)]
    half_wires = [net.wire({"c": 1}) for _ in range(n_slot)]
    y_rows, zl_rows = pl.ds(0, own * 6 // 8), pl.ds(own * 6 // 8, own - own * 6 // 8)
    far_wires = net.wire({"y": 1}), net.wire({"zl": 1})
    near_wires = net.wire({"y": 1}), net.wire({"zl": 1})
    n_local = 64
    out_shapes = [job.shape(sizes) for job in (norm_job, gd_job, out_job, gate_job, down_job)]

    def kernel(
        norm_ref, w_attn_ref, outp_ref, gate_ref, down_ref, gd_ref, q_pos_ref, k_pos_ref, cos_ref,
        sin_ref, norms_ref, gds_ref, w_out_ref, w_gate_ref, w_down_ref, q_ref, kv_ref, lse_ref,
        half_ref, terms_ref,
        nv, wa, wo, q, kv, o, terms, far, gd_stage, gate_stage, down_stage,
        send_sem, recv_sem, local_sem,
    ):
        net.open(send_sem, recv_sem)
        norms.open(norm_ref, norms_ref)
        downs.open(down_ref, w_down_ref)
        outs.open(outp_ref, wo)
        gds.open(gd_ref, gds_ref)
        gates.open(gate_ref, w_gate_ref)
        used = iter(range(n_local))

        def local(src, dst):
            cp = pltpu.make_async_copy(src, dst, local_sem.at[next(used)])
            cp.start()
            return cp

        def start(steps):
            for _, runner, hops, *what in steps:
                if not hops:
                    runner.run(hops, *what)

        start(first)
        got_norm = local(norm_ref, nv.at[0, 0])
        start(out_steps)
        got_attn = [local(w_attn_ref, wa)]
        got_attn += [
            local(out_job.cut(outp_ref, p), outs.own(p)) for p in range(len(out_job.orders))
        ]
        got_gd, got_gate = local(gd_ref, gd_stage), local(gate_ref, gate_stage)
        got_down = local(down_ref, down_stage)
        got_norm.wait()
        kept = [local(norm_job.cut(nv.at[0, 0], p), norms.own(p)) for p in range(CHUNKS)]
        got_gd.wait()
        kept += [local(gd_job.cut(gd_stage, p), gds.own(p)) for p in range(CHUNKS)]
        got_gate.wait()
        kept += [local(gate_job.cut(gate_stage, p), gates.own(p)) for p in range(team)]
        got_down.wait()
        kept += [local(down_job.cut(down_stage, p), downs.own(p)) for p in range(CHUNKS)]

        def turn(t, rows):
            h = HEAD // 2
            c, sn = cos_ref[rows], sin_ref[rows]
            front, back = t[:, :h], t[:, h:]
            return jnp.concatenate([front * c - back * sn, back * c + front * sn], axis=1).astype(
                BF16
            )

        def project(s):
            for j in range(n // own):
                rows = slice(s * n + j * own, s * n + (j + 1) * own)
                for g in range(heads):
                    cols = slice(g * HEAD, (g + 1) * HEAD)
                    q[rows, cols] = turn(dot(nv[s, j], wa[:, cols]), rows)
                kv[0, rows, :HEAD] = turn(dot(nv[s, j], wa[:, q_cols : q_cols + HEAD]), rows)
                kv[0, rows, HEAD:] = dot(nv[s, j], wa[:, q_cols + HEAD :]).astype(BF16)
            window = pl.ds(s * n, n)
            return [
                net.send(kv.at[0, window], kv.at[n_zh - z, window], kv_wires[s][z - 1])
                for z in range(1, n_zh)
            ]

        def attend(s, sent):
            for cp in sent:
                cp.wait_recv()
            rows = slice(s * n, (s + 1) * n)
            for g in range(heads):
                cols = slice(g * HEAD, (g + 1) * HEAD)
                scores = []
                for z in range(n_zh):
                    score = dot(q[rows, cols], kv[z, rows, :HEAD], COLS_T) * scaling
                    allowed = k_pos_ref[s, z] <= q_pos_ref[...]
                    scores.append(jnp.where(allowed, score, -jnp.inf))
                peak = scores[0].max(axis=1, keepdims=True)
                for score in scores[1:]:
                    peak = jnp.maximum(peak, score.max(axis=1, keepdims=True))
                exps = [jnp.exp(score - peak) for score in scores]
                total = sum(e.sum(axis=1, keepdims=True) for e in exps)
                inverse = 1.0 / total
                o[rows, cols] = sum(
                    dot((e * inverse).astype(BF16), kv[z, rows, HEAD:]) for z, e in enumerate(exps)
                ).astype(BF16)
                lse_ref[s, g] = peak + jnp.log(total)
            away = pl.ds(pl.multiple_of((1 - net.here["c"]) * half, half), half)
            here = pl.ds(pl.multiple_of(net.here["c"] * half, half), half)
            window = pl.ds(s * n, n)
            halves.append(net.send(o.at[window, away], half_ref.at[1, window], half_wires[s]))
            kept.append(local(o.at[window, here], half_ref.at[0, window]))

        def term(r):
            def tile(t, _):
                at = pl.ds(pl.multiple_of(t * TILE, TILE), TILE)
                weight = wo[:, :, at].reshape(q_cols, TILE)
                terms[r, :, at] = dot(o[r * own : (r + 1) * own], weight).astype(BF16)
                return 0

            lax.fori_loop(0, width // TILE, tile, 0)

        def add(r, window):
            terms[r, window] = (terms[r, window].astype(F32) + far[window].astype(F32)).astype(BF16)

        halves, late = [], []

        def relay(steps):
            for _, runner, hops, part, off, sends in steps:
                if not hops:
                    continue
                if runner in (norms, gds) and off["c"]:
                    late.append((runner, hops, part, off, sends))
                    continue
                runner.run(hops, part, off, sends)
                if runner is norms and part == CHUNKS - 1:
                    i, j = off["y"], off["zl"]
                    got[i, j] = local(norms_ref.at[0, i, j], nv.at[i, j])

        got = {}
        relay([step for step in first if step[1] is norms or step[0][1] <= ROOM])
        for cp in got_attn:
            cp.wait()
        start(gd_steps)
        got[0, 1].wait()
        sent = [project(0)]
        got[1, 0].wait()
        got[1, 1].wait()
        sent.append(project(1))
        relay([step for step in first if not (step[1] is norms or step[0][1] <= ROOM)])
        relay(out_steps)
        kept.append(local(wo, w_out_ref))
        relay([step for step in gd_steps if step[2] == 1])
        attend(0, sent[0])
        start(gate_steps)
        term(1)
        term(0)
        relay([step for step in gd_steps if step[2] > 1])
        attend(1, sent[1])
        term(3)
        to_far = (
            net.send(terms.at[3, y_rows], far.at[y_rows], far_wires[0]),
            net.send(terms.at[3, zl_rows], far.at[zl_rows], far_wires[1]),
        )
        term(2)
        kept.append(local(terms.at[0], terms_ref.at[0]))
        kept.append(local(q, q_ref))
        kept.append(local(kv, kv_ref))
        relay([step for step in gate_steps if step[2] == 1 and step[3] < 2])
        to_far[1].wait_recv()
        add(2, zl_rows)
        to_y = net.send(terms.at[2], terms_ref.at[1], near_wires[0])
        to_far[0].wait_recv()
        add(1, y_rows)
        to_zl = net.send(terms.at[1], terms_ref.at[2], near_wires[1])
        relay([step for step in gate_steps if not (step[2] == 1 and step[3] < 2)])
        for runner, *step in late:
            runner.run(*step)
        for cp in halves + [to_y, to_zl]:
            cp.wait_recv()
        net.close()
        for cp in kept:
            cp.wait()

    shape = jax.ShapeDtypeStruct
    vmem, hbm = pl.BlockSpec(memory_space=pltpu.VMEM), pl.BlockSpec(memory_space=pl.ANY)
    q_shape, kv_shape = (n_tok, q_cols), (n_zh, n_tok, 2 * HEAD)
    return pl.pallas_call(
        kernel,
        out_shape=[
            *[shape(dims, BF16) for dims in out_shapes],
            shape(q_shape, BF16),
            shape(kv_shape, BF16),
            shape((n_slot, heads, n, 1), F32),
            shape((2, n_tok, half), BF16),
            shape((3, own, width), BF16),
        ],
        in_specs=[hbm] * 6 + [vmem] * 4,
        out_specs=[hbm] * 7 + [vmem] + [hbm] * 2,
        scratch_shapes=[
            pltpu.VMEM((2, 2, own, width), BF16),
            pltpu.VMEM(w_attn.shape, BF16),
            pltpu.VMEM(out_shapes[2], BF16),
            pltpu.VMEM(q_shape, BF16),
            pltpu.VMEM(kv_shape, BF16),
            pltpu.VMEM(q_shape, BF16),
            pltpu.VMEM((4, own, width), BF16),
            pltpu.VMEM((own, width), BF16),
            pltpu.VMEM(gd.shape, BF16),
            pltpu.VMEM(gate_part.shape, BF16),
            pltpu.VMEM(down_part.shape, BF16),
            pltpu.SemaphoreType.DMA((net.count,)),
            pltpu.SemaphoreType.DMA((net.count,)),
            pltpu.SemaphoreType.DMA((n_local,)),
        ],
        cost_estimate=pl.CostEstimate(
            flops=0, bytes_accessed=160 * 3_000_000, transcendentals=0
        ),
        compiler_params=pltpu.CompilerParams(
            collective_id=collective_id, has_side_effects=True, vmem_limit_bytes=FFN_VMEM_LIMIT
        ),
    )(norm, w_attn, out_part, gate_part, down_part, gd, q_pos, k_pos, cos, sin)


def attention_back(
    ga, q, kv, lse, q_pos, k_pos, cos, sin, w_out, w_attn, out_parts, sums, scaling, collective_id
):
    net = Net({a: lax.axis_size(a) for a in AXES})
    own, width = ga.shape
    n_slot, n_zh, _, n = k_pos.shape
    n_tok = n_slot * n
    heads = q.shape[1] // HEAD
    columns = w_attn.shape[1]
    half = columns // 2
    ga_job = NearGather(ga, PAIRED_SLOTS, TO_TEAM_EVEN)
    gas = Relay(ga_job, 0, net)
    ga_steps = sorted(gas.steps, key=lambda step: step[0])
    adder = Adder(TeamSum(out_parts, CHUNKS // 2), 1, net)
    streams, made = [], []
    if sums:
        mixed_half, _, gate_half, _, o_half, _, gd = sums
        made = [(width, gate_half.shape[2])] * 2 + [(o_half.shape[2], width), (width, half)]
        made.append((mixed_half.shape[2], gd.shape[2]))
        streams = [Stream(net, made[4], False)]
        streams += [Stream(net, dims, i != 2) for i, dims in enumerate(made[:4])]
    n_chunks = n_zh * CHUNKS
    kv_wires = [[net.wire({"zh": z}) for z in range(1, n_zh)] for _ in range(n_slot)]
    half_wires = [net.wire({"c": 1}) for _ in range(n_slot)]
    y_rows, zl_rows = pl.ds(0, own // 2), pl.ds(own // 2, own // 2)
    far_wires = net.wire({"y": 1}), net.wire({"zl": 1})
    near_wires = net.wire({"y": 1}), net.wire({"zl": 1})
    n_sums = len(sums) if sums else 0
    n_local = 48

    def kernel(*refs):
        refs = iter(refs)

        def take(count):
            return list(itertools.islice(refs, count))

        ga_ref, q_ref, kv_ref, lse_ref, q_pos_ref, k_pos_ref = take(6)
        cos_ref, sin_ref, wo_ref, wa_ref, parts_ref = take(5)
        sum_ins = take(n_sums)
        gas_ref, half_ref, gn1_ref, added_ref = take(4)
        sum_outs, made_refs = take(len(streams)), take(len(made))
        gav, wo, wa, go, gkv, gkv_away, gkv_out, gkv_in, g_qkv, gn1, far = take(11)
        send_sem, recv_sem, local_sem = take(3)
        adder_scratch = take(3)
        net.open(send_sem, recv_sem)
        gas.open(ga_ref, gas_ref)
        adder.open(parts_ref, added_ref, *adder_scratch)
        for i, stream in enumerate(streams):
            stream.open([*made_refs[4:], *made_refs[:4]][i], sum_outs[i], *take(5))
        used = iter(range(n_local))

        def local(src, dst):
            cp = pltpu.make_async_copy(src, dst, local_sem.at[next(used)])
            cp.start()
            return cp

        plan = []
        for i in range(len(streams)):
            for k in range(n_chunks):
                plan.append((i, k, False))
                q_chunk = k - (n_chunks - CHUNKS)
                if i and q_chunk >= 0:
                    plan.append((i - 1, q_chunk, True))
        plan += [(i, q_chunk, True) for i in range(len(streams))[-1:] for q_chunk in range(CHUNKS)]
        issued, merged = [0] * len(streams), [0] * len(streams)
        ready = [False] * len(streams)

        def pump():
            for i, stream in enumerate(streams):
                while ready[i] and issued[i] < n_chunks and sum(issued) < sum(merged) + AHEAD:
                    stream.issue(issued[i])
                    issued[i] += 1
                if issued[i] < n_chunks:
                    return

        def there(i):
            if sums:
                ready[i] = True
                pump()

        def flow(steps):
            while plan and steps:
                i, k, last = plan[0]
                if last:
                    streams[i].last(k)
                elif k < issued[i]:
                    streams[i].merge(k)
                    merged[i] += 1
                    pump()
                else:
                    return
                plan.pop(0)
                steps -= 1

        if sums:
            wr, lt, ot, o_v, wr_sem, lt_sem, ot_sem = take(7)

        def product(lhs_ref, rhs_ref, term_ref, steps):
            n_cols = wr.shape[2]
            n_tiles = lhs_ref.shape[2] // own

            def lhs(t, slot, c):
                at = pl.ds(pl.multiple_of(t * own, own), own)
                return pltpu.make_async_copy(
                    lhs_ref.at[c, :, at], lt.at[slot, c], lt_sem.at[slot, c]
                )

            for part in range(rhs_ref.shape[2] // n_cols):
                window = pl.ds(part * n_cols, n_cols)
                rhs = [
                    pltpu.make_async_copy(rhs_ref.at[c, :, window], wr.at[c], wr_sem.at[c])
                    for c in range(2)
                ]
                for c in range(2):
                    rhs[c].start()
                    lhs(0, 0, c).start()
                for c in range(2):
                    rhs[c].wait()

                def store(t, slot, window=window):
                    at = pl.ds(pl.multiple_of(t * own, own), own)
                    return pltpu.make_async_copy(
                        ot.at[slot], term_ref.at[at, window], ot_sem.at[slot]
                    )

                def tile(t, _, store=store):
                    slot = lax.rem(t, 2)

                    @pl.when(t + 1 < n_tiles)
                    def _():
                        for c in range(2):
                            lhs(t + 1, 1 - slot, c).start()

                    for c in range(2):
                        lhs(t, slot, c).wait()

                    @pl.when(t >= 2)
                    def _():
                        store(t - 2, slot).wait()

                    value = dot(lt[slot].reshape(2 * n_tok, own), wr[...].reshape(2 * n_tok, n_cols), ROWS_T)
                    ot[slot] = value.astype(BF16)
                    store(t, slot).start()
                    return 0

                lax.fori_loop(0, n_tiles, tile, 0)
                store(n_tiles - 2, n_tiles % 2).wait()
                store(n_tiles - 1, 1 - n_tiles % 2).wait()
                flow(steps)

        for _, _, hops, *what in ga_steps:
            if not hops:
                gas.run(hops, *what)
        if sums:
            got_o = local(sum_ins[4], o_v)
        got_wo, got_wa = local(wo_ref, wo), local(wa_ref, wa)
        got_ga = local(ga_ref, gav.at[0, 0])
        got_ga.wait()
        kept = [local(ga_job.cut(gav.at[0, 0], p), gas.own(p)) for p in range(CHUNKS)]
        got_wo.wait()
        got_wa.wait()
        if sums:
            product(sum_ins[0], sum_ins[6], made_refs[4], 0)
            there(0)
            product(sum_ins[1], sum_ins[2], made_refs[0], 1)
            there(1)

        def turn_back(t, rows):
            h = HEAD // 2
            c, sn = cos_ref[rows], sin_ref[rows]
            front, back = t[:, :h], t[:, h:]
            return jnp.concatenate([front * c + back * sn, back * c - front * sn], axis=1).astype(
                BF16
            )

        def slot(s):
            keys = slice(s * n, (s + 1) * n)
            for j in range(2):
                at = pl.ds(s * n + j * own, own)
                go[at, :] = dot(gav[s, j], wo[...], COLS_T).astype(BF16)
            for turn, (g, j) in enumerate(itertools.product(range(heads), range(n // own))):
                rows = slice(s * n + j * own, s * n + (j + 1) * own)
                here = slice(j * own, (j + 1) * own)
                cols = slice(g * HEAD, (g + 1) * HEAD)
                q_g, go_g, lse_g = q_ref[rows, cols], go[rows, cols], lse_ref[s, g, here]
                probs, gps = [], []
                for z in range(n_zh):
                    score = dot(q_g, kv_ref[z, keys, :HEAD], COLS_T) * scaling
                    allowed = k_pos_ref[s, z] <= q_pos_ref[here]
                    probs.append(jnp.where(allowed, jnp.exp(score - lse_g), 0.0))
                    gps.append(dot(go_g, kv_ref[z, keys, HEAD:], COLS_T))
                delta = sum((p * gp).sum(axis=1, keepdims=True) for p, gp in zip(probs, gps))
                gq = 0.0
                for z in range(n_zh):
                    gs = (probs[z] * (gps[z] - delta)).astype(BF16)
                    gq += dot(gs, kv_ref[z, keys, :HEAD])
                    gk = dot(gs, q_g, ROWS_T) * scaling
                    gv = dot(probs[z].astype(BF16), go_g, ROWS_T)
                    total = gkv_away.at[z - 1] if z else gkv.at[s]
                    if turn:
                        gk, gv = gk + total[:, :HEAD], gv + total[:, HEAD:]
                    total[:, :HEAD] = gk
                    total[:, HEAD:] = gv
                g_qkv[rows, cols] = turn_back(gq * scaling, rows)
            sent = []
            for z in range(n_zh - 1):
                gkv_out[s, z] = gkv_away[z].astype(BF16)
                sent.append(net.send(gkv_out.at[s, z], gkv_in.at[s, z], kv_wires[s][z]))
            return sent

        def keys(s, sent):
            rows = slice(s * n, (s + 1) * n)
            q_cols = heads * HEAD
            mine = gkv[s]
            for z, cp in enumerate(sent):
                cp.wait_recv()
                mine = mine + gkv_in[s, z].astype(F32)
            g_qkv[rows, q_cols : q_cols + HEAD] = turn_back(mine[:, :HEAD], rows)
            g_qkv[rows, q_cols + HEAD :] = mine[:, HEAD:].astype(BF16)
            away = pl.ds(pl.multiple_of((1 - net.here["c"]) * half, half), half)
            here = pl.ds(pl.multiple_of(net.here["c"] * half, half), half)
            window = pl.ds(s * n, n)
            halves.append(
                net.send(g_qkv.at[window, away], half_ref.at[1, window], half_wires[s])
            )
            kept.append(local(g_qkv.at[window, here], half_ref.at[0, window]))

        def term(r):
            def tile(t, _):
                at = pl.ds(pl.multiple_of(t * TILE, TILE), TILE)
                value = dot(g_qkv[r * own : (r + 1) * own], wa[at, :], COLS_T)
                gn1[r, :, at] = value.astype(BF16)
                return 0

            lax.fori_loop(0, width // TILE, tile, 0)

        def add(r, window):
            gn1[r, window] = (gn1[r, window].astype(F32) + far[window].astype(F32)).astype(BF16)

        def add_out(hops):
            for _, _, at, *what in sorted(adder.steps, key=lambda step: step[0]):
                if at == hops:
                    adder.run(at, *what)

        def relay_late():
            for hops, part, off, sends in late:
                gas.run(hops, part, off, sends)

        halves, late, arrived, sent = [], [], set(), {}
        for _, _, hops, part, off, sends in ga_steps:
            if not hops:
                continue
            if off["c"]:
                late.append((hops, part, off, sends))
                continue
            gas.run(hops, part, off, sends)
            if part == CHUNKS - 1:
                i, j = off["y"], off["zl"]
                local(gas_ref.at[0, i, j], gav.at[i, j]).wait()
                arrived.add((i, j))
                if arrived >= {(0, 1), (1, 0)} and 0 not in sent:
                    flow(2)
                    sent[0] = slot(0)
                    flow(1)
        flow(1)
        sent[1] = slot(1)
        add_out(0)
        flow(2)
        if sums:
            product(sum_ins[1], sum_ins[3], made_refs[1], 2)
            there(2)
            relay_late()
            got_o.wait()
            others = [
                local(gas_ref.at[1, i, j], gn1.at[2 * i + j]) for i in range(2) for j in range(2)
            ]
            for cp in others:
                cp.wait()

            def output(t, _):
                at = pl.ds(pl.multiple_of(t * TILE, TILE), TILE)
                value = dot(o_v[0], gav[:, :, :, at].reshape(n_tok, TILE), ROWS_T)
                value += dot(o_v[1], gn1[:, :, at].reshape(n_tok, TILE), ROWS_T)
                block = pl.ds(pl.multiple_of(t * o_v.shape[2], o_v.shape[2]), o_v.shape[2])
                wr[0, block] = value.astype(BF16)
                return 0

            lax.fori_loop(0, width // TILE, output, 0)
            n_rows = o_v.shape[2]
            kept_out = [
                local(
                    wr.at[0, pl.ds(t * n_rows, n_rows)], made_refs[2].at[:, pl.ds(t * TILE, TILE)]
                )
                for t in range(width // TILE)
            ]
            for cp in kept_out:
                cp.wait()
            there(3)
            flow(FLOW[0])
        else:
            relay_late()
        keys(0, sent[0])
        term(1)
        term(0)
        add_out(1)
        flow(FLOW[1])
        keys(1, sent[1])
        term(3)
        to_far = (
            net.send(gn1.at[3, y_rows], far.at[y_rows], far_wires[0]),
            net.send(gn1.at[3, zl_rows], far.at[zl_rows], far_wires[1]),
        )
        term(2)
        kept.append(local(gn1.at[0], gn1_ref.at[0]))
        flow(FLOW[2])
        to_far[1].wait_recv()
        add(2, zl_rows)
        to_y = net.send(gn1.at[2], gn1_ref.at[1], near_wires[0])
        to_far[0].wait_recv()
        add(1, y_rows)
        to_zl = net.send(gn1.at[1], gn1_ref.at[2], near_wires[1])
        for cp in halves:
            cp.wait_recv()
        for cp in kept:
            cp.wait()
        if sums:
            flow(FLOW[3])
            product(sum_ins[5], half_ref, made_refs[3], 1)
            there(4)
        flow(100)
        assert not plan
        for cp in (to_y, to_zl):
            cp.wait_recv()
        adder.finish()
        net.close()
        for stream in streams:
            stream.close()

    shape = jax.ShapeDtypeStruct
    vmem, hbm = pl.BlockSpec(memory_space=pltpu.VMEM), pl.BlockSpec(memory_space=pl.ANY)
    scratch = [
        pltpu.VMEM((2, 2, own, width), BF16),
        pltpu.VMEM(w_out.shape, BF16),
        pltpu.VMEM(w_attn.shape, BF16),
        pltpu.VMEM((n_tok, heads * HEAD), BF16),
        pltpu.VMEM((n_slot, n, 2 * HEAD), F32),
        pltpu.VMEM((n_zh - 1, n, 2 * HEAD), F32),
        pltpu.VMEM((n_slot, n_zh - 1, n, 2 * HEAD), BF16),
        pltpu.VMEM((n_slot, n_zh - 1, n, 2 * HEAD), BF16),
        pltpu.VMEM((n_tok, columns), BF16),
        pltpu.VMEM((4, own, width), BF16),
        pltpu.VMEM((own, width), BF16),
        pltpu.SemaphoreType.DMA((net.count,)),
        pltpu.SemaphoreType.DMA((net.count,)),
        pltpu.SemaphoreType.DMA((n_local,)),
        *adder.scratch(),
    ]
    for stream in streams:
        scratch += stream.scratch()
    if sums:
        scratch += [
            pltpu.VMEM((2, n_tok, TILE), BF16),
            pltpu.VMEM((2, 2, n_tok, own), BF16),
            pltpu.VMEM((2, own, TILE), BF16),
            pltpu.VMEM(o_half.shape, BF16),
            pltpu.SemaphoreType.DMA((2,)),
            pltpu.SemaphoreType.DMA((2, 2)),
            pltpu.SemaphoreType.DMA((2,)),
        ]
    return pl.pallas_call(
        kernel,
        out_shape=[
            shape((2, 2, 2, own, width), BF16),
            shape((2, n_tok, half), BF16),
            shape((3, own, width), BF16),
            shape((2, own, width), BF16),
            *[stream.shape() for stream in streams],
            *[shape(dims, BF16) for dims in made],
        ],
        in_specs=[hbm] + [vmem] * 7 + [hbm] * (3 + n_sums),
        out_specs=[hbm] * (4 + len(streams) + len(made)),
        scratch_shapes=scratch,
        compiler_params=pltpu.CompilerParams(
            collective_id=collective_id, has_side_effects=True, vmem_limit_bytes=FFN_VMEM_LIMIT
        ),
    )(ga, q, kv, lse, q_pos, k_pos, cos, sin, w_out, w_attn, out_parts, *(sums or ()))


def positions(members):
    total = lax.axis_size("zh") * lax.axis_size("zl")
    half = jnp.arange(2)[None, :, None]
    row = jnp.arange(BLK)[None, None, :]
    j = members[:, None, None]
    return (jnp.where(half == 0, j, 2 * total - 1 - j) * BLK + row).reshape(-1)


OUTWARD = ("zh", "x", "c")
TILE = 512
TO_TEAM = [("zl", "y", "c")] * CHUNKS
TO_TEAM_EVEN = [("zl", "y", "c"), ("y", "zl", "c")] * (CHUNKS // 2)


def feed_forward(norm, gd, w_gate, w_down, up_part, collective_id):
    net = Net({a: lax.axis_size(a) for a in AXES})
    sizes = net.sizes
    own, width = norm.shape
    ff = w_gate.shape[1]
    half = ff // 2
    norm_job = NearGather(norm, PAIRED_SLOTS, TO_TEAM_EVEN)
    up_job = RowGather(up_part, None, [OUTWARD] * up_part.shape[0])
    norms, ups = Relay(norm_job, 0, net), Relay(up_job, 1, net)
    steps = sorted(norms.steps + ups.steps, key=lambda s: s[0])
    y_rows, zl_rows = pl.ds(0, own // 2), pl.ds(own // 2, own // 2)
    far_wires = net.wire({"y": 1}), net.wire({"zl": 1})
    near_wires = net.wire({"y": 1}), net.wire({"zl": 1})
    half_wires = [[net.wire({"c": 1}) for _ in range(3)] for _ in range(4)]
    n_local = 64

    def kernel(
        norm_ref, gd_ref, w_gate_ref, w_down_ref, up_ref,
        norms_ref, gate_half, up_half, mixed_half, gn2_ref, out_ref,
        wg, wu, wd, nv, gdv, gate, gm, gg, gu, mx, far, send_sem, recv_sem, local_sem,
    ):
        net.open(send_sem, recv_sem)
        norms.open(norm_ref, norms_ref)
        ups.open(up_ref, wu)
        used = iter(range(n_local))

        def local(src, dst):
            cp = pltpu.make_async_copy(src, dst, local_sem.at[next(used)])
            cp.start()
            return cp

        got_norm = local(norm_ref, nv.at[0])
        for _, runner, hops, *what in steps:
            if not hops:
                runner.run(hops, *what)
        got_gate = local(w_gate_ref, wg)
        got_gd = [local(gd_ref.at[0, 0, 0], gdv.at[0]), local(gd_ref.at[0, 1, 0], gdv.at[1])]
        got_down = local(w_down_ref, wd)
        got_up = [local(ups.job.cut(up_ref, p), ups.own(p)) for p in range(len(up_job.orders))]
        got_norm.wait()
        kept_norm = [local(norm_job.cut(nv.at[0], p), norms.own(p)) for p in range(CHUNKS)]

        def tiles(n, body):
            def step(t, _):
                body(pl.ds(pl.multiple_of(t * TILE, TILE), TILE))
                return 0

            lax.fori_loop(0, n // TILE, step, 0)

        gd_turn = [(0, 0), (1, 0), (0, 1), (1, 1)]

        def begin(turn):
            i, j = gd_turn[turn]
            r = 2 * i + j

            def one(t):
                gate[r, :, t] = dot(nv[r], wg[:, t])

            tiles(ff, one)
            got_gd[turn].wait()

            def two(t):
                gm[r, :, t] = dot(gdv[turn % 2], wd[t, :], COLS_T)

            tiles(ff, two)
            if turn + 2 < 4:
                got_gd.append(local(gd_ref.at[(0, *gd_turn[turn + 2])], gdv.at[turn % 2]))

        got_gate.wait()
        got_down.wait()
        begin(0)
        late = []
        arrived = {(1, 0): 0, (0, 1): 0, (1, 1): 0}
        turn = 1
        for _, runner, hops, part, off, sends in steps:
            if not hops:
                continue
            if runner is norms and off["c"]:
                late.append((hops, part, off, sends))
                continue
            runner.run(hops, part, off, sends)
            if runner is norms:
                arrived[off["y"], off["zl"]] += 1
                while turn < 4 and arrived[gd_turn[turn]] == CHUNKS:
                    i, j = gd_turn[turn]
                    local(norms_ref.at[0, i, j], nv.at[2 * i + j]).wait()
                    begin(turn)
                    turn += 1
        for cp in got_up + kept_norm:
            cp.wait()

        halves, busy = [], {}

        def finish(r, buf):
            for cp, remote in busy.pop(buf, []):
                net.settle(cp) if remote else cp.wait()

            def one(t):
                up = dot(nv[r], wu[:, t])
                g, m = gate[r, :, t], gm[r, :, t]
                s = 1.0 / (1.0 + jnp.exp(-g))
                gs = g * s
                mx[r, :, t] = (gs * up).astype(BF16)
                gg[buf, :, t] = (m * up * s * (1.0 + g * (1.0 - s))).astype(BF16)
                gu[buf, :, t] = (m * gs).astype(BF16)

            tiles(ff, one)
            mine = pl.ds(pl.multiple_of(net.here["c"] * half, half), half)
            other = pl.ds(pl.multiple_of((1 - net.here["c"]) * half, half), half)
            rows = pl.ds(r * own, own)
            for n, (ref, out) in enumerate(
                ((gg.at[buf], gate_half), (gu.at[buf], up_half), (mx.at[r], mixed_half))
            ):
                cp = local(ref.at[:, mine], out.at[0, rows])
                sent = net.send(ref.at[:, other], out.at[1, rows], half_wires[r][n])
                halves.append(sent)
                busy.setdefault(buf if n < 2 else "mixed", []).extend([(cp, False), (sent, True)])

            def two(t):
                term = dot(gg[buf], wg[t, :], COLS_T) + dot(gu[buf], wu[t, :], COLS_T)
                nv[r, :, t] = term.astype(BF16)

            tiles(width, two)

        def add(r, window):
            nv[r, window] = (nv[r, window].astype(F32) + far[window].astype(F32)).astype(BF16)

        finish(3, 0)
        to_far = (
            net.send(nv.at[3, y_rows], far.at[y_rows], far_wires[0]),
            net.send(nv.at[3, zl_rows], far.at[zl_rows], far_wires[1]),
        )
        finish(2, 1)
        to_far[1].wait_recv()
        add(2, zl_rows)
        to_y = net.send(nv.at[2], gn2_ref.at[1], near_wires[0])
        finish(1, 0)
        to_far[0].wait_recv()
        add(1, y_rows)
        to_zl = net.send(nv.at[1], gn2_ref.at[2], near_wires[1])
        finish(0, 1)
        stored = [local(nv.at[0], gn2_ref.at[0])]
        for n, r in enumerate((3, 2, 1, 0)):
            buf = n % 2
            for cp, remote in busy.pop(buf, []):
                net.settle(cp) if remote else cp.wait()

            def down(t):
                gg[buf, :, t] = dot(mx[r], wd[:, t]).astype(BF16)

            tiles(width, down)
            busy[buf] = [(local(gg.at[buf], out_ref.at[r // 2, r % 2]), False)]
        for hops, part, off, sends in late:
            norms.run(hops, part, off, sends)
        to_y.wait_recv()
        to_zl.wait_recv()
        for cp in halves:
            cp.wait_recv()
        net.close()
        for cps in busy.values():
            for cp, remote in cps:
                if not remote:
                    cp.wait()
        for cp in stored:
            cp.wait()

    shape = jax.ShapeDtypeStruct
    weight = pltpu.VMEM((width, ff), BF16)
    return pl.pallas_call(
        kernel,
        out_shape=[
            shape((2, 2, 2, own, width), BF16),
            *[shape((2, 4 * own, half), BF16)] * 3,
            shape((3, own, width), BF16),
            shape((2, 2, own, width), BF16),
        ],
        in_specs=[pl.BlockSpec(memory_space=pl.ANY)] * 5,
        out_specs=[pl.BlockSpec(memory_space=pl.ANY)] * 6,
        scratch_shapes=[
            weight,
            weight,
            pltpu.VMEM((ff, width), BF16),
            pltpu.VMEM((4, own, width), BF16),
            pltpu.VMEM((2, own, width), BF16),
            pltpu.VMEM((4, own, ff), F32),
            pltpu.VMEM((4, own, ff), F32),
            pltpu.VMEM((2, own, ff), BF16),
            pltpu.VMEM((2, own, ff), BF16),
            pltpu.VMEM((4, own, ff), BF16),
            pltpu.VMEM((own, width), BF16),
            pltpu.SemaphoreType.DMA((net.count,)),
            pltpu.SemaphoreType.DMA((net.count,)),
            pltpu.SemaphoreType.DMA((n_local,)),
        ],
        cost_estimate=pl.CostEstimate(
            flops=0, bytes_accessed=130 * 3_000_000, transcendentals=0
        ),
        compiler_params=pltpu.CompilerParams(
            collective_id=collective_id, has_side_effects=True, vmem_limit_bytes=FFN_VMEM_LIMIT
        ),
    )(norm, gd, w_gate, w_down, up_part)


def on_device(
    inputs,
    lengths,
    attn_gain,
    query_weight,
    key_matrix,
    value_matrix,
    output_weight,
    ffn_gain,
    gate_weight,
    up_weight,
    down_weight,
    cotangent,
):
    size = {a: lax.axis_size(a) for a in AXES}
    at = {a: lax.axis_index(a) for a in AXES}
    width = inputs.shape[3]
    own = inputs.shape[1] * inputs.shape[2]
    rows = query_weight.shape[0]
    n_dev = width // rows
    team = size["y"] * size["zl"]
    q_cols = query_weight.shape[1] // team
    kv_cols = key_matrix.shape[1] // team
    ff_rows = down_weight.shape[0]
    ff = gate_weight.shape[1] // team
    heads = q_cols // HEAD
    n_tok = team * own
    scaling = HEAD**-0.5

    def by_team(w):
        return w.reshape(rows, team, -1).transpose(1, 0, 2)

    def ff_cut(w):
        if ff_rows % 128 == 0:
            return ColumnSwap(w, ff_rows)
        cut = w.reshape(rows, *(size[a] for a in AXES), ff_rows)
        return Swap(cut.transpose(2, 3, 0, 5, 4, 1, 6).reshape(team, rows, ff), TEAM)

    attn_cut = jnp.concatenate(
        [by_team(query_weight), by_team(key_matrix), by_team(value_matrix)], axis=2
    )
    row = [jnp.pad(gain.astype(F32), (0, 64 - rows)) for gain in (attn_gain, ffn_gain)]
    tile = jnp.concatenate(
        [jnp.concatenate(row)[None], jnp.full((7, 128), lengths[0].astype(F32))]
    )
    tiles, _, gate_part, up_part, w_attn = exchange(
        [
            Gather(tile, AXES, [(("c", "x", "y"), ("zl", "zh"))], rank=0),
            Swap(attn_cut, TEAM),
            ff_cut(gate_weight),
            ff_cut(up_weight),
            RowGatherOf(1, attn_cut, [OUTWARD] * team),
        ],
        1,
    )
    gain_one = tiles[:, 0, :rows].reshape(1, width)
    gain_two = tiles[:, 0, 64 : 64 + rows].reshape(1, width)
    slots = tiles[: n_dev // (size["zh"] * size["zl"]), 1, 0].reshape(
        size["y"], size["x"], size["c"]
    )
    lens = slots[at["y"] ^ jnp.arange(2), at["x"], at["c"]].astype(jnp.int32)

    per_head = n_dev // team

    def head_home(i):
        f, t = i // per_head, i % per_head
        zl, y = f // size["y"], f % size["y"]
        zh, t = t % size["zh"], t // size["zh"]
        x, c = t % size["x"], t // size["x"]
        return (((zh * size["zl"] + zl) * size["y"] + y) * size["x"] + x) * size["c"] + c

    homes = [(i, head_home(i)) for i in range(n_dev)]
    out_part = lax.ppermute(output_weight, AXES, homes)

    def row_gather(part):
        return RowGather(part, None, [OUTWARD] * team)

    my_pos = positions((at["zh"] * size["zl"] + at["zl"])[None])
    valid = (my_pos < lengths[0]).astype(F32)[:, None]
    near_zl = at["zl"] ^ jnp.arange(2)
    near_zh = (at["zh"] + jnp.arange(size["zh"])) % size["zh"]
    q_pos = positions(at["zh"] * 2 + near_zl)
    n_q = q_pos.shape[0]
    k_pos = positions((near_zh[:, None] * 2 + near_zl[None, :]).reshape(-1))
    past = size["zh"] * n_q
    k_pos = jnp.where(k_pos[None] < lens[:, None], k_pos[None], past)
    k_pos = k_pos.reshape(2, size["zh"], 1, n_q)
    half = HEAD // 2
    freq = ROPE_BASE ** (-2.0 * jnp.arange(half).astype(F32) / HEAD)
    angles = q_pos.astype(F32)[:, None] * freq[None, :]
    q_pos = q_pos[:, None]
    cos = jnp.tile(jnp.cos(angles), (size["y"], 1))
    sin = jnp.tile(jnp.sin(angles), (size["y"], 1))

    tokens = inputs.reshape(own, width).astype(F32)
    scale_one = rms_scale(tokens)
    norm_one = (tokens * scale_one * gain_one).astype(BF16)
    gy = valid * cotangent.reshape(own, width).astype(F32)
    (
        norm_one_pair, gd_pair, w_out, w_gate, w_down, q, kv_all, lse, o_half, o_terms
    ) = attention_front(
        norm_one, w_attn, out_part, gate_part, down_weight, gy.astype(BF16), q_pos, k_pos, cos,
        sin, scaling, 2,
    )
    w_down = w_down.reshape(ff, width)
    norm_one_pair = norm_one_pair.reshape(2, n_tok, width)
    w_out = w_out.reshape(q_cols, width)

    def added(term, others):
        return term.astype(F32) + others[0].astype(F32) + others[1].astype(F32)

    h1 = tokens + added(o_terms[0], o_terms[1:])
    scale_two = rms_scale(h1)
    norm_two = (h1 * scale_two * gain_two).astype(BF16)
    norm_two_pair, gate_half, up_half, mixed_half, gn2_terms, out_parts = feed_forward(
        norm_two, gd_pair, w_gate, w_down, up_part, 5
    )
    norm_two_pair = norm_two_pair.reshape(2, n_tok, width)
    gd_pair = gd_pair.reshape(2, n_tok, width)
    gn2 = added(gn2_terms[0], gn2_terms[1:]) * gain_two
    gh1 = gy + scale_two * gn2 - h1 * scale_two**3 * jnp.mean(h1 * gn2, axis=-1, keepdims=True)

    pairs = size["x"] == size["zh"] == 2
    sums = (mixed_half, norm_two_pair, gate_half, up_half, o_half, norm_one_pair, gd_pair)
    sums = sums if pairs else None
    ga_pair, g_qkv_half, gn1_terms, out_added, *totals = attention_back(
        gh1.astype(BF16), q, kv_all, lse, q_pos, k_pos, cos, sin, w_out, w_attn, out_parts, sums,
        scaling, 8,
    )
    outputs = valid * (h1 + added(out_parts[0, 0], out_added))
    outputs = outputs.astype(BF16).reshape(inputs.shape)
    n_owners = math.prod(size[a] for a in OWNERS)

    def by_owner(total):
        return Swap(total.astype(BF16).reshape(n_owners, rows, -1), OWNERS)

    homeward = [(b, a) for a, b in homes]
    if pairs:
        down_grad, gate_sum, up_sum, out_sum, attn_sum = totals[:5]
        output_grad = lax.ppermute(out_sum, AXES, homeward)
    else:
        outer = size["zh"] * team

        def sum_peers(term, outer=1):
            return sum_over(sum_over(term, "x", outer).astype(BF16), "zh").astype(BF16)

        attn_term = dot(norm_one_pair, g_qkv_half, PAIR_ROWS_T).astype(BF16)
        gate_term = dot(norm_two_pair, gate_half, PAIR_ROWS_T).astype(BF16)
        up_term = dot(norm_two_pair, up_half, PAIR_ROWS_T).astype(BF16)
        out_term = dot(o_half, ga_pair.reshape(2, n_tok, width), PAIR_ROWS_T).astype(BF16)
        down_term = dot(mixed_half, gd_pair, PAIR_ROWS_T).astype(BF16)
        down_grad = sum_peers(down_term)
        output_grad = lax.ppermute(sum_peers(out_term), AXES, homeward)
        terms = (attn_term, gate_term, up_term)
        attn_sum, gate_sum, up_sum = exchange(
            [by_owner(sum_peers(term, outer)) for term in terms], 9
        )
    gn1 = added(gn1_terms[0], gn1_terms[1:]) * gain_one
    g_tokens = (
        gh1
        + scale_one * gn1
        - tokens * scale_one**3 * jnp.mean(tokens * gn1, axis=-1, keepdims=True)
    )
    input_grad = g_tokens.astype(BF16).reshape(inputs.shape)

    if ff_rows % 128 == 0:
        (query_grad, key_grad, value_grad, gate_grad, up_grad, attn_against, ffn_against) = finish(
            (attn_sum, gate_sum, up_sum),
            (query_weight, key_matrix, value_matrix, gate_weight, up_weight),
            ff_rows,
        )
        attn_against, ffn_against = attn_against[:, 0], ffn_against[:, 0]
    else:

        def ff_natural(total):
            cut = total.reshape(
                size["zl"], size["y"], size["c"], rows, size["x"], size["zh"], ff_rows
            )
            return cut.transpose(3, 5, 0, 1, 4, 2, 6).reshape(rows, -1).astype(F32)

        def side(part):
            return part.transpose(1, 0, 2).reshape(rows, -1).astype(F32)

        attn_sum = attn_sum.reshape(team, 2, rows, -1)
        query_grad = side(attn_sum[:, 0])
        key_grad = side(attn_sum[:, 1, :, :kv_cols])
        value_grad = side(attn_sum[:, 1, :, kv_cols:])
        gate_grad = ff_natural(gate_sum)
        up_grad = ff_natural(up_sum)

        def against(w, g):
            return jnp.sum(w.astype(F32) * g, axis=1)

        attn_against = (
            against(query_weight, query_grad)
            + against(key_matrix, key_grad)
            + against(value_matrix, value_grad)
        )
        ffn_against = against(gate_weight, gate_grad) + against(up_weight, up_grad)
    attn_gain_grad = attn_against / attn_gain.astype(F32)
    ffn_gain_grad = ffn_against / ffn_gain.astype(F32)
    return (
        outputs,
        input_grad,
        attn_gain_grad,
        query_grad,
        key_grad,
        value_grad,
        output_grad.astype(F32),
        ffn_gain_grad,
        gate_grad,
        up_grad,
        down_grad.astype(F32),
    )


def finish(sums, weights, block):
    sizes = {a: lax.axis_size(a) for a in AXES}
    rows = weights[0].shape[0]
    members = offsets(sizes, OWNERS)
    shares = offsets(sizes, ("x", "zh"))

    def kernel(
        attn, gate, up, wq, wk, wv, wg, wu, gq, gk, gv, gg, gu, attn_total, ffn_total
    ):
        totals = []

        def put(value, out, weight, start):
            value = value.astype(F32)
            width = value.shape[1]
            out[:, start : start + width] = value
            totals.append(
                jnp.sum(weight[:, start : start + width].astype(F32) * value, axis=1, keepdims=True)
            )

        q_width, kv_width = gq.shape[1] // 4, gk.shape[1] // 4
        for i, owner in enumerate(members):
            f = place(owner, TEAM, sizes)
            if owner["c"] == 0:
                put(attn[i], gq, wq, f * q_width)
            else:
                put(attn[i, :, :kv_width], gk, wk, f * kv_width)
                put(attn[i, :, kv_width:], gv, wv, f * kv_width)
        attn_total[...] = sum(totals)
        totals.clear()
        for i, owner in enumerate(members):
            for n, share in enumerate(shares):
                start = place({**owner, **share}, AXES, sizes) * block
                window = slice(n * block, (n + 1) * block)
                put(gate[i, :, window], gg, wg, start)
                put(up[i, :, window], gu, wu, start)
        ffn_total[...] = sum(totals)

    shape = jax.ShapeDtypeStruct
    return pl.pallas_call(
        kernel,
        out_shape=[shape(w.shape, F32) for w in weights] + [shape((rows, 1), F32)] * 2,
        in_specs=[pl.BlockSpec(memory_space=pltpu.VMEM)] * 8,
        out_specs=[pl.BlockSpec(memory_space=pltpu.VMEM)] * 7,
        compiler_params=pltpu.CompilerParams(vmem_limit_bytes=VMEM_LIMIT),
    )(*sums, *weights)


def solution(mesh):
    ctx, fsdp = mesh.shape["ctx"], mesh.shape["fsdp"]
    grid = Mesh(mesh.devices.reshape(ctx // 2, 2, 2, fsdp // 4, 2), AXES)
    act = P(("y", "x", "c"), None, ("zh", "zl"), None)
    row = P(AXES)
    return jax.shard_map(
        on_device,
        mesh=grid,
        in_specs=(act, P(("y", "x", "c"))) + (row,) * 9 + (act,),
        out_specs=(act, act) + (row,) * 9,
        check_vma=False,
    )
```
